512 devices in a mesh: xy: 32 (over z, x_lo), gz: 16 (over x_hi, y, core).
Axes of the slice: x: 4 (x_hi: 2, x_lo: 2; x = x_hi * 2 + x_lo), y: 4, z: 16, core: 2. Of those that a mesh axis runs over, the one named last changes fastest.
Arguments:
- e_check: float32 [3, 512, 384, 128], P(None, 'xy', 'gz'), may hold values from -6 to 6
- h_check: float32 [3, 512, 384, 128], P(None, 'xy', 'gz'), may hold values from -6 to 6
- adj_e_end: float32 [3, 512, 384, 128], P(None, 'xy', 'gz'), may hold values from -6 to 6
- adj_h_end: float32 [3, 512, 384, 128], P(None, 'xy', 'gz'), may hold values from -6 to 6
- background: float32 [512, 384, 128], P('xy', 'gz'), may hold values from 1 to 12
- conductivity: float32 [512, 384, 128], P('xy', 'gz'), may hold values from 0.02 to 0.5
- pattern: float32 [512, 128], P('xy'), may hold values from 0 to 8
- design_box: int32 [6], replicated, may hold values from 0 to 512, as said below
- pml_width: int32 [3], replicated, may hold values from 8 to 16
Outputs:
- adjoint_e: float32 [3, 512, 384, 128], P(None, 'xy', 'gz')
- adjoint_h: float32 [3, 512, 384, 128], P(None, 'xy', 'gz')
- pattern_grad: float32 [512, 128], P('xy', 'gz')
The draws below stay inside these ranges and needn't reach their ends.
Inputs may be any that keep to these rules, and one draw needn't show every extreme that they name: `design_box`: x_lo < 65, x_hi > 447, likewise for y with 128 and z with 384; z_lo = 0, and along the longest grid dimension the upper end equals that dimension's cell count.
All inputs are finite; a program needn't handle non-finite values.
Results may differ from the reference program's by a relative error of at most 0.0001.
Values sent between devices are 32-bit elements; how exact they have to be, the bound alone decides.
No kernel may reach another device: no remote copies, remote signals or barrier semaphores. Data moves between devices by JAX's collectives and lax.ppermute only.
A program may use at most 64 MiB of HBM per device.

```python
import math
import jax
import jax.numpy as jnp
from jax import lax

NY = 128
STEPS = 2
NX = 512
NZ = 384


def draw_design_box(key, part):
    key = jax.random.fold_in(key, 7)
    keys = jax.random.split(key, 6)
    longest = max(NX, NY, NZ)
    x_low = jax.random.randint(keys[0], (), 0, NX // 8 + 1)
    x_high = NX - jax.random.randint(keys[1], (), 0, NX // 8 + 1)
    y_low = jax.random.randint(keys[2], (), 0, NY // 8 + 1)
    y_high = NY - jax.random.randint(keys[3], (), 0, NY // 8 + 1)
    z_low = jnp.zeros((), jnp.int32)
    z_high = NZ - jax.random.randint(keys[5], (), 0, NZ // 8 + 1)
    if NY == longest:
        y_high = jnp.full((), NY, jnp.int32)
    elif NX == longest:
        x_high = jnp.full((), NX, jnp.int32)
    else:
        z_high = jnp.full((), NZ, jnp.int32)
    return jnp.stack([x_low, x_high, y_low, y_high, z_low, z_high]).astype(jnp.int32)


def shard_levels(own_key, dims, cuts, smallest, largest):
    def one(dim, parts):
        heights = jax.random.uniform(jax.random.fold_in(jax.random.fold_in(own_key, 6), dim), (parts,), jnp.float32, smallest / len(cuts), largest / len(cuts))
        return jnp.repeat(jnp.exp(heights), dims[dim] // parts).reshape((-1,) + (1,) * (len(dims) - dim - 1))

    factor_of = one(*cuts[0])
    for cut in cuts[1:]:
        factor_of = factor_of * one(*cut)
    return factor_of


def noise(own_key, dims, deviation, bound, shards=(), dtype=jnp.bfloat16):
    level = shard_levels(own_key, dims, shards, -0.22, 0.18) if shards else 1.0
    array = jax.random.normal(own_key, dims, jnp.float32) * deviation * level
    return jnp.minimum(jnp.maximum(array, -bound), bound).astype(dtype)


def setup_inputs(seed: int = 0) -> dict:
    arg_keys = jax.random.split(jax.random.key(seed), 10)
    e_check = noise(arg_keys[0], (3, NX, NZ, NY), 1.0, 6.0, ((1, 32), (2, 16)), jnp.float32)
    h_check = noise(arg_keys[1], (3, NX, NZ, NY), 1.0, 6.0, ((1, 32), (2, 16)), jnp.float32)
    adj_e_end = noise(arg_keys[2], (3, NX, NZ, NY), 1.0, 6.0, ((1, 32), (2, 16)), jnp.float32)
    adj_h_end = noise(arg_keys[3], (3, NX, NZ, NY), 1.0, 6.0, ((1, 32), (2, 16)), jnp.float32)
    background = jnp.clip(1.0 + 11.0 * jax.random.uniform(arg_keys[4], (NX, NZ, NY), jnp.float32) ** shard_levels(arg_keys[4], (NX, NZ, NY), ((0, 32), (1, 16)), -0.2, 0.2), 1.0, 12.0)
    conductivity = jnp.clip(jnp.exp(math.log(0.5) - 3.218876 * jax.random.uniform(arg_keys[5], (NX, NZ, NY), jnp.float32) ** shard_levels(arg_keys[5], (NX, NZ, NY), ((0, 32), (1, 16)), -0.2, 0.2)), 0.02, 0.5)
    pattern = jnp.clip(8.0 * jax.random.uniform(arg_keys[6], (NX, NY), jnp.float32) ** shard_levels(arg_keys[6], (NX, NY), ((0, 32),), -0.2, 0.2), 0.0, 8.0)
    design_box = draw_design_box(jax.random.fold_in(arg_keys[9], 71), 0)
    pml_width = jax.random.randint(arg_keys[8], (3,), 8, 17).astype(jnp.int32)
    return dict(e_check=e_check, h_check=h_check, adj_e_end=adj_e_end, adj_h_end=adj_h_end, background=background, conductivity=conductivity, pattern=pattern, design_box=design_box, pml_width=pml_width)


TIME_STEP = 0.5
SIGMA_PEAK = 1.0


def ahead_diff(values, axis):
    rest = lax.slice_in_dim(values, 1, values.shape[axis], axis=axis)
    zero_plane = jnp.zeros_like(lax.slice_in_dim(values, 0, 1, axis=axis))
    return jnp.concatenate([rest, zero_plane], axis) - values


def behind_diff(values, axis):
    first = lax.slice_in_dim(values, 0, values.shape[axis] - 1, axis=axis)
    zero_plane = jnp.zeros_like(lax.slice_in_dim(values, 0, 1, axis=axis))
    return values - jnp.concatenate([zero_plane, first], axis)


def curl_plus(vector):
    comp_x, comp_y, comp_z = vector[0], vector[1], vector[2]
    return jnp.stack([ahead_diff(comp_z, 2) - ahead_diff(comp_y, 1),
                      ahead_diff(comp_x, 1) - ahead_diff(comp_z, 0),
                      ahead_diff(comp_y, 0) - ahead_diff(comp_x, 2)])


def curl_minus(vector):
    comp_x, comp_y, comp_z = vector[0], vector[1], vector[2]
    return jnp.stack([behind_diff(comp_z, 2) - behind_diff(comp_y, 1),
                      behind_diff(comp_x, 1) - behind_diff(comp_z, 0),
                      behind_diff(comp_y, 0) - behind_diff(comp_x, 2)])


def depth_cube(index, total, width):
    place = index.astype(jnp.float32)
    layer = width.astype(jnp.float32)
    low_side = layer - place
    high_side = place - (total - 1 - layer)
    depth = jnp.maximum(jnp.maximum(low_side, high_side), 0.0) / layer
    return depth * depth * depth


def inside_range(index, lower, upper):
    return ((index >= lower) & (index < upper)).astype(jnp.float32)


def coefficients(background, conductivity, pattern, design_box, pml_width, x_index, z_index, y_index, total_x, total_z, total_y):
    mask = (inside_range(x_index, design_box[0], design_box[1])[:, None, None]
            * inside_range(z_index, design_box[4], design_box[5])[None, :, None]
            * inside_range(y_index, design_box[2], design_box[3])[None, None, :])
    sigma = SIGMA_PEAK * (depth_cube(x_index, total_x, pml_width[0])[:, None, None]
                          + depth_cube(z_index, total_z, pml_width[2])[None, :, None]
                          + depth_cube(y_index, total_y, pml_width[1])[None, None, :])
    permittivity = background + mask * pattern[:, None, :]
    loss = (conductivity + sigma) * (TIME_STEP / 2)
    denom = permittivity + loss
    coef_a = (permittivity - loss) / denom
    coef_b = TIME_STEP / denom
    slope_a = 2.0 * loss / (denom * denom)
    slope_b = -TIME_STEP / (denom * denom)
    mag_loss = sigma * (TIME_STEP / 2)
    coef_c = (1.0 - mag_loss) / (1.0 + mag_loss)
    coef_d = TIME_STEP / (1.0 + mag_loss)
    return mask, coef_a, coef_b, slope_a, slope_b, coef_c, coef_d


def reference(e_check, h_check, adj_e_end, adj_h_end, background, conductivity, pattern, design_box, pml_width):
    x_index = jnp.arange(NX).astype(jnp.int32)
    z_index = jnp.arange(NZ).astype(jnp.int32)
    y_index = jnp.arange(NY).astype(jnp.int32)
    mask, coef_a, coef_b, slope_a, slope_b, coef_c, coef_d = coefficients(
        background, conductivity, pattern, design_box, pml_width, x_index, z_index, y_index, NX, NZ, NY)
    electric = e_check
    magnetic = h_check
    saved_e = []
    saved_curl = []
    for turn in range(STEPS):
        magnetic = coef_c * magnetic - coef_d * curl_plus(electric)
        curl_now = curl_minus(magnetic)
        saved_e.append(electric)
        saved_curl.append(curl_now)
        electric = coef_a * electric + coef_b * curl_now
    back_e = adj_e_end
    back_h = adj_h_end
    total = jnp.zeros((NX, NZ, NY), jnp.float32)
    for turn in range(STEPS - 1, -1, -1):
        combined = back_h + curl_plus(coef_b * back_e)
        total = total + jnp.sum(back_e * (slope_a * saved_e[turn] + slope_b * saved_curl[turn]), axis=0)
        back_h = coef_c * combined
        back_e = coef_a * back_e - curl_minus(coef_d * combined)
    pattern_grad = jnp.sum(mask * total, axis=1)
    return back_e, back_h, pattern_grad
```

```python
import functools

import jax
import jax.numpy as jnp
from jax import lax
from jax.experimental import pallas as pl
from jax.experimental.pallas import tpu as pltpu
from jax.sharding import PartitionSpec as P

TIME_STEP = 0.5
SIGMA_PEAK = 1.0
HALF = TIME_STEP / 2
EXT = 8
VMEM_LIMIT = 32 * 1024 * 1024

FIRST_ROWS = (2, 2, 1, 1, 1, 1, 2, 2, 1, 1, 1, 1, 2, 2)
LAST_ROWS = (2, 2, 2, 2, 2, 1, 2, 2, 2, 2, 2, 1, 2, 2)
FIRST_AT = tuple(sum(FIRST_ROWS[:k]) for k in range(14))
LAST_AT = tuple(sum(LAST_ROWS[:k]) for k in range(14))
FIRST_SIZE = -(-sum(FIRST_ROWS) // 8) * 8
LAST_SIZE = -(-sum(LAST_ROWS) // 8) * 8
SLOTS = 14
BACK_PLANES = 11
FRONT_PLANES = 9

ANY = pl.BlockSpec(memory_space=pl.ANY)
VMEM = pl.BlockSpec(memory_space=pltpu.VMEM)
SMEM = pl.BlockSpec(memory_space=pltpu.SMEM)


def shifted(shard, axis, by):
    size = lax.axis_size(axis)
    pairs = [(i, i + by) for i in range(size) if 0 <= i + by < size]
    return lax.ppermute(shard, axis, pairs)


def slot(refs, k):
    return refs[k // 3].at[k % 3] if k < 12 else refs[k - 8]


def edge_rows(*refs):
    fields, outs, scratch = refs[:6], refs[6:8], refs[8:]
    first_out, last_out = outs
    tiles, sems = scratch[:12], scratch[12]
    rows_z = fields[4].shape[1]
    copies = []
    for k, ref in enumerate(fields):
        for side, start in enumerate((0, rows_z - EXT)):
            src = ref.at[:, :, pl.ds(start, EXT), :] if k < 4 else ref.at[:, pl.ds(start, EXT), :]
            copy = pltpu.make_async_copy(src, tiles[2 * k + side], sems.at[2 * k + side])
            copy.start()
            copies.append(copy)
    for copy in copies:
        copy.wait()

    def plane(x, carry):
        for k in range(SLOTS):
            pair = (tiles[2 * (k // 3)], tiles[2 * (k // 3) + 1]) if k < 12 else (
                tiles[2 * (k - 8)], tiles[2 * (k - 8) + 1])
            low = pair[0].at[k % 3, x] if k < 12 else pair[0].at[x]
            high = pair[1].at[k % 3, x] if k < 12 else pair[1].at[x]
            count = FIRST_ROWS[k]
            first_out[x, pl.ds(FIRST_AT[k], count), :] = low[pl.ds(0, count), :]
            count = LAST_ROWS[k]
            last_out[x, pl.ds(LAST_AT[k], count), :] = high[pl.ds(EXT - count, count), :]
        return carry

    lax.fori_loop(0, fields[4].shape[0], plane, 0)


def lane_index(shape):
    return lax.broadcasted_iota(jnp.int32, shape, 1)


def y_ahead(v):
    cols = v.shape[1]
    moved = pltpu.roll(v, cols - 1, 1)
    return jnp.where(lane_index(v.shape) == cols - 1, 0.0, moved) - v


def y_behind(v):
    moved = pltpu.roll(v, 1, 1)
    return v - jnp.where(lane_index(v.shape) == 0, 0.0, moved)


def z_ahead(v):
    return pltpu.roll(v, v.shape[0] - 1, 0) - v


def z_behind(v):
    return v - pltpu.roll(v, 1, 0)


def plus_x(v):
    return y_ahead(v[2]) - z_ahead(v[1])


def plus_y(v, next_z):
    return z_ahead(v[0]) - (next_z - v[2])


def plus_z(v, next_y):
    return (next_y - v[1]) - y_ahead(v[0])


def plus(v, next_y, next_z):
    return plus_x(v), plus_y(v, next_z), plus_z(v, next_y)


def minus(v, prev_y, prev_z):
    return (
        y_behind(v[2]) - z_behind(v[1]),
        z_behind(v[0]) - (v[2] - prev_z),
        (v[1] - prev_y) - y_behind(v[0]),
    )


def minus_first(v_x, prev_y, prev_z):
    return None, z_behind(v_x) + prev_z, -prev_y - y_behind(v_x)


def depth_cube(place, total, layer):
    depth = jnp.maximum(jnp.maximum(layer - place, place - (total - 1 - layer)), 0.0) / layer
    return depth * depth * depth


class Grid:
    def __init__(self, box, pml, pos, rows_x, rows_z, cols, total_x, total_z):
        rows = rows_z + EXT
        self.shape = (rows, cols)
        self.box = box
        self.width_x = pml[0].astype(jnp.float32)
        self.total_x = total_x
        self.x_start = pos[0] * rows_x
        self.rows_z = rows_z
        row = lax.broadcasted_iota(jnp.int32, self.shape, 0)
        z = pos[1] * rows_z + jnp.where(row < rows_z + EXT // 2, row, row - rows)
        y = lane_index(self.shape)
        self.inside = (z >= 0) & (z < total_z)
        self.sigma_zy = depth_cube(
            z.astype(jnp.float32), total_z, pml[2].astype(jnp.float32)
        ) + depth_cube(y.astype(jnp.float32), cols, pml[1].astype(jnp.float32))
        picked = (z >= box[4]) & (z < box[5]) & (y >= box[2]) & (y < box[3])
        self.mask_zy = jnp.where(picked, 1.0, 0.0)

    def sigma(self, x):
        place = jnp.full((1, self.shape[1]), (self.x_start + x).astype(jnp.float32))
        return SIGMA_PEAK * (self.sigma_zy + depth_cube(place, self.total_x, self.width_x))

    def mask_x(self, x):
        at = self.x_start + x
        return jnp.where((at >= self.box[0]) & (at < self.box[1]), 1.0, 0.0)

    def magnetic(self, sigma, x_inside=None):
        inside = self.inside if x_inside is None else self.inside & x_inside
        inverse = 1.0 / (1.0 + HALF * sigma)
        return (
            jnp.where(inside, 2.0 * inverse - 1.0, 0.0),
            jnp.where(inside, TIME_STEP * inverse, 0.0),
        )

    def electric(self, x, background, conductivity, pattern_row, sigma):
        permittivity = background + self.mask_zy * (pattern_row * self.mask_x(x))
        loss = HALF * (conductivity + sigma)
        inverse = jnp.where(self.inside, 1.0 / (permittivity + loss), 0.0)
        return (permittivity - loss) * inverse, TIME_STEP * inverse, loss, inverse


def full_plane(ref, tile_ref, k, x):
    own = ref[k % 3, x] if k < 12 else ref[x]
    return jnp.concatenate([own, tile_ref[k, x]], axis=0)


def fill_tile(tile_ref, above, below, k, x):
    count = FIRST_ROWS[k]
    tile_ref[k, x, pl.ds(0, count), :] = above[x, pl.ds(FIRST_AT[k], count), :]
    count = LAST_ROWS[k]
    tile_ref[k, x, pl.ds(EXT - count, count), :] = below[x, pl.ds(LAST_AT[k], count), :]


def field_ref(fields, k):
    return fields[k // 3] if k < 12 else fields[k - 8]


def triple(fields, tile_ref, group, x):
    return tuple(full_plane(fields[group], tile_ref, 3 * group + c, x) for c in range(3))


def edge_planes(geometry, pos, box, pml, pattern, *refs):
    fields, (above, below), (to_next, to_prev, tile) = refs[:6], refs[6:8], refs[8:]
    rows_x = geometry[0]
    grid = Grid(box, pml, (pos[0], pos[1]), *geometry)

    def fill(x, carry):
        for k in range(SLOTS):
            tile[k, x] = jnp.zeros(tile.shape[2:], jnp.float32)
            fill_tile(tile, above, below, k, x)
        return carry

    lax.fori_loop(0, rows_x, fill, 0)

    def coefs(x):
        sigma = grid.sigma(x)
        coef_a, coef_b, _, _ = grid.electric(
            x,
            full_plane(fields[4], tile, 12, x),
            full_plane(fields[5], tile, 13, x),
            pattern[pl.ds(x, 1), :],
            sigma,
        )
        return (coef_a, coef_b) + grid.magnetic(sigma)

    def load(x):
        return [triple(fields, tile, g, x) for g in range(4)]

    one, two = rows_x - 2, rows_x - 1
    e1, h1, p1, q1 = load(one)
    e2, h2, p2, q2 = load(two)
    _, cb1, da1, db1 = coefs(one)
    ca2, cb2, da2, db2 = coefs(two)
    before = (
        da1 * h1[1] - db1 * plus_y(e1, e2[2]),
        da1 * h1[2] - db1 * plus_z(e1, e2[1]),
    )
    partial = [da2 * h - db2 * c for h, c in zip(h2, plus(e2, 0.0, 0.0))]
    curl = minus_first(partial[0], before[0], before[1])
    to_next[0], to_next[1] = partial[1], partial[2]
    to_next[2] = ca2 * e2[0]
    to_next[3] = ca2 * e2[1] + cb2 * curl[1]
    to_next[4] = ca2 * e2[2] + cb2 * curl[2]
    to_next[5] = cb2
    u1 = [cb1 * v for v in p1]
    u2 = [cb2 * v for v in p2]
    before = (
        db1 * (q1[1] + plus_y(u1, u2[2])),
        db1 * (q1[2] + plus_z(u1, u2[1])),
    )
    partial = [q + c for q, c in zip(q2, plus(u2, 0.0, 0.0))]
    curl = minus_first(db2 * partial[0], before[0], before[1])
    to_next[6], to_next[7] = partial[1], partial[2]
    to_next[8] = ca2 * p2[0]
    to_next[9] = ca2 * p2[1] - curl[1]
    to_next[10] = ca2 * p2[2] - curl[2]

    e1, h1, p1, q1 = load(0)
    e2, _, p2, _ = load(1)
    ca1, cb1, da1, db1 = coefs(0)
    _, cb2, _, _ = coefs(1)
    whole = [da1 * h - db1 * c for h, c in zip(h1, plus(e1, e2[1], e2[2]))]
    curl = minus(whole, 0.0, 0.0)
    to_prev[0], to_prev[1] = e1[1], e1[2]
    to_prev[2] = ca1 * e1[1] + cb1 * curl[1]
    to_prev[3] = ca1 * e1[2] + cb1 * curl[2]
    to_prev[4] = cb1
    u1 = [cb1 * v for v in p1]
    whole = [db1 * (q + c) for q, c in zip(q1, plus(u1, cb2 * p2[1], cb2 * p2[2]))]
    curl = minus(whole, 0.0, 0.0)
    to_prev[5], to_prev[6] = u1[1], u1[2]
    to_prev[7] = ca1 * p1[1] - curl[1]
    to_prev[8] = ca1 * p1[2] - curl[2]


def sweep(geometry, pos, box, pml, pattern, *refs):
    fields, (tile, back, front) = refs[:6], refs[6:9]
    out_e, out_h, out_sum = refs[9:12]
    mag, adj_mag, ele, adj_ele, ca, cb, da, db, loss_at, inv_at, sums = refs[12:]
    rows_x, rows_z, cols = geometry[:3]
    grid = Grid(box, pml, (pos[0], pos[1]), *geometry)
    last = rows_x - 1

    def coefs(x, carry):
        sigma = grid.sigma(x)
        ca[x + 1], cb[x + 1], loss_at[x], inv_at[x] = grid.electric(
            x,
            full_plane(fields[4], tile, 12, x),
            full_plane(fields[5], tile, 13, x),
            pattern[pl.ds(x, 1), :],
            sigma,
        )
        da[x + 1], db[x + 1] = grid.magnetic(sigma)
        return carry

    lax.fori_loop(0, rows_x, coefs, 0)
    cb[rows_x + 1] = front[4]

    at = jnp.full(grid.shape, grid.x_start)
    da0, db0 = grid.magnetic(grid.sigma(-1), at > 0)
    cb0 = back[5]
    e_y, e_z = full_plane(fields[0], tile, 1, 0), full_plane(fields[0], tile, 2, 0)
    h_y, h_z = back[0] + db0 * e_z, back[1] - db0 * e_y
    ele[0, 0] = back[2] + cb0 * (y_behind(h_z) - z_behind(h_y))
    ele[1, 0] = back[3] - cb0 * h_z
    ele[2, 0] = back[4] + cb0 * h_y
    p_y, p_z = full_plane(fields[2], tile, 7, 0), full_plane(fields[2], tile, 8, 0)
    m_y, m_z = back[6] - cb[1] * p_z, back[7] + cb[1] * p_y
    n_y, n_z = db0 * m_y, db0 * m_z
    adj_ele[0, 0] = back[8] - (y_behind(n_z) - z_behind(n_y))
    adj_ele[1, 0] = back[9] + n_z
    adj_ele[2, 0] = back[10] - n_y
    da[0], db[0], cb[0] = da0, db0, cb0

    def first(x, carry):
        at_last = jnp.full(grid.shape, x) == last
        ahead = jnp.minimum(x + 1, last)
        e, h, p, q = [triple(fields, tile, g, x) for g in range(4)]
        a, b, c, d = ca[x + 1], cb[x + 1], da[x + 1], db[x + 1]
        e_y = jnp.where(at_last, front[0], full_plane(fields[0], tile, 1, ahead))
        e_z = jnp.where(at_last, front[1], full_plane(fields[0], tile, 2, ahead))
        new_h = [c * v - d * w for v, w in zip(h, plus(e, e_y, e_z))]
        prev_h, prev_m = carry
        curl = minus(new_h, *prev_h)
        b_ahead = cb[ahead + 1]
        u_y = jnp.where(at_last, front[5], b_ahead * full_plane(fields[2], tile, 7, ahead))
        u_z = jnp.where(at_last, front[6], b_ahead * full_plane(fields[2], tile, 8, ahead))
        new_m = [v + w for v, w in zip(q, plus([b * v for v in p], u_y, u_z))]
        scaled = [d * v for v in new_m]
        adj_curl = minus(scaled, *prev_m)
        dot_e, dot_r = 0.0, 0.0
        for k in range(3):
            mag[k, x + 1] = new_h[k]
            adj_mag[k, x + 1] = new_m[k]
            ele[k, x + 1] = a * e[k] + b * curl[k]
            new_p = a * p[k] - adj_curl[k]
            adj_ele[k, x + 1] = new_p
            dot_e = dot_e + new_p[:rows_z] * e[k][:rows_z]
            dot_r = dot_r + new_p[:rows_z] * curl[k][:rows_z]
        inverse = inv_at[x, pl.ds(0, rows_z), :]
        sums[x] = inverse * inverse * (
            2.0 * loss_at[x, pl.ds(0, rows_z), :] * dot_e - TIME_STEP * dot_r
        )
        return new_h[1:], scaled[1:]

    lax.fori_loop(0, rows_x, first, ([h_y, h_z], [n_y, n_z]))

    cb_after = front[4]
    ele[1, rows_x + 1] = front[2] + cb_after * mag[2, rows_x]
    ele[2, rows_x + 1] = front[3] - cb_after * mag[1, rows_x]
    d_last = db[rows_x]
    adj_ele[1, rows_x + 1] = front[7] - d_last * adj_mag[2, rows_x]
    adj_ele[2, rows_x + 1] = front[8] + d_last * adj_mag[1, rows_x]

    e = [ele[k, 0] for k in range(3)]
    before_h = [da0 * h_y - db0 * plus_y(e, ele[2, 1]), da0 * h_z - db0 * plus_z(e, ele[1, 1])]
    u = [cb0 * adj_ele[k, 0] for k in range(3)]
    before_m = [
        db0 * (da0 * m_y + plus_y(u, cb[1] * adj_ele[2, 1])),
        db0 * (da0 * m_z + plus_z(u, cb[1] * adj_ele[1, 1])),
    ]

    mask_own = grid.mask_zy[:rows_z]

    def second(x, carry):
        e = [ele[k, x + 1] for k in range(3)]
        p1 = [adj_ele[k, x + 1] for k in range(3)]
        a, b, c, d = ca[x + 1], cb[x + 1], da[x + 1], db[x + 1]
        new_h = [
            c * mag[k, x + 1] - d * w
            for k, w in enumerate(plus(e, ele[1, x + 2], ele[2, x + 2]))
        ]
        prev_h, prev_m = carry
        curl = minus(new_h, *prev_h)
        b_ahead = cb[x + 2]
        u = [b * v for v in p1]
        new_m = [
            c * adj_mag[k, x + 1] + w
            for k, w in enumerate(plus(u, b_ahead * adj_ele[1, x + 2], b_ahead * adj_ele[2, x + 2]))
        ]
        scaled = [d * v for v in new_m]
        adj_curl = minus(scaled, *prev_m)
        dot_e, dot_r = 0.0, 0.0
        for k in range(3):
            out_h[k, x] = c[:rows_z] * new_m[k][:rows_z]
            out_e[k, x] = a[:rows_z] * p1[k][:rows_z] - adj_curl[k][:rows_z]
            p = fields[2][k, x]
            dot_e = dot_e + p * e[k][:rows_z]
            dot_r = dot_r + p * curl[k][:rows_z]
        inverse = inv_at[x, pl.ds(0, rows_z), :]
        terms = sums[x] + inverse * inverse * (
            2.0 * loss_at[x, pl.ds(0, rows_z), :] * dot_e - TIME_STEP * dot_r
        )
        picked = terms * (mask_own * grid.mask_x(x))
        total = picked[0:8]
        for start in range(8, rows_z, 8):
            total = total + picked[start : start + 8]
        out_sum[pl.ds(x, 1), :] = jnp.sum(total, axis=0, keepdims=True)
        return new_h[1:], scaled[1:]

    lax.fori_loop(0, rows_x, second, (before_h, before_m))


def shards(
    e_check, h_check, adj_e_end, adj_h_end, background, conductivity, pattern, design_box, pml_width
):
    rows_x, rows_z, cols = background.shape
    size_x, size_z = lax.axis_size("xy"), lax.axis_size("gz")
    geometry = (rows_x, rows_z, cols, rows_x * size_x, rows_z * size_z)
    pos = jnp.stack([lax.axis_index("xy"), lax.axis_index("gz")]).astype(jnp.int32)
    fields = (e_check, h_check, adj_e_end, adj_h_end, background, conductivity)
    f32 = jnp.float32
    params = pltpu.CompilerParams(vmem_limit_bytes=VMEM_LIMIT)

    def tiles(ref):
        return pltpu.VMEM(ref.shape[:-2] + (EXT, cols), f32)

    first_rows, last_rows = pl.pallas_call(
        edge_rows,
        out_shape=(
            jax.ShapeDtypeStruct((rows_x, FIRST_SIZE, cols), f32),
            jax.ShapeDtypeStruct((rows_x, LAST_SIZE, cols), f32),
        ),
        in_specs=[ANY] * 6,
        out_specs=[VMEM] * 2,
        scratch_shapes=[tiles(ref) for ref in fields for _ in range(2)]
        + [pltpu.SemaphoreType.DMA((12,))],
        compiler_params=params,
        name="edge_rows",
    )(*fields)
    above = shifted(first_rows, "gz", -1)
    below = shifted(last_rows, "gz", 1)

    plane = (rows_z + EXT, cols)
    to_next, to_prev, tile = pl.pallas_call(
        functools.partial(edge_planes, geometry),
        out_shape=(
            jax.ShapeDtypeStruct((BACK_PLANES,) + plane, f32),
            jax.ShapeDtypeStruct((FRONT_PLANES,) + plane, f32),
            jax.ShapeDtypeStruct((SLOTS, rows_x, EXT, cols), f32),
        ),
        in_specs=[SMEM] * 3 + [VMEM] * 9,
        out_specs=[VMEM] * 3,
        compiler_params=params,
        name="edge_planes",
    )(pos, design_box, pml_width, pattern, *fields, above, below)
    back = shifted(to_next, "xy", 1)
    front = shifted(to_prev, "xy", -1)

    def planes(*lead):
        return pltpu.VMEM(lead + plane, f32)

    count = rows_x + 2
    back_e, back_h, local_sum = pl.pallas_call(
        functools.partial(sweep, geometry),
        out_shape=(
            jax.ShapeDtypeStruct(e_check.shape, f32),
            jax.ShapeDtypeStruct(e_check.shape, f32),
            jax.ShapeDtypeStruct((rows_x, cols), f32),
        ),
        in_specs=[SMEM] * 3 + [VMEM] * 10,
        out_specs=[VMEM] * 3,
        scratch_shapes=[planes(3, count)] * 4
        + [planes(count)] * 4
        + [planes(rows_x)] * 2
        + [pltpu.VMEM((rows_x, rows_z, cols), f32)],
        compiler_params=params,
        name="sweep",
    )(pos, design_box, pml_width, pattern, *fields, tile, back, front)

    share = cols // size_z
    parts = lax.all_to_all(local_sum.T, "gz", split_axis=0, concat_axis=0, tiled=True)
    pattern_grad = jnp.sum(parts.reshape(size_z, share, rows_x), axis=0).T
    return (back_e, back_h, pattern_grad)


def solution(mesh):
    field = P(None, "xy", "gz", None)
    cell = P("xy", "gz", None)
    return jax.shard_map(
        shards,
        mesh=mesh,
        in_specs=(field, field, field, field, cell, cell, P("xy", None), P(), P()),
        out_specs=(field, field, P("xy", "gz")),
        check_vma=False,
    )
```

```python
import functools

import jax
import jax.numpy as jnp
from jax import lax
from jax.experimental import pallas as pl
from jax.experimental.pallas import tpu as pltpu
from jax.sharding import PartitionSpec as P

TIME_STEP = 0.5
SIGMA_PEAK = 1.0
HALF = TIME_STEP / 2
EXT = 8
UNROLL = 4
VMEM_LIMIT = 32 * 1024 * 1024

FIRST_ROWS = (2, 2, 1, 1, 1, 1, 2, 2, 1, 1, 1, 1, 2, 2)
LAST_ROWS = (2, 2, 2, 2, 2, 1, 2, 2, 2, 2, 2, 1, 2, 2)
FIRST_AT = tuple(sum(FIRST_ROWS[:k]) for k in range(14))
LAST_AT = tuple(sum(LAST_ROWS[:k]) for k in range(14))
FIRST_SIZE = -(-sum(FIRST_ROWS) // 8) * 8
LAST_SIZE = -(-sum(LAST_ROWS) // 8) * 8
SLOTS = 14
BACK_PLANES = 11
FRONT_PLANES = 9

HBM = pl.BlockSpec(memory_space=pltpu.HBM)
VMEM = pl.BlockSpec(memory_space=pltpu.VMEM)
SMEM = pl.BlockSpec(memory_space=pltpu.SMEM)


def shifted(shard, axis, by):
    size = lax.axis_size(axis)
    pairs = [(i, i + by) for i in range(size) if 0 <= i + by < size]
    return lax.ppermute(shard, axis, pairs)


def slot(refs, k):
    return refs[k // 3].at[k % 3] if k < 12 else refs[k - 8]


def edge_rows(*refs):
    fields, outs, scratch = refs[:6], refs[6:8], refs[8:]
    first_out, last_out = outs
    tiles, sems = scratch[:12], scratch[12]
    rows_z = fields[4].shape[1]
    copies = []
    for k, ref in enumerate(fields):
        for side, start in enumerate((0, rows_z - EXT)):
            src = ref.at[:, :, pl.ds(start, EXT), :] if k < 4 else ref.at[:, pl.ds(start, EXT), :]
            copy = pltpu.make_async_copy(src, tiles[2 * k + side], sems.at[2 * k + side])
            copy.start()
            copies.append(copy)
    for copy in copies:
        copy.wait()

    def plane(x, carry):
        for k in range(SLOTS):
            pair = (tiles[2 * (k // 3)], tiles[2 * (k // 3) + 1]) if k < 12 else (
                tiles[2 * (k - 8)], tiles[2 * (k - 8) + 1])
            low = pair[0].at[k % 3, x] if k < 12 else pair[0].at[x]
            high = pair[1].at[k % 3, x] if k < 12 else pair[1].at[x]
            count = FIRST_ROWS[k]
            first_out[x, pl.ds(FIRST_AT[k], count), :] = low[pl.ds(0, count), :]
            count = LAST_ROWS[k]
            last_out[x, pl.ds(LAST_AT[k], count), :] = high[pl.ds(EXT - count, count), :]
        return carry

    lax.fori_loop(0, fields[4].shape[0], plane, 0)


def lane_index(shape):
    return lax.broadcasted_iota(jnp.int32, shape, 1)


def y_ahead(v):
    cols = v.shape[1]
    moved = pltpu.roll(v, cols - 1, 1)
    return jnp.where(lane_index(v.shape) == cols - 1, 0.0, moved) - v


def y_behind(v):
    moved = pltpu.roll(v, 1, 1)
    return v - jnp.where(lane_index(v.shape) == 0, 0.0, moved)


def z_ahead(v):
    return pltpu.roll(v, v.shape[0] - 1, 0) - v


def z_behind(v):
    return v - pltpu.roll(v, 1, 0)


def plus_x(v):
    return y_ahead(v[2]) - z_ahead(v[1])


def plus_y(v, next_z):
    return z_ahead(v[0]) - (next_z - v[2])


def plus_z(v, next_y):
    return (next_y - v[1]) - y_ahead(v[0])


def plus(v, next_y, next_z):
    return plus_x(v), plus_y(v, next_z), plus_z(v, next_y)


def minus(v, prev_y, prev_z):
    return (
        y_behind(v[2]) - z_behind(v[1]),
        z_behind(v[0]) - (v[2] - prev_z),
        (v[1] - prev_y) - y_behind(v[0]),
    )


def minus_first(v_x, prev_y, prev_z):
    return None, z_behind(v_x) + prev_z, -prev_y - y_behind(v_x)


def depth_cube(place, total, layer):
    depth = jnp.maximum(jnp.maximum(layer - place, place - (total - 1 - layer)), 0.0) / layer
    return depth * depth * depth


class Grid:
    def __init__(self, box, pml, pos, rows_x, rows_z, cols, total_x, total_z):
        rows = rows_z + EXT
        self.shape = (rows, cols)
        self.box = box
        self.width_x = pml[0].astype(jnp.float32)
        self.total_x = total_x
        self.x_start = pos[0] * rows_x
        self.rows_z = rows_z
        row = lax.broadcasted_iota(jnp.int32, self.shape, 0)
        z = pos[1] * rows_z + jnp.where(row < rows_z + EXT // 2, row, row - rows)
        y = lane_index(self.shape)
        self.inside = (z >= 0) & (z < total_z)
        self.sigma_zy = depth_cube(
            z.astype(jnp.float32), total_z, pml[2].astype(jnp.float32)
        ) + depth_cube(y.astype(jnp.float32), cols, pml[1].astype(jnp.float32))
        picked = (z >= box[4]) & (z < box[5]) & (y >= box[2]) & (y < box[3])
        self.mask_zy = jnp.where(picked, 1.0, 0.0)

    def sigma(self, x):
        place = jnp.full((1, self.shape[1]), (self.x_start + x).astype(jnp.float32))
        return SIGMA_PEAK * (self.sigma_zy + depth_cube(place, self.total_x, self.width_x))

    def mask_x(self, x):
        at = self.x_start + x
        return jnp.where((at >= self.box[0]) & (at < self.box[1]), 1.0, 0.0)

    def magnetic(self, sigma, x_inside=None):
        inside = self.inside if x_inside is None else self.inside & x_inside
        inverse = 1.0 / (1.0 + HALF * sigma)
        return (
            jnp.where(inside, 2.0 * inverse - 1.0, 0.0),
            jnp.where(inside, TIME_STEP * inverse, 0.0),
        )

    def electric(self, x, background, conductivity, pattern_row, sigma):
        permittivity = background + self.mask_zy * (pattern_row * self.mask_x(x))
        loss = HALF * (conductivity + sigma)
        inverse = jnp.where(self.inside, 1.0 / (permittivity + loss), 0.0)
        return (permittivity - loss) * inverse, TIME_STEP * inverse, loss, inverse


def full_plane(ref, tile_ref, k, x):
    own = ref[k % 3, x] if k < 12 else ref[x]
    return jnp.concatenate([own, tile_ref[k, x]], axis=0)


def fill_tile(tile_ref, above, below, k, x):
    count = FIRST_ROWS[k]
    tile_ref[k, x, pl.ds(0, count), :] = above[x, pl.ds(FIRST_AT[k], count), :]
    count = LAST_ROWS[k]
    tile_ref[k, x, pl.ds(EXT - count, count), :] = below[x, pl.ds(LAST_AT[k], count), :]


def field_ref(fields, k):
    return fields[k // 3] if k < 12 else fields[k - 8]


def triple(fields, tile_ref, group, x):
    return tuple(full_plane(fields[group], tile_ref, 3 * group + c, x) for c in range(3))


def edge_planes(geometry, pos, box, pml, pattern, *refs):
    fields, (above, below), (to_next, to_prev, tile) = refs[:6], refs[6:8], refs[8:]
    rows_x = geometry[0]
    grid = Grid(box, pml, (pos[0], pos[1]), *geometry)

    def fill(x, carry):
        for k in range(SLOTS):
            tile[k, x] = jnp.zeros(tile.shape[2:], jnp.float32)
            fill_tile(tile, above, below, k, x)
        return carry

    lax.fori_loop(0, rows_x, fill, 0)

    def coefs(x):
        sigma = grid.sigma(x)
        coef_a, coef_b, _, _ = grid.electric(
            x,
            full_plane(fields[4], tile, 12, x),
            full_plane(fields[5], tile, 13, x),
            pattern[pl.ds(x, 1), :],
            sigma,
        )
        return (coef_a, coef_b) + grid.magnetic(sigma)

    def load(x):
        return [triple(fields, tile, g, x) for g in range(4)]

    one, two = rows_x - 2, rows_x - 1
    e1, h1, p1, q1 = load(one)
    e2, h2, p2, q2 = load(two)
    _, cb1, da1, db1 = coefs(one)
    ca2, cb2, da2, db2 = coefs(two)
    before = (
        da1 * h1[1] - db1 * plus_y(e1, e2[2]),
        da1 * h1[2] - db1 * plus_z(e1, e2[1]),
    )
    partial = [da2 * h - db2 * c for h, c in zip(h2, plus(e2, 0.0, 0.0))]
    curl = minus_first(partial[0], before[0], before[1])
    to_next[0], to_next[1] = partial[1], partial[2]
    to_next[2] = ca2 * e2[0]
    to_next[3] = ca2 * e2[1] + cb2 * curl[1]
    to_next[4] = ca2 * e2[2] + cb2 * curl[2]
    to_next[5] = cb2
    u1 = [cb1 * v for v in p1]
    u2 = [cb2 * v for v in p2]
    before = (
        db1 * (q1[1] + plus_y(u1, u2[2])),
        db1 * (q1[2] + plus_z(u1, u2[1])),
    )
    partial = [q + c for q, c in zip(q2, plus(u2, 0.0, 0.0))]
    curl = minus_first(db2 * partial[0], before[0], before[1])
    to_next[6], to_next[7] = partial[1], partial[2]
    to_next[8] = ca2 * p2[0]
    to_next[9] = ca2 * p2[1] - curl[1]
    to_next[10] = ca2 * p2[2] - curl[2]

    e1, h1, p1, q1 = load(0)
    e2, _, p2, _ = load(1)
    ca1, cb1, da1, db1 = coefs(0)
    _, cb2, _, _ = coefs(1)
    whole = [da1 * h - db1 * c for h, c in zip(h1, plus(e1, e2[1], e2[2]))]
    curl = minus(whole, 0.0, 0.0)
    to_prev[0], to_prev[1] = e1[1], e1[2]
    to_prev[2] = ca1 * e1[1] + cb1 * curl[1]
    to_prev[3] = ca1 * e1[2] + cb1 * curl[2]
    to_prev[4] = cb1
    u1 = [cb1 * v for v in p1]
    whole = [db1 * (q + c) for q, c in zip(q1, plus(u1, cb2 * p2[1], cb2 * p2[2]))]
    curl = minus(whole, 0.0, 0.0)
    to_prev[5], to_prev[6] = u1[1], u1[2]
    to_prev[7] = ca1 * p1[1] - curl[1]
    to_prev[8] = ca1 * p1[2] - curl[2]


def sweep(geometry, pos, box, pml, pattern, *refs):
    fields, (tile, back, front) = refs[:6], refs[6:9]
    out_e, out_h, out_sum = refs[9:12]
    mag, adj_mag, ele, adj_ele, ca, cb, da, db, loss_at, inv_at, sums, grad = refs[12:]
    rows_x, rows_z, cols = geometry[:3]
    grid = Grid(box, pml, (pos[0], pos[1]), *geometry)
    last = rows_x - 1

    def coefs(x, carry):
        sigma = grid.sigma(x)
        ca[x + 1], cb[x + 1], loss_at[x], inv_at[x] = grid.electric(
            x,
            full_plane(fields[4], tile, 12, x),
            full_plane(fields[5], tile, 13, x),
            pattern[pl.ds(x, 1), :],
            sigma,
        )
        da[x + 1], db[x + 1] = grid.magnetic(sigma)
        return carry

    lax.fori_loop(0, rows_x, coefs, 0, unroll=UNROLL)
    grad[...] = jnp.zeros(grad.shape, jnp.float32)
    cb[rows_x + 1] = front[4]

    at = jnp.full(grid.shape, grid.x_start)
    da0, db0 = grid.magnetic(grid.sigma(-1), at > 0)
    cb0 = back[5]
    e_y, e_z = full_plane(fields[0], tile, 1, 0), full_plane(fields[0], tile, 2, 0)
    h_y, h_z = back[0] + db0 * e_z, back[1] - db0 * e_y
    ele[0, 0] = back[2] + cb0 * (y_behind(h_z) - z_behind(h_y))
    ele[1, 0] = back[3] - cb0 * h_z
    ele[2, 0] = back[4] + cb0 * h_y
    p_y, p_z = full_plane(fields[2], tile, 7, 0), full_plane(fields[2], tile, 8, 0)
    m_y, m_z = back[6] - cb[1] * p_z, back[7] + cb[1] * p_y
    n_y, n_z = db0 * m_y, db0 * m_z
    adj_ele[0, 0] = back[8] - (y_behind(n_z) - z_behind(n_y))
    adj_ele[1, 0] = back[9] + n_z
    adj_ele[2, 0] = back[10] - n_y
    da[0], db[0], cb[0] = da0, db0, cb0

    def first(x, carry):
        at_last = jnp.full(grid.shape, x) == last
        ahead = jnp.minimum(x + 1, last)
        e, h, p, q = [triple(fields, tile, g, x) for g in range(4)]
        a, b, c, d = ca[x + 1], cb[x + 1], da[x + 1], db[x + 1]
        e_y = jnp.where(at_last, front[0], full_plane(fields[0], tile, 1, ahead))
        e_z = jnp.where(at_last, front[1], full_plane(fields[0], tile, 2, ahead))
        new_h = [c * v - d * w for v, w in zip(h, plus(e, e_y, e_z))]
        prev_h, prev_m = carry
        curl = minus(new_h, *prev_h)
        b_ahead = cb[ahead + 1]
        u_y = jnp.where(at_last, front[5], b_ahead * full_plane(fields[2], tile, 7, ahead))
        u_z = jnp.where(at_last, front[6], b_ahead * full_plane(fields[2], tile, 8, ahead))
        new_m = [v + w for v, w in zip(q, plus([b * v for v in p], u_y, u_z))]
        scaled = [d * v for v in new_m]
        adj_curl = minus(scaled, *prev_m)
        dot_e, dot_r = 0.0, 0.0
        for k in range(3):
            mag[k, x + 1] = new_h[k]
            adj_mag[k, x + 1] = new_m[k]
            ele[k, x + 1] = a * e[k] + b * curl[k]
            new_p = a * p[k] - adj_curl[k]
            adj_ele[k, x + 1] = new_p
            dot_e = dot_e + new_p[:rows_z] * e[k][:rows_z]
            dot_r = dot_r + new_p[:rows_z] * curl[k][:rows_z]
        inverse = inv_at[x, pl.ds(0, rows_z), :]
        sums[x] = inverse * inverse * (
            2.0 * loss_at[x, pl.ds(0, rows_z), :] * dot_e - TIME_STEP * dot_r
        )
        return new_h[1:], scaled[1:]

    lax.fori_loop(0, rows_x, first, ([h_y, h_z], [n_y, n_z]), unroll=UNROLL)

    cb_after = front[4]
    ele[1, rows_x + 1] = front[2] + cb_after * mag[2, rows_x]
    ele[2, rows_x + 1] = front[3] - cb_after * mag[1, rows_x]
    d_last = db[rows_x]
    adj_ele[1, rows_x + 1] = front[7] - d_last * adj_mag[2, rows_x]
    adj_ele[2, rows_x + 1] = front[8] + d_last * adj_mag[1, rows_x]

    e = [ele[k, 0] for k in range(3)]
    before_h = [da0 * h_y - db0 * plus_y(e, ele[2, 1]), da0 * h_z - db0 * plus_z(e, ele[1, 1])]
    u = [cb0 * adj_ele[k, 0] for k in range(3)]
    before_m = [
        db0 * (da0 * m_y + plus_y(u, cb[1] * adj_ele[2, 1])),
        db0 * (da0 * m_z + plus_z(u, cb[1] * adj_ele[1, 1])),
    ]

    mask_own = grid.mask_zy[:rows_z]

    def second(x, carry):
        e = [ele[k, x + 1] for k in range(3)]
        p1 = [adj_ele[k, x + 1] for k in range(3)]
        a, b, c, d = ca[x + 1], cb[x + 1], da[x + 1], db[x + 1]
        new_h = [
            c * mag[k, x + 1] - d * w
            for k, w in enumerate(plus(e, ele[1, x + 2], ele[2, x + 2]))
        ]
        prev_h, prev_m = carry
        curl = minus(new_h, *prev_h)
        b_ahead = cb[x + 2]
        u = [b * v for v in p1]
        new_m = [
            c * adj_mag[k, x + 1] + w
            for k, w in enumerate(plus(u, b_ahead * adj_ele[1, x + 2], b_ahead * adj_ele[2, x + 2]))
        ]
        scaled = [d * v for v in new_m]
        adj_curl = minus(scaled, *prev_m)
        dot_e, dot_r = 0.0, 0.0
        for k in range(3):
            out_h[k, x] = c[:rows_z] * new_m[k][:rows_z]
            out_e[k, x] = a[:rows_z] * p1[k][:rows_z] - adj_curl[k][:rows_z]
            p = fields[2][k, x]
            dot_e = dot_e + p * e[k][:rows_z]
            dot_r = dot_r + p * curl[k][:rows_z]
        inverse = inv_at[x, pl.ds(0, rows_z), :]
        terms = sums[x] + inverse * inverse * (
            2.0 * loss_at[x, pl.ds(0, rows_z), :] * dot_e - TIME_STEP * dot_r
        )
        picked = terms * (mask_own * grid.mask_x(x))
        total = picked[0:8]
        for start in range(8, rows_z, 8):
            total = total + picked[start : start + 8]
        grad[pl.ds(x, 1), :] = jnp.sum(total, axis=0, keepdims=True)
        return new_h[1:], scaled[1:]

    lax.fori_loop(0, rows_x, second, (before_h, before_m), unroll=UNROLL)

    out_sum[...] = jnp.transpose(grad[...])


def add_shares(parts, out):
    share, rows_x = out.shape
    total = parts[pl.ds(0, share), :]
    for j in range(1, parts.shape[0] // share):
        total = total + parts[pl.ds(j * share, share), :]
    out[...] = total[:, :rows_x]


def shards(
    e_check, h_check, adj_e_end, adj_h_end, background, conductivity, pattern, design_box, pml_width
):
    rows_x, rows_z, cols = background.shape
    size_x, size_z = lax.axis_size("xy"), lax.axis_size("gz")
    geometry = (rows_x, rows_z, cols, rows_x * size_x, rows_z * size_z)
    pos = jnp.stack([lax.axis_index("xy"), lax.axis_index("gz")]).astype(jnp.int32)
    fields = (e_check, h_check, adj_e_end, adj_h_end, background, conductivity)
    f32 = jnp.float32
    params = pltpu.CompilerParams(vmem_limit_bytes=VMEM_LIMIT)

    def tiles(ref):
        return pltpu.VMEM(ref.shape[:-2] + (EXT, cols), f32)

    first_rows, last_rows = pl.pallas_call(
        edge_rows,
        out_shape=(
            jax.ShapeDtypeStruct((rows_x, FIRST_SIZE, cols), f32),
            jax.ShapeDtypeStruct((rows_x, LAST_SIZE, cols), f32),
        ),
        in_specs=[HBM] * 6,
        out_specs=[VMEM] * 2,
        scratch_shapes=[tiles(ref) for ref in fields for _ in range(2)]
        + [pltpu.SemaphoreType.DMA((12,))],
        compiler_params=pltpu.CompilerParams(vmem_limit_bytes=60 * 1024 * 1024),
        name="edge_rows",
    )(*fields)
    above = shifted(first_rows, "gz", -1)
    below = shifted(last_rows, "gz", 1)

    plane = (rows_z + EXT, cols)
    to_next, to_prev, tile = pl.pallas_call(
        functools.partial(edge_planes, geometry),
        out_shape=(
            jax.ShapeDtypeStruct((BACK_PLANES,) + plane, f32),
            jax.ShapeDtypeStruct((FRONT_PLANES,) + plane, f32),
            jax.ShapeDtypeStruct((SLOTS, rows_x, EXT, cols), f32),
        ),
        in_specs=[SMEM] * 3 + [VMEM] * 9,
        out_specs=[VMEM] * 3,
        compiler_params=params,
        name="edge_planes",
    )(pos, design_box, pml_width, pattern, *fields, above, below)
    back = shifted(to_next, "xy", 1)
    front = shifted(to_prev, "xy", -1)

    def planes(*lead):
        return pltpu.VMEM(lead + plane, f32)

    count = rows_x + 2
    back_e, back_h, local_sum = pl.pallas_call(
        functools.partial(sweep, geometry),
        out_shape=(
            jax.ShapeDtypeStruct(e_check.shape, f32),
            jax.ShapeDtypeStruct(e_check.shape, f32),
            jax.ShapeDtypeStruct((cols, cols), f32),
        ),
        in_specs=[SMEM] * 3 + [VMEM] * 10,
        out_specs=[VMEM] * 3,
        scratch_shapes=[planes(3, count)] * 4
        + [planes(count)] * 4
        + [planes(rows_x)] * 2
        + [pltpu.VMEM((rows_x, rows_z, cols), f32), pltpu.VMEM((cols, cols), f32)],
        compiler_params=params,
        name="sweep",
    )(pos, design_box, pml_width, pattern, *fields, tile, back, front)

    parts = lax.all_to_all(local_sum, "gz", split_axis=0, concat_axis=0, tiled=True)
    pattern_grad = pl.pallas_call(
        add_shares,
        out_shape=jax.ShapeDtypeStruct((cols // size_z, rows_x), f32),
        in_specs=[VMEM],
        out_specs=VMEM,
        name="add_shares",
    )(parts).T
    return (back_e, back_h, pattern_grad)


def solution(mesh):
    field = P(None, "xy", "gz", None)
    cell = P("xy", "gz", None)
    return jax.shard_map(
        shards,
        mesh=mesh,
        in_specs=(field, field, field, field, cell, cell, P("xy", None), P(), P()),
        out_specs=(field, field, P("xy", "gz")),
        check_vma=False,
    )
```

```python
import functools

import jax
import jax.numpy as jnp
from jax import lax
from jax.experimental import pallas as pl
from jax.experimental.pallas import tpu as pltpu
from jax.sharding import PartitionSpec as P

TIME_STEP = 0.5
SIGMA_PEAK = 1.0
HALF = TIME_STEP / 2
EXT = 8
UNROLL = 4
VMEM_LIMIT = 32 * 1024 * 1024
FIRST_VMEM_LIMIT = 60 * 1024 * 1024

FIRST_ROWS = (2, 2, 1, 1, 1, 1, 2, 2, 1, 1, 1, 1, 2, 2)
LAST_ROWS = (2, 2, 2, 2, 2, 1, 2, 2, 2, 2, 2, 1, 2, 2)
FIRST_AT = tuple(sum(FIRST_ROWS[:k]) for k in range(14))
LAST_AT = tuple(sum(LAST_ROWS[:k]) for k in range(14))
ROWS = max(sum(FIRST_ROWS), sum(LAST_ROWS))
SLOTS = 14
PLANES = 9
NEXT_ROWS = tuple((k, r) for k in (0, 1, 5, 6) for r in (0, -1)) + ((4, 0),)
PREV_ROWS = tuple(
    (k, r) for k, rs in ((0, (0, -1)), (1, (0, -2, -1)), (5, (0, -1)), (6, (0, -2, -1)))
    for r in rs
) + ((3, -1), (8, -1), (4, -1))
SINGLE_ROWS = 16
EDGE_PLANES = 38

HBM = pl.BlockSpec(memory_space=pltpu.HBM)
VMEM = pl.BlockSpec(memory_space=pltpu.VMEM)
SMEM = pl.BlockSpec(memory_space=pltpu.SMEM)


def swapped(shard, axis, first):
    size = lax.axis_size(axis)
    pairs = [(i, j) for k in range(first, size - 1, 2) for i, j in ((k, k + 1), (k + 1, k))]
    return lax.ppermute(shard, axis, pairs)


def swap_both(far, near, axis):
    far, near = swapped(far, axis, 1), swapped(near, axis, 0)
    return far, near


def is_even(axis):
    return lax.rem(lax.axis_index(axis), 2) == 0


def edge_rows(*refs):
    fields, pattern, outs, scratch = refs[:6], refs[6], refs[7:9], refs[9:]
    far_out, near_out = outs
    tiles, sems = scratch[:12], scratch[12]
    rows_z = fields[4].shape[1]
    copies = []
    for k, ref in enumerate(fields):
        for side, start in enumerate((0, rows_z - EXT)):
            src = ref.at[:, :, pl.ds(start, EXT), :] if k < 4 else ref.at[:, pl.ds(start, EXT), :]
            copy = pltpu.make_async_copy(src, tiles[2 * k + side], sems.at[2 * k + side])
            copy.start()
            copies.append(copy)
    rows_x = fields[4].shape[0]
    copy = pltpu.make_async_copy(pattern, near_out.at[pl.ds(rows_x * ROWS, rows_x)], sems.at[12])
    copy.start()
    copies.append(copy)
    for copy in copies:
        copy.wait()

    def write(first_out, last_out):
        for x in range(rows_x):
            for k in range(SLOTS):
                group = k // 3 if k < 12 else k - 8
                at = (k % 3, x) if k < 12 else (x,)
                low, high = tiles[2 * group], tiles[2 * group + 1]
                count, start = FIRST_ROWS[k], x * ROWS + FIRST_AT[k]
                first_out[start : start + count, :] = low[(*at, slice(0, count), slice(None))]
                count, start = LAST_ROWS[k], x * ROWS + LAST_AT[k]
                last_out[start : start + count, :] = high[(*at, slice(EXT - count, EXT), slice(None))]

    @pl.when(is_even("gz"))
    def _():
        write(far_out, near_out)

    @pl.when(~is_even("gz"))
    def _():
        write(near_out, far_out)


def lane_index(shape):
    return lax.broadcasted_iota(jnp.int32, shape, 1)


def y_ahead(v):
    cols = v.shape[1]
    moved = pltpu.roll(v, cols - 1, 1)
    return jnp.where(lane_index(v.shape) == cols - 1, 0.0, moved) - v


def y_behind(v):
    moved = pltpu.roll(v, 1, 1)
    return v - jnp.where(lane_index(v.shape) == 0, 0.0, moved)


def z_ahead(v):
    return pltpu.roll(v, v.shape[0] - 1, 0) - v


def z_behind(v):
    return v - pltpu.roll(v, 1, 0)


def plus_x(v):
    return y_ahead(v[2]) - z_ahead(v[1])


def plus_y(v, next_z):
    return z_ahead(v[0]) - (next_z - v[2])


def plus_z(v, next_y):
    return (next_y - v[1]) - y_ahead(v[0])


def plus(v, next_y, next_z):
    return plus_x(v), plus_y(v, next_z), plus_z(v, next_y)


def minus(v, prev_y, prev_z):
    return (
        y_behind(v[2]) - z_behind(v[1]),
        z_behind(v[0]) - (v[2] - prev_z),
        (v[1] - prev_y) - y_behind(v[0]),
    )


def plus_yz(v_y, v_z):
    return y_ahead(v_z) - z_ahead(v_y), v_z, -v_y


def minus_yz(v_y, v_z):
    return y_behind(v_z) - z_behind(v_y), -v_z, v_y


def dot(left, right):
    return sum(a * b for a, b in zip(left, right))


def depth_cube(place, total, layer):
    depth = jnp.maximum(jnp.maximum(layer - place, place - (total - 1 - layer)), 0.0) / layer
    return depth * depth * depth


class Grid:
    def __init__(self, box, pml, rows_x, rows_z, cols, total_x, total_z):
        rows = rows_z + EXT
        self.shape = (rows, cols)
        self.box = box
        self.width_x = pml[0].astype(jnp.float32)
        self.total_x = total_x
        self.x_start = lax.axis_index("xy") * rows_x
        self.rows_z = rows_z
        row = lax.broadcasted_iota(jnp.int32, self.shape, 0)
        z = lax.axis_index("gz") * rows_z + jnp.where(row < rows_z + EXT // 2, row, row - rows)
        y = lane_index(self.shape)
        self.inside = (z >= 0) & (z < total_z)
        self.sigma_zy = depth_cube(
            z.astype(jnp.float32), total_z, pml[2].astype(jnp.float32)
        ) + depth_cube(y.astype(jnp.float32), cols, pml[1].astype(jnp.float32))
        picked = (z >= box[4]) & (z < box[5]) & (y >= box[2]) & (y < box[3])
        self.mask_zy = jnp.where(picked, 1.0, 0.0)

    def sigma(self, x):
        place = jnp.full((1, self.shape[1]), (self.x_start + x).astype(jnp.float32))
        return SIGMA_PEAK * (self.sigma_zy + depth_cube(place, self.total_x, self.width_x))

    def mask_x(self, x):
        at = self.x_start + x
        return jnp.where((at >= self.box[0]) & (at < self.box[1]), 1.0, 0.0)

    def magnetic(self, sigma, x_inside=None):
        inside = self.inside if x_inside is None else self.inside & x_inside
        inverse = 1.0 / (1.0 + HALF * sigma)
        return (
            jnp.where(inside, 2.0 * inverse - 1.0, 0.0),
            jnp.where(inside, TIME_STEP * inverse, 0.0),
        )

    def electric(self, x, background, conductivity, pattern_row, sigma):
        permittivity = background + self.mask_zy * (pattern_row * self.mask_x(x))
        loss = HALF * (conductivity + sigma)
        inverse = jnp.where(self.inside, 1.0 / (permittivity + loss), 0.0)
        return (permittivity - loss) * inverse, TIME_STEP * inverse, loss, inverse


def full_plane(ref, tile_ref, k, x):
    own = ref[k % 3, x] if k < 12 else ref[x]
    return jnp.concatenate([own, tile_ref[k, x]], axis=0)


def fill_tile(tile_ref, far, near, even, k, x):
    for count, at, start in (
        (FIRST_ROWS[k], FIRST_AT[k], 0),
        (LAST_ROWS[k], LAST_AT[k], EXT - LAST_ROWS[k]),
    ):
        rows = pl.ds(x * ROWS + at, count)
        own, other = (near, far) if start == 0 else (far, near)
        tile_ref[k, x, pl.ds(start, count), :] = jnp.where(even, own[rows, :], other[rows, :])


def field_ref(fields, k):
    return fields[k // 3] if k < 12 else fields[k - 8]


def triple(fields, tile_ref, group, x):
    return tuple(full_plane(fields[group], tile_ref, 3 * group + c, x) for c in range(3))


def edge_planes(geometry, box, pml, *refs):
    fields, (rows_far, rows_near), (far, near) = refs[:6], refs[6:8], refs[8:10]
    tile, buffers, planes = refs[10], refs[11:13], refs[13]
    rows_x, rows_z = geometry[:2]
    grid = Grid(box, pml, *geometry)
    even = is_even("gz")
    for x in (0, 1, rows_x - 2, rows_x - 1):
        for k in range(SLOTS):
            tile[k, x] = jnp.zeros(tile.shape[2:], jnp.float32)
            fill_tile(tile, rows_far, rows_near, even, k, x)

    def coefs(x):
        sigma = grid.sigma(x)
        coef_a, coef_b, _, _ = grid.electric(
            x,
            full_plane(fields[4], tile, 12, x),
            full_plane(fields[5], tile, 13, x),
            rows_near[pl.ds(rows_x * ROWS + x, 1), :],
            sigma,
        )
        return (coef_a, coef_b) + grid.magnetic(sigma)

    def load(x):
        return [triple(fields, tile, g, x) for g in range(4)]

    def pack(buffer, values, rows):
        for k, value in enumerate(values):
            buffer[pl.ds(k * rows_z, rows_z), :] = value[:rows_z]
            planes[k] = value
        start = PLANES * rows_z
        buffer[pl.ds(start, SINGLE_ROWS), :] = jnp.zeros((SINGLE_ROWS, value.shape[1]), jnp.float32)
        for i, (k, r) in enumerate(rows):
            at = rows_z + r if r >= 0 else rows_z + EXT + r
            buffer[pl.ds(start + i, 1), :] = planes[k, pl.ds(at, 1), :]

    one, two = rows_x - 2, rows_x - 1
    e1, h1, p1, q1 = load(one)
    e2, h2, p2, q2 = load(two)
    _, cb1, da1, db1 = coefs(one)
    ca2, cb2, da2, db2 = coefs(two)
    before = (
        da1 * h1[1] - db1 * plus_y(e1, e2[2]),
        da1 * h1[2] - db1 * plus_z(e1, e2[1]),
    )
    mag = [da2 * h - db2 * c for h, c in zip(h2, plus(e2, 0.0, 0.0))]
    ele = [ca2 * e + cb2 * c for e, c in zip(e2, minus(mag, *before))]
    mag2 = (
        da2 * mag[1] - db2 * plus_y(ele, 0.0),
        da2 * mag[2] - db2 * plus_z(ele, 0.0),
    )
    u1 = [cb1 * v for v in p1]
    u2 = [cb2 * v for v in p2]
    before = (
        db1 * (q1[1] + plus_y(u1, u2[2])),
        db1 * (q1[2] + plus_z(u1, u2[1])),
    )
    adj = [q + c for q, c in zip(q2, plus(u2, 0.0, 0.0))]
    curl = minus([db2 * v for v in adj], *before)
    u2 = [cb2 * (ca2 * p - c) for p, c in zip(p2, curl)]
    adj2 = (da2 * adj[1] + plus_y(u2, 0.0), da2 * adj[2] + plus_z(u2, 0.0))
    pack(buffers[0], (mag[1], mag[2]) + mag2 + (cb2, adj[1], adj[2]) + adj2, NEXT_ROWS)

    e1, h1, p1, q1 = load(0)
    e2, _, p2, _ = load(1)
    ca1, cb1, da1, db1 = coefs(0)
    _, cb2, _, _ = coefs(1)
    mag = [da1 * h - db1 * c for h, c in zip(h1, plus(e1, e2[1], e2[2]))]
    curl = minus(mag, 0.0, 0.0)
    ele = (ca1 * e1[1] + cb1 * curl[1], ca1 * e1[2] + cb1 * curl[2])
    u1 = [cb1 * v for v in p1]
    adj = [db1 * (q + c) for q, c in zip(q1, plus(u1, cb2 * p2[1], cb2 * p2[2]))]
    curl = minus(adj, 0.0, 0.0)
    adj_ele = (ca1 * p1[1] - curl[1], ca1 * p1[2] - curl[2])
    pack(buffers[1], e1[1:] + ele + (cb1, u1[1], u1[2]) + adj_ele, PREV_ROWS)

    even = is_even("xy")
    to_next, to_prev = buffers[0][...], buffers[1][...]
    far[...] = jnp.where(even, to_prev, to_next)
    near[...] = jnp.where(even, to_next, to_prev)


def sweep(geometry, box, pml, *refs):
    fields, (rows_far, rows_near) = refs[:6], refs[6:8]
    full_e, full_h, grad, edge, edge_e, edge_h = refs[8:14]
    tile, mag, adj_mag, ele, adj_ele, ca, cb, da, db = refs[14:23]
    by_e, by_r, sums, out_e, out_h, sems = refs[23:]
    rows_x, rows_z, cols = geometry[:3]
    grid = Grid(box, pml, *geometry)
    last = rows_x - 1
    own = pl.ds(0, rows_z)
    even = is_even("gz")
    tile[...] = jnp.zeros(tile.shape, jnp.float32)
    for x in range(rows_x):
        for k in range(SLOTS):
            fill_tile(tile, rows_far, rows_near, even, k, x)

    def coefs(x, carry):
        sigma = grid.sigma(x)
        ca[x], cb[x], loss, inverse = grid.electric(
            x,
            full_plane(fields[4], tile, 12, x),
            full_plane(fields[5], tile, 13, x),
            rows_near[pl.ds(rows_x * ROWS + x, 1), :],
            sigma,
        )
        da[x], db[x] = grid.magnetic(sigma)
        weight = (inverse * inverse * (grid.mask_zy * grid.mask_x(x)))[:rows_z]
        by_e[x] = 2.0 * loss[:rows_z] * weight
        by_r[x] = -TIME_STEP * weight
        return carry

    lax.fori_loop(0, rows_x, coefs, 0, unroll=UNROLL)
    zero = jnp.zeros(grid.shape, jnp.float32)
    cb[rows_x] = zero
    for k in (1, 2):
        ele[k, rows_x] = zero
        adj_ele[k, rows_x] = zero

    def first(x, carry):
        prev_h, prev_m = carry
        at_last = jnp.full(grid.shape, x) == last
        ahead = jnp.minimum(x + 1, last)
        e, h, p, q = [triple(fields, tile, g, x) for g in range(4)]
        a, b, c, d = ca[x], cb[x], da[x], db[x]
        e_y = jnp.where(at_last, 0.0, full_plane(fields[0], tile, 1, ahead))
        e_z = jnp.where(at_last, 0.0, full_plane(fields[0], tile, 2, ahead))
        new_h = [c * v - d * w for v, w in zip(h, plus(e, e_y, e_z))]
        curl = minus(new_h, *prev_h)
        b_ahead = cb[x + 1]
        u_y = b_ahead * full_plane(fields[2], tile, 7, ahead)
        u_z = b_ahead * full_plane(fields[2], tile, 8, ahead)
        new_m = [v + w for v, w in zip(q, plus([b * v for v in p], u_y, u_z))]
        scaled = [d * v for v in new_m]
        adj_curl = minus(scaled, *prev_m)
        dot_e, dot_r = 0.0, 0.0
        for k in range(3):
            mag[k, x] = new_h[k]
            adj_mag[k, x] = new_m[k]
            ele[k, x] = a * e[k] + b * curl[k]
            new_p = a * p[k] - adj_curl[k]
            adj_ele[k, x] = new_p
            dot_e = dot_e + new_p[:rows_z] * e[k][:rows_z]
            dot_r = dot_r + new_p[:rows_z] * curl[k][:rows_z]
        sums[x] = by_e[x] * dot_e + by_r[x] * dot_r

        @pl.when((x == 0) | (x == last))
        def _():
            at = jnp.where(x == 0, 0, 3)
            for k in range(3):
                edge[at + k] = curl[k]

        return new_h[1:], scaled[1:]

    lax.fori_loop(0, rows_x, first, ([zero, zero], [zero, zero]), unroll=UNROLL)

    def out_copies(x):
        return [
            pltpu.make_async_copy(ref.at[:, pl.ds(x, 1)], full.at[:, pl.ds(x, 1)], sems.at[i, x])
            for i, (ref, full) in enumerate(((out_e, full_e), (out_h, full_h)))
        ]

    def second(x, carry):
        prev_h, prev_m = carry
        e = [ele[k, x] for k in range(3)]
        p1 = [adj_ele[k, x] for k in range(3)]
        a, b, c, d = ca[x], cb[x], da[x], db[x]
        new_h = [
            c * mag[k, x] - d * w for k, w in enumerate(plus(e, ele[1, x + 1], ele[2, x + 1]))
        ]
        curl = minus(new_h, *prev_h)
        b_ahead = cb[x + 1]
        u = [b * v for v in p1]
        ahead = plus(u, b_ahead * adj_ele[1, x + 1], b_ahead * adj_ele[2, x + 1])
        new_m = [c * adj_mag[k, x] + w for k, w in enumerate(ahead)]
        scaled = [d * v for v in new_m]
        adj_curl = minus(scaled, *prev_m)
        dot_e, dot_r = 0.0, 0.0
        for k in range(3):
            out_h[k, x] = c[:rows_z] * new_m[k][:rows_z]
            out_e[k, x] = a[:rows_z] * p1[k][:rows_z] - adj_curl[k][:rows_z]
            p = fields[2][k, x]
            dot_e = dot_e + p * e[k][:rows_z]
            dot_r = dot_r + p * curl[k][:rows_z]
        terms = sums[x] + by_e[x] * dot_e + by_r[x] * dot_r
        total = terms[0:8]
        for start in range(8, rows_z, 8):
            total = total + terms[start : start + 8]
        grad[pl.ds(x, 1), :] = jnp.sum(total, axis=0, keepdims=True)

        @pl.when((x > 1) & (x < last - 1))
        def _():
            for copy in out_copies(x):
                copy.start()

        return new_h[1:], scaled[1:]

    lax.fori_loop(0, rows_x, second, ([zero, zero], [zero, zero]), unroll=UNROLL)

    kept = [ele[1, 0], ele[2, 0]] + [adj_ele[k, 0] for k in range(3)]
    kept += [mag[1, last], mag[2, last], db[last] * adj_mag[1, last], db[last] * adj_mag[2, last]]
    kept += [adj_ele[k, last] for k in range(3)]
    kept += [ref[x] for x in (0, last) for ref in (ca, cb, da, db)] + [da[last - 1], db[last - 1]]
    kept += [full_plane(fields[0], tile, k, 0) for k in (1, 2)]
    kept += [cb[0] * full_plane(fields[2], tile, k, 0) for k in (7, 8)]
    for k, value in enumerate(kept):
        edge[6 + k] = value
    start = 6 + len(kept)
    for k, value in enumerate((by_e[0], by_r[0], by_r[1], by_r[last - 1], by_e[last], by_r[last])):
        edge[start + k, own, :] = value
    for i, x in enumerate((0, 1, last - 1, last)):
        for k in range(3):
            edge_e[k, i] = out_e[k, x]
            edge_h[k, i] = out_h[k, x]
    for x in range(2, last - 1):
        for copy in out_copies(x):
            copy.wait()


def response(geometry, box, pml, *refs):
    e_ref, p_ref, edge, local_e, local_h, local_grad, far, near = refs[:8]
    edge_e, edge_h, shares, buffers, tile, grad = refs[8:]
    rows_x, rows_z, cols = geometry[:3]
    last = rows_x - 1
    grid = Grid(box, pml, *geometry)
    even = is_even("xy")
    buffers[0] = jnp.where(even, far[...], near[...])
    buffers[1] = jnp.where(even, near[...], far[...])
    grad[...] = jnp.zeros(grad.shape, jnp.float32)
    grad[pl.ds(0, rows_x), :] = local_grad[...]
    for side, rows in enumerate((NEXT_ROWS, PREV_ROWS)):
        for k in range(PLANES):
            tile[side, k] = jnp.zeros(tile.shape[2:], jnp.float32)
        for i, (k, r) in enumerate(rows):
            row = buffers[side, pl.ds(PLANES * rows_z + i, 1), :]
            tile[side, k, pl.ds(r if r >= 0 else EXT + r, 1), :] = row

    def unpack(side):
        return [
            jnp.concatenate([buffers[side, pl.ds(k * rows_z, rows_z), :], tile[side, k]], axis=0)
            for k in range(PLANES)
        ]

    def own(v):
        return v[:rows_z]

    def weight(k):
        return edge[32 + k, pl.ds(0, rows_z), :]

    def add_rows(x, terms):
        total = terms[0:8]
        for start in range(8, rows_z, 8):
            total = total + terms[start : start + 8]
        grad[pl.ds(x, 1), :] += jnp.sum(total, axis=0, keepdims=True)

    def write(ref, local, i, change, scale=1.0):
        for k in range(3):
            ref[k, i] = local[k, i] if change[k] is None else local[k, i] + own(change[k])

    h_y, h_z, h2_y, h2_z, cb_b, m_y, m_z, m2_y, m2_z = unpack(0)
    at = jnp.full(grid.shape, grid.x_start)
    da_b, db_b = grid.magnetic(grid.sigma(-1), at > 0)
    ca_f, cb_f, da_f, db_f = (edge[18 + k] for k in range(4))
    e_y, e_z, u_y, u_z = (edge[28 + k] for k in range(4))
    dh_y, dh_z = db_b * e_z, -(db_b * e_y)
    h_y, h_z = h_y + dh_y, h_z + dh_z
    d_ele = (cb_f * h_z, -(cb_f * h_y))
    ele_y, ele_z = edge[6] + d_ele[0], edge[7] + d_ele[1]
    back = [cb_b * v for v in minus_yz(dh_y, dh_z)]
    h2_y = h2_y + da_b * dh_y - db_b * plus_y(back, ele_z)
    h2_z = h2_z + da_b * dh_z - db_b * plus_z(back, ele_y)
    dm_y, dm_z = -u_z, u_y
    n_y, n_z = db_b * (m_y + dm_y), db_b * (m_z + dm_z)
    d_p = (-n_z, n_y)
    p_y, p_z = edge[9] + d_p[0], edge[10] + d_p[1]
    back = [-(cb_b * v) for v in minus_yz(db_b * dm_y, db_b * dm_z)]
    m2_y = m2_y + da_b * dm_y + plus_y(back, cb_f * p_z)
    m2_z = m2_z + da_b * dm_z + plus_z(back, cb_f * p_y)
    d_h2 = [-(db_f * v) for v in plus_yz(*d_ele)]
    d_m2 = plus_yz(cb_f * d_p[0], cb_f * d_p[1])
    d_r2 = minus(d_h2, h2_y, h2_z)
    d_n2 = [db_f * v for v in d_m2]
    curl = minus(d_n2, db_b * m2_y, db_b * m2_z)
    write(edge_e, local_e, 0, (-curl[0], ca_f * d_p[0] - curl[1], ca_f * d_p[1] - curl[2]))
    write(edge_e, local_e, 1, (None, -d_n2[2], d_n2[1]))
    write(edge_h, local_h, 0, [da_f * v for v in d_m2])
    write(edge_h, local_h, 1, (None, None, None))
    p2 = [p_ref[k, 0] for k in range(3)]
    along_e = sum(
        own(d_p[k - 1]) * e_ref[k, 0] + p2[k] * own(d_ele[k - 1]) for k in (1, 2)
    )
    along_r = dot(p2, [own(v) for v in d_r2])
    along_r = along_r + own(d_p[0] * edge[1] + d_p[1] * edge[2] + p_y * h_z - p_z * h_y)
    add_rows(0, weight(0) * along_e + weight(1) * along_r)
    add_rows(1, weight(2) * (p_ref[1, 1] * own(d_h2[2]) - p_ref[2, 1] * own(d_h2[1])))

    e_y, e_z, e1_y, e1_z, cb_n, u_y, u_z, p_y, p_z = unpack(1)
    ca_l, cb_l, da_l, db_l = (edge[22 + k] for k in range(4))
    da_k, db_k = edge[26], edge[27]
    dh_y, dh_z = db_l * e_z, -(db_l * e_y)
    dm_y, dm_z = -u_z, u_y
    dn_y, dn_z = db_l * dm_y, db_l * dm_z
    d_r1 = minus_yz(dh_y, dh_z)
    d_ele = [cb_l * v for v in d_r1]
    d_p = [-v for v in minus_yz(dn_y, dn_z)]
    e1_y = e1_y + cb_n * (edge[12] + dh_z)
    e1_z = e1_z - cb_n * (edge[11] + dh_y)
    p_y = p_y - (edge[14] + dn_z)
    p_z = p_z + (edge[13] + dn_y)
    d_h2 = [-(db_l * v) for v in plus(d_ele, e1_y, e1_z)]
    d_h2 = [d_h2[0], d_h2[1] + da_l * dh_y, d_h2[2] + da_l * dh_z]
    d_u = [cb_l * v for v in d_p]
    d_m2 = plus(d_u, cb_n * p_y, cb_n * p_z)
    d_m2 = [d_m2[0], d_m2[1] + da_l * dm_y, d_m2[2] + da_l * dm_z]
    k_h2 = (db_k * d_ele[2], -(db_k * d_ele[1]))
    k_m2 = (-d_u[2], d_u[1])
    k_n2 = (db_k * k_m2[0], db_k * k_m2[1])
    k_r2 = minus_yz(*k_h2)
    d_r2 = minus(d_h2, *k_h2)
    write(edge_e, local_e, 2, [-v for v in minus_yz(*k_n2)])
    curl = minus([db_l * v for v in d_m2], *k_n2)
    write(edge_e, local_e, 3, [ca_l * v - c for v, c in zip(d_p, curl)])
    write(edge_h, local_h, 2, (None, da_k * k_m2[0], da_k * k_m2[1]))
    write(edge_h, local_h, 3, [da_l * v for v in d_m2])
    p2 = [p_ref[k, last] for k in range(3)]
    along_e = dot([own(v) for v in d_p], [e_ref[k, last] for k in range(3)])
    along_e = along_e + dot(p2, [own(v) for v in d_ele])
    along_r = dot(p2, [own(v) for v in d_r2])
    for k in range(3):
        new_p = own(edge[15 + k] + d_p[k])
        along_r = along_r + own(d_p[k] * edge[3 + k]) + new_p * own(d_r1[k])
    add_rows(last, weight(4) * along_e + weight(5) * along_r)
    p2 = [p_ref[k, last - 1] for k in range(3)]
    add_rows(last - 1, weight(3) * dot(p2, [own(v) for v in k_r2]))

    shares[...] = jnp.transpose(grad[...])


def finish(parts, edge_e, edge_h, in_e, in_h, out_e, out_h, out, sems):
    last = out_e.shape[1] - 2
    copies = []
    for i, (edge, full) in enumerate(((edge_e, out_e), (edge_h, out_h))):
        for side, start in enumerate((0, last)):
            copy = pltpu.make_async_copy(
                edge.at[:, pl.ds(2 * side, 2)], full.at[:, pl.ds(start, 2)], sems.at[2 * i + side]
            )
            copy.start()
            copies.append(copy)
    share, rows_x = out.shape
    total = parts[pl.ds(0, share), :]
    for j in range(1, parts.shape[0] // share):
        total = total + parts[pl.ds(j * share, share), :]
    out[...] = total[:, :rows_x]
    for copy in copies:
        copy.wait()


def shards(
    e_check, h_check, adj_e_end, adj_h_end, background, conductivity, pattern, design_box, pml_width
):
    rows_x, rows_z, cols = background.shape
    size_x, size_z = lax.axis_size("xy"), lax.axis_size("gz")
    geometry = (rows_x, rows_z, cols, rows_x * size_x, rows_z * size_z)
    fields = (e_check, h_check, adj_e_end, adj_h_end, background, conductivity)
    f32 = jnp.float32
    params = pltpu.CompilerParams(vmem_limit_bytes=VMEM_LIMIT)

    def array(*shape):
        return jax.ShapeDtypeStruct(shape, f32)

    def tiles(ref):
        return pltpu.VMEM(ref.shape[:-2] + (EXT, cols), f32)

    rows_far, rows_near = pl.pallas_call(
        edge_rows,
        out_shape=(array(rows_x * ROWS, cols), array(rows_x * ROWS + rows_x, cols)),
        in_specs=[HBM] * 7,
        out_specs=[VMEM] * 2,
        scratch_shapes=[tiles(ref) for ref in fields for _ in range(2)]
        + [pltpu.SemaphoreType.DMA((13,))],
        compiler_params=pltpu.CompilerParams(vmem_limit_bytes=FIRST_VMEM_LIMIT),
        name="edge_rows",
    )(*fields, pattern)
    rows_far, rows_near = swap_both(rows_far, rows_near, "gz")

    def planes(*lead):
        return pltpu.VMEM(lead + (rows_z + EXT, cols), f32)

    size = PLANES * rows_z + SINGLE_ROWS
    message = pltpu.VMEM((size, cols), f32)
    tile = pltpu.VMEM((SLOTS, rows_x, EXT, cols), f32)
    far, near = pl.pallas_call(
        functools.partial(edge_planes, geometry),
        out_shape=(array(size, cols),) * 2,
        in_specs=[SMEM] * 2 + [VMEM] * 8,
        out_specs=[VMEM] * 2,
        scratch_shapes=[tile, message, message, planes(PLANES)],
        compiler_params=params,
        name="edge_planes",
    )(design_box, pml_width, *fields, rows_far, rows_near)
    far, near = swap_both(far, near, "xy")

    count = rows_x + 1
    local_e, local_h, local_grad, edge, edge_e, edge_h = pl.pallas_call(
        functools.partial(sweep, geometry),
        out_shape=(
            array(*e_check.shape),
            array(*e_check.shape),
            array(rows_x, cols),
            array(EDGE_PLANES, rows_z + EXT, cols),
            array(3, 4, rows_z, cols),
            array(3, 4, rows_z, cols),
        ),
        in_specs=[SMEM] * 2 + [VMEM] * 8,
        out_specs=[HBM] * 2 + [VMEM] * 4,
        scratch_shapes=[tile]
        + [planes(3, count)] * 4
        + [planes(count)] * 4
        + [pltpu.VMEM((rows_x, rows_z, cols), f32)] * 3
        + [pltpu.VMEM((3, rows_x, rows_z, cols), f32)] * 2
        + [pltpu.SemaphoreType.DMA((2, rows_x))],
        compiler_params=params,
        cost_estimate=pl.CostEstimate(flops=50000000, bytes_accessed=8000000, transcendentals=0),
        name="sweep",
    )(design_box, pml_width, *fields, rows_far, rows_near)

    edge_e, edge_h, shares = pl.pallas_call(
        functools.partial(response, geometry),
        out_shape=(array(*edge_e.shape), array(*edge_h.shape), array(cols, cols)),
        in_specs=[SMEM] * 2 + [VMEM] * 8,
        out_specs=[VMEM] * 3,
        scratch_shapes=[
            pltpu.VMEM((2, size, cols), f32),
            pltpu.VMEM((2, PLANES, EXT, cols), f32),
            pltpu.VMEM((cols, cols), f32),
        ],
        compiler_params=params,
        name="response",
    )(design_box, pml_width, e_check, adj_e_end, edge, edge_e, edge_h, local_grad, far, near)

    parts = lax.all_to_all(shares, "gz", split_axis=0, concat_axis=0, tiled=True)
    back_e, back_h, pattern_grad = pl.pallas_call(
        finish,
        out_shape=(array(*e_check.shape), array(*e_check.shape), array(cols // size_z, rows_x)),
        in_specs=[VMEM] * 3 + [HBM] * 2,
        out_specs=[HBM] * 2 + [VMEM],
        scratch_shapes=[pltpu.SemaphoreType.DMA((4,))],
        input_output_aliases={3: 0, 4: 1},
        compiler_params=pltpu.CompilerParams(vmem_limit_bytes=8 * 1024 * 1024),
        name="finish",
    )(parts, edge_e, edge_h, local_e, local_h)
    return (back_e, back_h, pattern_grad.T)


def solution(mesh):
    field = P(None, "xy", "gz", None)
    cell = P("xy", "gz", None)
    return jax.shard_map(
        shards,
        mesh=mesh,
        in_specs=(field, field, field, field, cell, cell, P("xy", None), P(), P()),
        out_specs=(field, field, P("xy", "gz")),
        check_vma=False,
    )
```

```python
import functools

import jax
import jax.numpy as jnp
from jax import lax
from jax.experimental import pallas as pl
from jax.experimental.pallas import tpu as pltpu
from jax.sharding import PartitionSpec as P

TIME_STEP = 0.5
SIGMA_PEAK = 1.0
HALF = TIME_STEP / 2
EXT = 8
UNROLL = 4
VMEM_LIMIT = 32 * 1024 * 1024

FIRST_ROWS = (2, 2, 1, 1, 1, 1, 2, 2, 1, 1, 1, 1, 2, 2)
LAST_ROWS = (2, 2, 2, 2, 2, 1, 2, 2, 2, 2, 2, 1, 2, 2)
FIRST_AT = tuple(sum(FIRST_ROWS[:k]) for k in range(14))
LAST_AT = tuple(sum(LAST_ROWS[:k]) for k in range(14))
ROWS = max(sum(FIRST_ROWS), sum(LAST_ROWS))
PERIOD = 4
SLOTS = 14
PLANES = 9
NEXT_ROWS = tuple((k, r) for k in (0, 1, 5, 6) for r in (0, -1)) + ((4, 0),)
PREV_ROWS = tuple(
    (k, r) for k, rs in ((0, (0, -1)), (1, (0, -2, -1)), (5, (0, -1)), (6, (0, -2, -1)))
    for r in rs
) + ((3, -1), (8, -1), (4, -1))
SINGLE_ROWS = 16
EDGE_PLANES = 38

HBM = pl.BlockSpec(memory_space=pltpu.HBM)
VMEM = pl.BlockSpec(memory_space=pltpu.VMEM)
SMEM = pl.BlockSpec(memory_space=pltpu.SMEM)


def swapped(shard, axis, first):
    size = lax.axis_size(axis)
    pairs = [(i, j) for k in range(first, size - 1, 2) for i, j in ((k, k + 1), (k + 1, k))]
    return lax.ppermute(shard, axis, pairs)


def swap_both(far, near, axis):
    far, near = swapped(far, axis, 1), swapped(near, axis, 0)
    return far, near


def is_even(axis):
    return lax.rem(lax.axis_index(axis), 2) == 0


def rows_of(ref, group):
    return ref.at[pl.ds(pl.multiple_of(group * (PERIOD * ROWS), 8), PERIOD * ROWS)]


def load_fields(*refs):
    sources, copies_of, (far, near) = refs[:9], refs[9:18], refs[18:20]
    first, last, sems = refs[20:]
    rows_x, rows_z = sources[4].shape[:2]
    copies = []
    for i, (source, target) in enumerate(zip(sources, copies_of)):
        copy = pltpu.make_async_copy(source, target, sems.at[i])
        copy.start()
        copies.append(copy)

    for i in range(6):
        copies[i].wait()
        field = copies_of[i]

        def pack(group, carry):
            first_rows, last_rows = rows_of(first, group), rows_of(last, group)
            for n in range(PERIOD):
                x = group * PERIOD + n
                for k in range(3 * i, 3 * i + 3) if i < 4 else (8 + i,):
                    at = (k % 3, x) if i < 4 else (x,)
                    count, start = FIRST_ROWS[k], n * ROWS + FIRST_AT[k]
                    rows = field[(*at, slice(0, count), slice(None))]
                    first_rows[start : start + count, :] = rows
                    count, start = LAST_ROWS[k], n * ROWS + LAST_AT[k]
                    rows = field[(*at, slice(rows_z - count, rows_z), slice(None))]
                    last_rows[start : start + count, :] = rows
            return carry

        lax.fori_loop(0, rows_x // PERIOD, pack, 0)
    for copy in copies[6:]:
        copy.wait()
    even = is_even("gz")
    far[...] = jnp.where(even, first[...], last[...])
    near[...] = jnp.where(even, last[...], first[...])


def lane_index(shape):
    return lax.broadcasted_iota(jnp.int32, shape, 1)


def y_ahead(v):
    cols = v.shape[1]
    moved = pltpu.roll(v, cols - 1, 1)
    return jnp.where(lane_index(v.shape) == cols - 1, 0.0, moved) - v


def y_behind(v):
    moved = pltpu.roll(v, 1, 1)
    return v - jnp.where(lane_index(v.shape) == 0, 0.0, moved)


def z_ahead(v):
    return pltpu.roll(v, v.shape[0] - 1, 0) - v


def z_behind(v):
    return v - pltpu.roll(v, 1, 0)


def plus_x(v):
    return y_ahead(v[2]) - z_ahead(v[1])


def plus_y(v, next_z):
    return z_ahead(v[0]) - (next_z - v[2])


def plus_z(v, next_y):
    return (next_y - v[1]) - y_ahead(v[0])


def plus(v, next_y, next_z):
    return plus_x(v), plus_y(v, next_z), plus_z(v, next_y)


def minus(v, prev_y, prev_z):
    return (
        y_behind(v[2]) - z_behind(v[1]),
        z_behind(v[0]) - (v[2] - prev_z),
        (v[1] - prev_y) - y_behind(v[0]),
    )


def plus_yz(v_y, v_z):
    return y_ahead(v_z) - z_ahead(v_y), v_z, -v_y


def minus_yz(v_y, v_z):
    return y_behind(v_z) - z_behind(v_y), -v_z, v_y


def dot(left, right):
    return sum(a * b for a, b in zip(left, right))


def depth_cube(place, total, layer):
    depth = jnp.maximum(jnp.maximum(layer - place, place - (total - 1 - layer)), 0.0) / layer
    return depth * depth * depth


class Grid:
    def __init__(self, box, pml, rows_x, rows_z, cols, total_x, total_z):
        rows = rows_z + EXT
        self.shape = (rows, cols)
        self.box = box
        self.width_x = pml[0].astype(jnp.float32)
        self.total_x = total_x
        self.x_start = lax.axis_index("xy") * rows_x
        self.rows_z = rows_z
        row = lax.broadcasted_iota(jnp.int32, self.shape, 0)
        z = lax.axis_index("gz") * rows_z + jnp.where(row < rows_z + EXT // 2, row, row - rows)
        y = lane_index(self.shape)
        self.inside = (z >= 0) & (z < total_z)
        self.sigma_zy = depth_cube(
            z.astype(jnp.float32), total_z, pml[2].astype(jnp.float32)
        ) + depth_cube(y.astype(jnp.float32), cols, pml[1].astype(jnp.float32))
        picked = (z >= box[4]) & (z < box[5]) & (y >= box[2]) & (y < box[3])
        self.mask_zy = jnp.where(picked, 1.0, 0.0)

    def sigma(self, x):
        place = jnp.full((1, self.shape[1]), (self.x_start + x).astype(jnp.float32))
        return SIGMA_PEAK * (self.sigma_zy + depth_cube(place, self.total_x, self.width_x))

    def mask_x(self, x):
        at = self.x_start + x
        return jnp.where((at >= self.box[0]) & (at < self.box[1]), 1.0, 0.0)

    def magnetic(self, sigma, x_inside=None):
        inside = self.inside if x_inside is None else self.inside & x_inside
        inverse = 1.0 / (1.0 + HALF * sigma)
        return (
            jnp.where(inside, 2.0 * inverse - 1.0, 0.0),
            jnp.where(inside, TIME_STEP * inverse, 0.0),
        )

    def electric(self, x, background, conductivity, pattern_row, sigma):
        permittivity = background + self.mask_zy * (pattern_row * self.mask_x(x))
        loss = HALF * (conductivity + sigma)
        inverse = jnp.where(self.inside, 1.0 / (permittivity + loss), 0.0)
        return (permittivity - loss) * inverse, TIME_STEP * inverse, loss, inverse


def full_plane(ref, tile_ref, k, x):
    own = ref[k % 3, x] if k < 12 else ref[x]
    return jnp.concatenate([own, tile_ref[k, x]], axis=0)


def fill_tiles(tile_ref, far, near, even, group, planes):
    far, near = rows_of(far, group), rows_of(near, group)
    for n in planes:
        x = group * PERIOD + n
        for k in range(SLOTS):
            tile_ref[k, x] = jnp.zeros(tile_ref.shape[2:], jnp.float32)
            for count, at, start in (
                (FIRST_ROWS[k], FIRST_AT[k], 0),
                (LAST_ROWS[k], LAST_AT[k], EXT - LAST_ROWS[k]),
            ):
                rows = pl.ds(n * ROWS + at, count)
                own, other = (near, far) if start == 0 else (far, near)
                tile_ref[k, x, pl.ds(start, count), :] = jnp.where(even, own[rows, :], other[rows, :])


def triple(fields, tile_ref, group, x):
    return tuple(full_plane(fields[group], tile_ref, 3 * group + c, x) for c in range(3))


def edge_planes(geometry, box, pml, *refs):
    fields, pattern, (rows_far, rows_near) = refs[:6], refs[6], refs[7:9]
    far, near, tile, buffers, planes = refs[9], refs[10], refs[11], refs[12:14], refs[14]
    rows_x, rows_z = geometry[:2]
    grid = Grid(box, pml, *geometry)
    even = is_even("gz")
    fill_tiles(tile, rows_far, rows_near, even, 0, (0, 1))
    fill_tiles(tile, rows_far, rows_near, even, rows_x // PERIOD - 1, (PERIOD - 2, PERIOD - 1))

    def coefs(x):
        sigma = grid.sigma(x)
        coef_a, coef_b, _, _ = grid.electric(
            x,
            full_plane(fields[4], tile, 12, x),
            full_plane(fields[5], tile, 13, x),
            pattern[pl.ds(x, 1), :],
            sigma,
        )
        return (coef_a, coef_b) + grid.magnetic(sigma)

    def load(x):
        return [triple(fields, tile, g, x) for g in range(4)]

    def pack(buffer, values, rows):
        for k, value in enumerate(values):
            buffer[pl.ds(k * rows_z, rows_z), :] = value[:rows_z]
            planes[k] = value
        start = PLANES * rows_z
        buffer[pl.ds(start, SINGLE_ROWS), :] = jnp.zeros((SINGLE_ROWS, value.shape[1]), jnp.float32)
        for i, (k, r) in enumerate(rows):
            at = rows_z + r if r >= 0 else rows_z + EXT + r
            buffer[pl.ds(start + i, 1), :] = planes[k, pl.ds(at, 1), :]

    one, two = rows_x - 2, rows_x - 1
    e1, h1, p1, q1 = load(one)
    e2, h2, p2, q2 = load(two)
    _, cb1, da1, db1 = coefs(one)
    ca2, cb2, da2, db2 = coefs(two)
    before = (
        da1 * h1[1] - db1 * plus_y(e1, e2[2]),
        da1 * h1[2] - db1 * plus_z(e1, e2[1]),
    )
    mag = [da2 * h - db2 * c for h, c in zip(h2, plus(e2, 0.0, 0.0))]
    ele = [ca2 * e + cb2 * c for e, c in zip(e2, minus(mag, *before))]
    mag2 = (
        da2 * mag[1] - db2 * plus_y(ele, 0.0),
        da2 * mag[2] - db2 * plus_z(ele, 0.0),
    )
    u1 = [cb1 * v for v in p1]
    u2 = [cb2 * v for v in p2]
    before = (
        db1 * (q1[1] + plus_y(u1, u2[2])),
        db1 * (q1[2] + plus_z(u1, u2[1])),
    )
    adj = [q + c for q, c in zip(q2, plus(u2, 0.0, 0.0))]
    curl = minus([db2 * v for v in adj], *before)
    u2 = [cb2 * (ca2 * p - c) for p, c in zip(p2, curl)]
    adj2 = (da2 * adj[1] + plus_y(u2, 0.0), da2 * adj[2] + plus_z(u2, 0.0))
    pack(buffers[0], (mag[1], mag[2]) + mag2 + (cb2, adj[1], adj[2]) + adj2, NEXT_ROWS)

    e1, h1, p1, q1 = load(0)
    e2, _, p2, _ = load(1)
    ca1, cb1, da1, db1 = coefs(0)
    _, cb2, _, _ = coefs(1)
    mag = [da1 * h - db1 * c for h, c in zip(h1, plus(e1, e2[1], e2[2]))]
    curl = minus(mag, 0.0, 0.0)
    ele = (ca1 * e1[1] + cb1 * curl[1], ca1 * e1[2] + cb1 * curl[2])
    u1 = [cb1 * v for v in p1]
    adj = [db1 * (q + c) for q, c in zip(q1, plus(u1, cb2 * p2[1], cb2 * p2[2]))]
    curl = minus(adj, 0.0, 0.0)
    adj_ele = (ca1 * p1[1] - curl[1], ca1 * p1[2] - curl[2])
    pack(buffers[1], e1[1:] + ele + (cb1, u1[1], u1[2]) + adj_ele, PREV_ROWS)

    even = is_even("xy")
    to_next, to_prev = buffers[0][...], buffers[1][...]
    far[...] = jnp.where(even, to_prev, to_next)
    near[...] = jnp.where(even, to_next, to_prev)


def sweep(geometry, box, pml, *refs):
    fields, pattern, (rows_far, rows_near) = refs[:6], refs[6], refs[7:9]
    full_e, full_h, grad, edge, edge_e, edge_h = refs[9:15]
    tile, mag, adj_mag, ele, adj_ele, ca, cb, da, db = refs[15:24]
    by_e, by_r, sums, out_e, out_h, sems = refs[24:]
    rows_x, rows_z, cols = geometry[:3]
    grid = Grid(box, pml, *geometry)
    last = rows_x - 1
    own = pl.ds(0, rows_z)
    even = is_even("gz")

    def fill(group, carry):
        fill_tiles(tile, rows_far, rows_near, even, group, range(PERIOD))
        return carry

    lax.fori_loop(0, rows_x // PERIOD, fill, 0)

    def coefs(x, carry):
        sigma = grid.sigma(x)
        ca[x], cb[x], loss, inverse = grid.electric(
            x,
            full_plane(fields[4], tile, 12, x),
            full_plane(fields[5], tile, 13, x),
            pattern[pl.ds(x, 1), :],
            sigma,
        )
        da[x], db[x] = grid.magnetic(sigma)
        weight = (inverse * inverse * (grid.mask_zy * grid.mask_x(x)))[:rows_z]
        by_e[x] = 2.0 * loss[:rows_z] * weight
        by_r[x] = -TIME_STEP * weight
        return carry

    lax.fori_loop(0, rows_x, coefs, 0, unroll=UNROLL)
    zero = jnp.zeros(grid.shape, jnp.float32)
    cb[rows_x] = zero
    for k in (1, 2):
        ele[k, rows_x] = zero
        adj_ele[k, rows_x] = zero

    def first(x, carry):
        prev_h, prev_m = carry
        at_last = jnp.full(grid.shape, x) == last
        ahead = jnp.minimum(x + 1, last)
        e, h, p, q = [triple(fields, tile, g, x) for g in range(4)]
        a, b, c, d = ca[x], cb[x], da[x], db[x]
        e_y = jnp.where(at_last, 0.0, full_plane(fields[0], tile, 1, ahead))
        e_z = jnp.where(at_last, 0.0, full_plane(fields[0], tile, 2, ahead))
        new_h = [c * v - d * w for v, w in zip(h, plus(e, e_y, e_z))]
        curl = minus(new_h, *prev_h)
        b_ahead = cb[x + 1]
        u_y = b_ahead * full_plane(fields[2], tile, 7, ahead)
        u_z = b_ahead * full_plane(fields[2], tile, 8, ahead)
        new_m = [v + w for v, w in zip(q, plus([b * v for v in p], u_y, u_z))]
        scaled = [d * v for v in new_m]
        adj_curl = minus(scaled, *prev_m)
        dot_e, dot_r = 0.0, 0.0
        for k in range(3):
            mag[k, x] = new_h[k]
            adj_mag[k, x] = new_m[k]
            ele[k, x] = a * e[k] + b * curl[k]
            new_p = a * p[k] - adj_curl[k]
            adj_ele[k, x] = new_p
            dot_e = dot_e + new_p[:rows_z] * e[k][:rows_z]
            dot_r = dot_r + new_p[:rows_z] * curl[k][:rows_z]
        sums[x] = by_e[x] * dot_e + by_r[x] * dot_r
        return new_h[1:], scaled[1:]

    lax.fori_loop(0, rows_x, first, ([zero, zero], [zero, zero]), unroll=UNROLL)

    def out_copies(group):
        part = pl.ds(group * UNROLL, UNROLL)
        return [
            pltpu.make_async_copy(ref.at[:, part], full.at[:, part], sems.at[i, group])
            for i, (ref, full) in enumerate(((out_e, full_e), (out_h, full_h)))
        ]

    def second(x, carry):
        prev_h, prev_m = carry
        e = [ele[k, x] for k in range(3)]
        p1 = [adj_ele[k, x] for k in range(3)]
        a, b, c, d = ca[x], cb[x], da[x], db[x]
        new_h = [
            c * mag[k, x] - d * w for k, w in enumerate(plus(e, ele[1, x + 1], ele[2, x + 1]))
        ]
        curl = minus(new_h, *prev_h)
        b_ahead = cb[x + 1]
        u = [b * v for v in p1]
        ahead = plus(u, b_ahead * adj_ele[1, x + 1], b_ahead * adj_ele[2, x + 1])
        new_m = [c * adj_mag[k, x] + w for k, w in enumerate(ahead)]
        scaled = [d * v for v in new_m]
        adj_curl = minus(scaled, *prev_m)
        dot_e, dot_r = 0.0, 0.0
        for k in range(3):
            out_h[k, x] = c[:rows_z] * new_m[k][:rows_z]
            out_e[k, x] = a[:rows_z] * p1[k][:rows_z] - adj_curl[k][:rows_z]
            p = fields[2][k, x]
            dot_e = dot_e + p * e[k][:rows_z]
            dot_r = dot_r + p * curl[k][:rows_z]
        terms = sums[x] + by_e[x] * dot_e + by_r[x] * dot_r
        total = terms[0:8]
        for start in range(8, rows_z, 8):
            total = total + terms[start : start + 8]
        grad[pl.ds(x, 1), :] = jnp.sum(total, axis=0, keepdims=True)
        return new_h[1:], scaled[1:]

    def second_group(group, carry):
        for i in range(UNROLL):
            carry = second(group * UNROLL + i, carry)
        for copy in out_copies(group):
            copy.start()
        return carry

    groups = rows_x // UNROLL
    lax.fori_loop(0, groups, second_group, ([zero, zero], [zero, zero]))

    first_curl = minus([mag[k, 0] for k in range(3)], 0.0, 0.0)
    last_curl = minus([mag[k, last] for k in range(3)], mag[1, last - 1], mag[2, last - 1])
    for k in range(3):
        edge[k], edge[3 + k] = first_curl[k], last_curl[k]
    kept = [ele[1, 0], ele[2, 0]] + [adj_ele[k, 0] for k in range(3)]
    kept += [mag[1, last], mag[2, last], db[last] * adj_mag[1, last], db[last] * adj_mag[2, last]]
    kept += [adj_ele[k, last] for k in range(3)]
    kept += [ref[x] for x in (0, last) for ref in (ca, cb, da, db)] + [da[last - 1], db[last - 1]]
    kept += [full_plane(fields[0], tile, k, 0) for k in (1, 2)]
    kept += [cb[0] * full_plane(fields[2], tile, k, 0) for k in (7, 8)]
    for k, value in enumerate(kept):
        edge[6 + k] = value
    start = 6 + len(kept)
    for k, value in enumerate((by_e[0], by_r[0], by_r[1], by_r[last - 1], by_e[last], by_r[last])):
        edge[start + k, own, :] = value
    for i, x in enumerate((0, 1, last - 1, last)):
        for k in range(3):
            edge_e[k, i] = out_e[k, x]
            edge_h[k, i] = out_h[k, x]
    for group in range(groups):
        for copy in out_copies(group):
            copy.wait()


def response(geometry, box, pml, *refs):
    e_ref, p_ref, edge, local_e, local_h, local_grad, far, near = refs[:8]
    edge_e, edge_h, shares, buffers, tile, grad = refs[8:]
    rows_x, rows_z, cols = geometry[:3]
    last = rows_x - 1
    grid = Grid(box, pml, *geometry)
    even = is_even("xy")
    buffers[0] = jnp.where(even, far[...], near[...])
    buffers[1] = jnp.where(even, near[...], far[...])
    grad[...] = jnp.zeros(grad.shape, jnp.float32)
    grad[pl.ds(0, rows_x), :] = local_grad[...]
    for side, rows in enumerate((NEXT_ROWS, PREV_ROWS)):
        for k in range(PLANES):
            tile[side, k] = jnp.zeros(tile.shape[2:], jnp.float32)
        for i, (k, r) in enumerate(rows):
            row = buffers[side, pl.ds(PLANES * rows_z + i, 1), :]
            tile[side, k, pl.ds(r if r >= 0 else EXT + r, 1), :] = row

    def unpack(side):
        return [
            jnp.concatenate([buffers[side, pl.ds(k * rows_z, rows_z), :], tile[side, k]], axis=0)
            for k in range(PLANES)
        ]

    def own(v):
        return v[:rows_z]

    def weight(k):
        return edge[32 + k, pl.ds(0, rows_z), :]

    def add_rows(x, terms):
        total = terms[0:8]
        for start in range(8, rows_z, 8):
            total = total + terms[start : start + 8]
        grad[pl.ds(x, 1), :] += jnp.sum(total, axis=0, keepdims=True)

    def write(ref, local, i, change, scale=1.0):
        for k in range(3):
            ref[k, i] = local[k, i] if change[k] is None else local[k, i] + own(change[k])

    h_y, h_z, h2_y, h2_z, cb_b, m_y, m_z, m2_y, m2_z = unpack(0)
    at = jnp.full(grid.shape, grid.x_start)
    da_b, db_b = grid.magnetic(grid.sigma(-1), at > 0)
    ca_f, cb_f, da_f, db_f = (edge[18 + k] for k in range(4))
    e_y, e_z, u_y, u_z = (edge[28 + k] for k in range(4))
    dh_y, dh_z = db_b * e_z, -(db_b * e_y)
    h_y, h_z = h_y + dh_y, h_z + dh_z
    d_ele = (cb_f * h_z, -(cb_f * h_y))
    ele_y, ele_z = edge[6] + d_ele[0], edge[7] + d_ele[1]
    back = [cb_b * v for v in minus_yz(dh_y, dh_z)]
    h2_y = h2_y + da_b * dh_y - db_b * plus_y(back, ele_z)
    h2_z = h2_z + da_b * dh_z - db_b * plus_z(back, ele_y)
    dm_y, dm_z = -u_z, u_y
    n_y, n_z = db_b * (m_y + dm_y), db_b * (m_z + dm_z)
    d_p = (-n_z, n_y)
    p_y, p_z = edge[9] + d_p[0], edge[10] + d_p[1]
    back = [-(cb_b * v) for v in minus_yz(db_b * dm_y, db_b * dm_z)]
    m2_y = m2_y + da_b * dm_y + plus_y(back, cb_f * p_z)
    m2_z = m2_z + da_b * dm_z + plus_z(back, cb_f * p_y)
    d_h2 = [-(db_f * v) for v in plus_yz(*d_ele)]
    d_m2 = plus_yz(cb_f * d_p[0], cb_f * d_p[1])
    d_r2 = minus(d_h2, h2_y, h2_z)
    d_n2 = [db_f * v for v in d_m2]
    curl = minus(d_n2, db_b * m2_y, db_b * m2_z)
    write(edge_e, local_e, 0, (-curl[0], ca_f * d_p[0] - curl[1], ca_f * d_p[1] - curl[2]))
    write(edge_e, local_e, 1, (None, -d_n2[2], d_n2[1]))
    write(edge_h, local_h, 0, [da_f * v for v in d_m2])
    write(edge_h, local_h, 1, (None, None, None))
    p2 = [p_ref[k, 0] for k in range(3)]
    along_e = sum(
        own(d_p[k - 1]) * e_ref[k, 0] + p2[k] * own(d_ele[k - 1]) for k in (1, 2)
    )
    along_r = dot(p2, [own(v) for v in d_r2])
    along_r = along_r + own(d_p[0] * edge[1] + d_p[1] * edge[2] + p_y * h_z - p_z * h_y)
    add_rows(0, weight(0) * along_e + weight(1) * along_r)
    add_rows(1, weight(2) * (p_ref[1, 1] * own(d_h2[2]) - p_ref[2, 1] * own(d_h2[1])))

    e_y, e_z, e1_y, e1_z, cb_n, u_y, u_z, p_y, p_z = unpack(1)
    ca_l, cb_l, da_l, db_l = (edge[22 + k] for k in range(4))
    da_k, db_k = edge[26], edge[27]
    dh_y, dh_z = db_l * e_z, -(db_l * e_y)
    dm_y, dm_z = -u_z, u_y
    dn_y, dn_z = db_l * dm_y, db_l * dm_z
    d_r1 = minus_yz(dh_y, dh_z)
    d_ele = [cb_l * v for v in d_r1]
    d_p = [-v for v in minus_yz(dn_y, dn_z)]
    e1_y = e1_y + cb_n * (edge[12] + dh_z)
    e1_z = e1_z - cb_n * (edge[11] + dh_y)
    p_y = p_y - (edge[14] + dn_z)
    p_z = p_z + (edge[13] + dn_y)
    d_h2 = [-(db_l * v) for v in plus(d_ele, e1_y, e1_z)]
    d_h2 = [d_h2[0], d_h2[1] + da_l * dh_y, d_h2[2] + da_l * dh_z]
    d_u = [cb_l * v for v in d_p]
    d_m2 = plus(d_u, cb_n * p_y, cb_n * p_z)
    d_m2 = [d_m2[0], d_m2[1] + da_l * dm_y, d_m2[2] + da_l * dm_z]
    k_h2 = (db_k * d_ele[2], -(db_k * d_ele[1]))
    k_m2 = (-d_u[2], d_u[1])
    k_n2 = (db_k * k_m2[0], db_k * k_m2[1])
    k_r2 = minus_yz(*k_h2)
    d_r2 = minus(d_h2, *k_h2)
    write(edge_e, local_e, 2, [-v for v in minus_yz(*k_n2)])
    curl = minus([db_l * v for v in d_m2], *k_n2)
    write(edge_e, local_e, 3, [ca_l * v - c for v, c in zip(d_p, curl)])
    write(edge_h, local_h, 2, (None, da_k * k_m2[0], da_k * k_m2[1]))
    write(edge_h, local_h, 3, [da_l * v for v in d_m2])
    p2 = [p_ref[k, last] for k in range(3)]
    along_e = dot([own(v) for v in d_p], [e_ref[k, last] for k in range(3)])
    along_e = along_e + dot(p2, [own(v) for v in d_ele])
    along_r = dot(p2, [own(v) for v in d_r2])
    for k in range(3):
        new_p = own(edge[15 + k] + d_p[k])
        along_r = along_r + own(d_p[k] * edge[3 + k]) + new_p * own(d_r1[k])
    add_rows(last, weight(4) * along_e + weight(5) * along_r)
    p2 = [p_ref[k, last - 1] for k in range(3)]
    add_rows(last - 1, weight(3) * dot(p2, [own(v) for v in k_r2]))

    shares[...] = jnp.transpose(grad[...])


def finish(parts, edge_e, edge_h, in_e, in_h, out_e, out_h, out, sems):
    last = out_e.shape[1] - 2
    copies = []
    for i, (edge, full) in enumerate(((edge_e, out_e), (edge_h, out_h))):
        for side, start in enumerate((0, last)):
            copy = pltpu.make_async_copy(
                edge.at[:, pl.ds(2 * side, 2)], full.at[:, pl.ds(start, 2)], sems.at[2 * i + side]
            )
            copy.start()
            copies.append(copy)
    share, rows_x = out.shape
    total = parts[pl.ds(0, share), :]
    for j in range(1, parts.shape[0] // share):
        total = total + parts[pl.ds(j * share, share), :]
    out[...] = total[:, :rows_x]
    for copy in copies:
        copy.wait()


def shards(
    e_check, h_check, adj_e_end, adj_h_end, background, conductivity, pattern, design_box, pml_width
):
    rows_x, rows_z, cols = background.shape
    size_x, size_z = lax.axis_size("xy"), lax.axis_size("gz")
    geometry = (rows_x, rows_z, cols, rows_x * size_x, rows_z * size_z)
    fields = (e_check, h_check, adj_e_end, adj_h_end, background, conductivity)
    f32 = jnp.float32
    params = pltpu.CompilerParams(vmem_limit_bytes=VMEM_LIMIT)

    def array(*shape):
        return jax.ShapeDtypeStruct(shape, f32)

    message = pltpu.VMEM((rows_x * ROWS, cols), f32)
    inputs = fields + (pattern, design_box, pml_width)
    *inputs, design_box, pml_width, rows_far, rows_near = pl.pallas_call(
        load_fields,
        out_shape=tuple(pltpu.VMEM(ref.shape, ref.dtype) for ref in inputs) + (message,) * 2,
        in_specs=[HBM] * 9,
        out_specs=[VMEM] * 11,
        scratch_shapes=[message] * 2 + [pltpu.SemaphoreType.DMA((9,))],
        compiler_params=pltpu.CompilerParams(vmem_limit_bytes=8 * 1024 * 1024),
        name="load_fields",
    )(*(pltpu.with_memory_space_constraint(ref, pltpu.HBM) for ref in inputs))
    rows_far, rows_near = swap_both(rows_far, rows_near, "gz")

    def planes(*lead):
        return pltpu.VMEM(lead + (rows_z + EXT, cols), f32)

    size = PLANES * rows_z + SINGLE_ROWS
    message = pltpu.VMEM((size, cols), f32)
    tile = pltpu.VMEM((SLOTS, rows_x, EXT, cols), f32)
    far, near = pl.pallas_call(
        functools.partial(edge_planes, geometry),
        out_shape=(array(size, cols),) * 2,
        in_specs=[SMEM] * 2 + [VMEM] * 9,
        out_specs=[VMEM] * 2,
        scratch_shapes=[tile, message, message, planes(PLANES)],
        compiler_params=params,
        name="edge_planes",
    )(design_box, pml_width, *inputs, rows_far, rows_near)
    far, near = swap_both(far, near, "xy")

    count = rows_x + 1
    local_e, local_h, local_grad, edge, edge_e, edge_h = pl.pallas_call(
        functools.partial(sweep, geometry),
        out_shape=(
            array(*e_check.shape),
            array(*e_check.shape),
            array(rows_x, cols),
            array(EDGE_PLANES, rows_z + EXT, cols),
            array(3, 4, rows_z, cols),
            array(3, 4, rows_z, cols),
        ),
        in_specs=[SMEM] * 2 + [VMEM] * 9,
        out_specs=[HBM] * 2 + [VMEM] * 4,
        scratch_shapes=[tile]
        + [planes(3, count)] * 4
        + [planes(count)] * 4
        + [pltpu.VMEM((rows_x, rows_z, cols), f32)] * 3
        + [pltpu.VMEM((3, rows_x, rows_z, cols), f32)] * 2
        + [pltpu.SemaphoreType.DMA((2, rows_x // UNROLL))],
        compiler_params=params,
        cost_estimate=pl.CostEstimate(flops=50000000, bytes_accessed=8000000, transcendentals=0),
        name="sweep",
    )(design_box, pml_width, *inputs, rows_far, rows_near)

    edge_e, edge_h, shares = pl.pallas_call(
        functools.partial(response, geometry),
        out_shape=(array(*edge_e.shape), array(*edge_h.shape), array(cols, cols)),
        in_specs=[SMEM] * 2 + [VMEM] * 8,
        out_specs=[VMEM] * 3,
        scratch_shapes=[
            pltpu.VMEM((2, size, cols), f32),
            pltpu.VMEM((2, PLANES, EXT, cols), f32),
            pltpu.VMEM((cols, cols), f32),
        ],
        compiler_params=params,
        name="response",
    )(design_box, pml_width, inputs[0], inputs[2], edge, edge_e, edge_h, local_grad, far, near)

    parts = lax.all_to_all(shares, "gz", split_axis=0, concat_axis=0, tiled=True)
    back_e, back_h, pattern_grad = pl.pallas_call(
        finish,
        out_shape=(array(*e_check.shape), array(*e_check.shape), array(cols // size_z, rows_x)),
        in_specs=[VMEM] * 3 + [HBM] * 2,
        out_specs=[HBM] * 2 + [VMEM],
        scratch_shapes=[pltpu.SemaphoreType.DMA((4,))],
        input_output_aliases={3: 0, 4: 1},
        compiler_params=pltpu.CompilerParams(vmem_limit_bytes=8 * 1024 * 1024),
        name="finish",
    )(parts, edge_e, edge_h, local_e, local_h)
    return (back_e, back_h, pattern_grad.T)


def solution(mesh):
    field = P(None, "xy", "gz", None)
    cell = P("xy", "gz", None)
    return jax.shard_map(
        shards,
        mesh=mesh,
        in_specs=(field, field, field, field, cell, cell, P("xy", None), P(), P()),
        out_specs=(field, field, P("xy", "gz")),
        check_vma=False,
    )
```

```python
import functools

import jax
import jax.numpy as jnp
from jax import lax
from jax.experimental import pallas as pl
from jax.experimental.pallas import tpu as pltpu
from jax.sharding import PartitionSpec as P

TIME_STEP = 0.5
SIGMA_PEAK = 1.0
HALF = TIME_STEP / 2
EXT = 8
UNROLL = 4
VMEM_LIMIT = 32 * 1024 * 1024

FIRST_ROWS = (2, 2, 1, 1, 1, 1, 2, 2, 1, 1, 1, 1, 2, 2)
LAST_ROWS = (2, 2, 2, 2, 2, 1, 2, 2, 2, 2, 2, 1, 2, 2)
FIRST_AT = tuple(sum(FIRST_ROWS[:k]) for k in range(14))
LAST_AT = tuple(sum(LAST_ROWS[:k]) for k in range(14))
ROWS = max(sum(FIRST_ROWS), sum(LAST_ROWS))
PERIOD = 4
SLOTS = 14
PLANES = 9
NEXT_ROWS = tuple((k, r) for k in (0, 1, 5, 6) for r in (0, -1)) + ((4, 0),)
PREV_ROWS = tuple(
    (k, r) for k, rs in ((0, (0, -1)), (1, (0, -2, -1)), (5, (0, -1)), (6, (0, -2, -1)))
    for r in rs
) + ((3, -1), (8, -1), (4, -1))
SINGLE_ROWS = 16
EDGE_PLANES = 38

HBM = pl.BlockSpec(memory_space=pltpu.HBM)
VMEM = pl.BlockSpec(memory_space=pltpu.VMEM)
SMEM = pl.BlockSpec(memory_space=pltpu.SMEM)


def swapped(shard, axis, first):
    size = lax.axis_size(axis)
    pairs = [(i, j) for k in range(first, size - 1, 2) for i, j in ((k, k + 1), (k + 1, k))]
    return lax.ppermute(shard, axis, pairs)


def swap_both(far, near, axis):
    far, near = swapped(far, axis, 1), swapped(near, axis, 0)
    return far, near


def is_even(axis):
    return lax.rem(lax.axis_index(axis), 2) == 0


def rows_of(ref, group):
    return ref.at[pl.ds(pl.multiple_of(group * (PERIOD * ROWS), 8), PERIOD * ROWS)]


def load_fields(*refs):
    sources, copies_of, (far, near) = refs[:9], refs[9:18], refs[18:20]
    first, last, sems = refs[20:]
    rows_x, rows_z = sources[4].shape[:2]
    copies = []
    for i, (source, target) in enumerate(zip(sources, copies_of)):
        copy = pltpu.make_async_copy(source, target, sems.at[i])
        copy.start()
        copies.append(copy)

    for i in range(6):
        copies[i].wait()
        field = copies_of[i]

        def pack(group, carry):
            first_rows, last_rows = rows_of(first, group), rows_of(last, group)
            for n in range(PERIOD):
                x = group * PERIOD + n
                for k in range(3 * i, 3 * i + 3) if i < 4 else (8 + i,):
                    at = (k % 3, x) if i < 4 else (x,)
                    count, start = FIRST_ROWS[k], n * ROWS + FIRST_AT[k]
                    rows = field[(*at, slice(0, count), slice(None))]
                    first_rows[start : start + count, :] = rows
                    count, start = LAST_ROWS[k], n * ROWS + LAST_AT[k]
                    rows = field[(*at, slice(rows_z - count, rows_z), slice(None))]
                    last_rows[start : start + count, :] = rows
            return carry

        lax.fori_loop(0, rows_x // PERIOD, pack, 0)
    for copy in copies[6:]:
        copy.wait()
    even = is_even("gz")
    far[...] = jnp.where(even, first[...], last[...])
    near[...] = jnp.where(even, last[...], first[...])


def lane_index(shape):
    return lax.broadcasted_iota(jnp.int32, shape, 1)


def y_ahead(v):
    cols = v.shape[1]
    moved = pltpu.roll(v, cols - 1, 1)
    return jnp.where(lane_index(v.shape) == cols - 1, 0.0, moved) - v


def y_behind(v):
    moved = pltpu.roll(v, 1, 1)
    return v - jnp.where(lane_index(v.shape) == 0, 0.0, moved)


def z_ahead(v):
    return pltpu.roll(v, v.shape[0] - 1, 0) - v


def z_behind(v):
    return v - pltpu.roll(v, 1, 0)


def plus_x(v):
    return y_ahead(v[2]) - z_ahead(v[1])


def plus_y(v, next_z):
    return z_ahead(v[0]) - (next_z - v[2])


def plus_z(v, next_y):
    return (next_y - v[1]) - y_ahead(v[0])


def plus(v, next_y, next_z):
    return plus_x(v), plus_y(v, next_z), plus_z(v, next_y)


def minus(v, prev_y, prev_z):
    return (
        y_behind(v[2]) - z_behind(v[1]),
        z_behind(v[0]) - (v[2] - prev_z),
        (v[1] - prev_y) - y_behind(v[0]),
    )


def plus_yz(v_y, v_z):
    return y_ahead(v_z) - z_ahead(v_y), v_z, -v_y


def minus_yz(v_y, v_z):
    return y_behind(v_z) - z_behind(v_y), -v_z, v_y


def dot(left, right):
    return sum(a * b for a, b in zip(left, right))


def depth_cube(place, total, layer):
    depth = jnp.maximum(jnp.maximum(layer - place, place - (total - 1 - layer)), 0.0) / layer
    return depth * depth * depth


class Grid:
    def __init__(self, box, pml, rows_x, rows_z, cols, total_x, total_z):
        rows = rows_z + EXT
        self.shape = (rows, cols)
        self.box = box
        self.width_x = pml[0].astype(jnp.float32)
        self.total_x = total_x
        self.x_start = lax.axis_index("xy") * rows_x
        self.rows_z = rows_z
        row = lax.broadcasted_iota(jnp.int32, self.shape, 0)
        z = lax.axis_index("gz") * rows_z + jnp.where(row < rows_z + EXT // 2, row, row - rows)
        y = lane_index(self.shape)
        self.inside = (z >= 0) & (z < total_z)
        self.sigma_zy = depth_cube(
            z.astype(jnp.float32), total_z, pml[2].astype(jnp.float32)
        ) + depth_cube(y.astype(jnp.float32), cols, pml[1].astype(jnp.float32))
        picked = (z >= box[4]) & (z < box[5]) & (y >= box[2]) & (y < box[3])
        self.mask_zy = jnp.where(picked, 1.0, 0.0)

    def sigma(self, x):
        place = jnp.full((1, self.shape[1]), (self.x_start + x).astype(jnp.float32))
        return SIGMA_PEAK * (self.sigma_zy + depth_cube(place, self.total_x, self.width_x))

    def mask_x(self, x):
        at = self.x_start + x
        return jnp.where((at >= self.box[0]) & (at < self.box[1]), 1.0, 0.0)

    def magnetic(self, sigma, x_inside=None):
        inside = self.inside if x_inside is None else self.inside & x_inside
        inverse = 1.0 / (1.0 + HALF * sigma)
        return (
            jnp.where(inside, 2.0 * inverse - 1.0, 0.0),
            jnp.where(inside, TIME_STEP * inverse, 0.0),
        )

    def electric(self, x, background, conductivity, pattern_row, sigma):
        permittivity = background + self.mask_zy * (pattern_row * self.mask_x(x))
        loss = HALF * (conductivity + sigma)
        inverse = jnp.where(self.inside, 1.0 / (permittivity + loss), 0.0)
        return (permittivity - loss) * inverse, TIME_STEP * inverse, loss, inverse


def full_plane(ref, tile_ref, k, x):
    own = ref[k % 3, x] if k < 12 else ref[x]
    return jnp.concatenate([own, tile_ref[k, x]], axis=0)


def fill_tiles(tile_ref, far, near, even, group, planes):
    far, near = rows_of(far, group), rows_of(near, group)
    for n in planes:
        x = group * PERIOD + n
        for k in range(SLOTS):
            tile_ref[k, x] = jnp.zeros(tile_ref.shape[2:], jnp.float32)
            for count, at, start in (
                (FIRST_ROWS[k], FIRST_AT[k], 0),
                (LAST_ROWS[k], LAST_AT[k], EXT - LAST_ROWS[k]),
            ):
                rows = pl.ds(n * ROWS + at, count)
                own, other = (near, far) if start == 0 else (far, near)
                tile_ref[k, x, pl.ds(start, count), :] = jnp.where(even, own[rows, :], other[rows, :])


def triple(fields, tile_ref, group, x):
    return tuple(full_plane(fields[group], tile_ref, 3 * group + c, x) for c in range(3))


def edge_planes(geometry, box, pml, *refs):
    fields, pattern, (rows_far, rows_near) = refs[:6], refs[6], refs[7:9]
    far, near, tile, buffers, planes = refs[9], refs[10], refs[11], refs[12:14], refs[14]
    rows_x, rows_z = geometry[:2]
    grid = Grid(box, pml, *geometry)
    even = is_even("gz")
    fill_tiles(tile, rows_far, rows_near, even, 0, (0, 1))
    fill_tiles(tile, rows_far, rows_near, even, rows_x // PERIOD - 1, (PERIOD - 2, PERIOD - 1))

    def coefs(x):
        sigma = grid.sigma(x)
        coef_a, coef_b, _, _ = grid.electric(
            x,
            full_plane(fields[4], tile, 12, x),
            full_plane(fields[5], tile, 13, x),
            pattern[pl.ds(x, 1), :],
            sigma,
        )
        return (coef_a, coef_b) + grid.magnetic(sigma)

    def load(x):
        return [triple(fields, tile, g, x) for g in range(4)]

    def pack(buffer, values, rows):
        for k, value in enumerate(values):
            buffer[pl.ds(k * rows_z, rows_z), :] = value[:rows_z]
            planes[k] = value
        start = PLANES * rows_z
        buffer[pl.ds(start, SINGLE_ROWS), :] = jnp.zeros((SINGLE_ROWS, value.shape[1]), jnp.float32)
        for i, (k, r) in enumerate(rows):
            at = rows_z + r if r >= 0 else rows_z + EXT + r
            buffer[pl.ds(start + i, 1), :] = planes[k, pl.ds(at, 1), :]

    one, two = rows_x - 2, rows_x - 1
    e1, h1, p1, q1 = load(one)
    e2, h2, p2, q2 = load(two)
    _, cb1, da1, db1 = coefs(one)
    ca2, cb2, da2, db2 = coefs(two)
    before = (
        da1 * h1[1] - db1 * plus_y(e1, e2[2]),
        da1 * h1[2] - db1 * plus_z(e1, e2[1]),
    )
    mag = [da2 * h - db2 * c for h, c in zip(h2, plus(e2, 0.0, 0.0))]
    ele = [ca2 * e + cb2 * c for e, c in zip(e2, minus(mag, *before))]
    mag2 = (
        da2 * mag[1] - db2 * plus_y(ele, 0.0),
        da2 * mag[2] - db2 * plus_z(ele, 0.0),
    )
    u1 = [cb1 * v for v in p1]
    u2 = [cb2 * v for v in p2]
    before = (
        db1 * (q1[1] + plus_y(u1, u2[2])),
        db1 * (q1[2] + plus_z(u1, u2[1])),
    )
    adj = [q + c for q, c in zip(q2, plus(u2, 0.0, 0.0))]
    curl = minus([db2 * v for v in adj], *before)
    u2 = [cb2 * (ca2 * p - c) for p, c in zip(p2, curl)]
    adj2 = (da2 * adj[1] + plus_y(u2, 0.0), da2 * adj[2] + plus_z(u2, 0.0))
    pack(buffers[0], (mag[1], mag[2]) + mag2 + (cb2, adj[1], adj[2]) + adj2, NEXT_ROWS)

    e1, h1, p1, q1 = load(0)
    e2, _, p2, _ = load(1)
    ca1, cb1, da1, db1 = coefs(0)
    _, cb2, _, _ = coefs(1)
    mag = [da1 * h - db1 * c for h, c in zip(h1, plus(e1, e2[1], e2[2]))]
    curl = minus(mag, 0.0, 0.0)
    ele = (ca1 * e1[1] + cb1 * curl[1], ca1 * e1[2] + cb1 * curl[2])
    u1 = [cb1 * v for v in p1]
    adj = [db1 * (q + c) for q, c in zip(q1, plus(u1, cb2 * p2[1], cb2 * p2[2]))]
    curl = minus(adj, 0.0, 0.0)
    adj_ele = (ca1 * p1[1] - curl[1], ca1 * p1[2] - curl[2])
    pack(buffers[1], e1[1:] + ele + (cb1, u1[1], u1[2]) + adj_ele, PREV_ROWS)

    even = is_even("xy")
    to_next, to_prev = buffers[0][...], buffers[1][...]
    size = to_next.shape[0]
    far[...] = jnp.where(even, to_prev, to_next)
    near[pl.ds(0, size), :] = jnp.where(even, to_next, to_prev)
    near[pl.ds(size, 8), :] = jnp.zeros((8, to_next.shape[1]), jnp.float32)


def sweep(geometry, box, pml, *refs):
    fields, pattern, (rows_far, rows_near) = refs[:6], refs[6], refs[7:9]
    full_e, full_h, grad, edge, edge_e, edge_h = refs[9:15]
    tile, mag, adj_mag, ele, adj_ele, ca, cb, da, db = refs[15:24]
    by_e, by_r, sums, out_e, out_h, sems = refs[24:]
    rows_x, rows_z, cols = geometry[:3]
    grid = Grid(box, pml, *geometry)
    last = rows_x - 1
    own = pl.ds(0, rows_z)
    even = is_even("gz")

    def fill(group, carry):
        fill_tiles(tile, rows_far, rows_near, even, group, range(PERIOD))
        return carry

    lax.fori_loop(0, rows_x // PERIOD, fill, 0)

    def coefs(x, carry):
        sigma = grid.sigma(x)
        ca[x], cb[x], loss, inverse = grid.electric(
            x,
            full_plane(fields[4], tile, 12, x),
            full_plane(fields[5], tile, 13, x),
            pattern[pl.ds(x, 1), :],
            sigma,
        )
        da[x], db[x] = grid.magnetic(sigma)
        weight = (inverse * inverse * (grid.mask_zy * grid.mask_x(x)))[:rows_z]
        by_e[x] = 2.0 * loss[:rows_z] * weight
        by_r[x] = -TIME_STEP * weight
        return carry

    lax.fori_loop(0, rows_x, coefs, 0, unroll=UNROLL)
    zero = jnp.zeros(grid.shape, jnp.float32)
    cb[rows_x] = zero
    for k in (1, 2):
        ele[k, rows_x] = zero
        adj_ele[k, rows_x] = zero

    def first(x, carry):
        prev_h, prev_m = carry
        at_last = jnp.full(grid.shape, x) == last
        ahead = jnp.minimum(x + 1, last)
        e, h, p, q = [triple(fields, tile, g, x) for g in range(4)]
        a, b, c, d = ca[x], cb[x], da[x], db[x]
        e_y = jnp.where(at_last, 0.0, full_plane(fields[0], tile, 1, ahead))
        e_z = jnp.where(at_last, 0.0, full_plane(fields[0], tile, 2, ahead))
        new_h = [c * v - d * w for v, w in zip(h, plus(e, e_y, e_z))]
        curl = minus(new_h, *prev_h)
        b_ahead = cb[x + 1]
        u_y = b_ahead * full_plane(fields[2], tile, 7, ahead)
        u_z = b_ahead * full_plane(fields[2], tile, 8, ahead)
        new_m = [v + w for v, w in zip(q, plus([b * v for v in p], u_y, u_z))]
        scaled = [d * v for v in new_m]
        adj_curl = minus(scaled, *prev_m)
        dot_e, dot_r = 0.0, 0.0
        for k in range(3):
            mag[k, x] = new_h[k]
            adj_mag[k, x] = new_m[k]
            ele[k, x] = a * e[k] + b * curl[k]
            new_p = a * p[k] - adj_curl[k]
            adj_ele[k, x] = new_p
            dot_e = dot_e + new_p[:rows_z] * e[k][:rows_z]
            dot_r = dot_r + new_p[:rows_z] * curl[k][:rows_z]
        sums[x] = by_e[x] * dot_e + by_r[x] * dot_r
        return new_h[1:], scaled[1:]

    lax.fori_loop(0, rows_x, first, ([zero, zero], [zero, zero]), unroll=UNROLL)

    def out_copies(group):
        part = pl.ds(group * UNROLL, UNROLL)
        return [
            pltpu.make_async_copy(ref.at[:, part], full.at[:, part], sems.at[i, group])
            for i, (ref, full) in enumerate(((out_e, full_e), (out_h, full_h)))
        ]

    def second(x, carry):
        prev_h, prev_m = carry
        e = [ele[k, x] for k in range(3)]
        p1 = [adj_ele[k, x] for k in range(3)]
        a, b, c, d = ca[x], cb[x], da[x], db[x]
        new_h = [
            c * mag[k, x] - d * w for k, w in enumerate(plus(e, ele[1, x + 1], ele[2, x + 1]))
        ]
        curl = minus(new_h, *prev_h)
        b_ahead = cb[x + 1]
        u = [b * v for v in p1]
        ahead = plus(u, b_ahead * adj_ele[1, x + 1], b_ahead * adj_ele[2, x + 1])
        new_m = [c * adj_mag[k, x] + w for k, w in enumerate(ahead)]
        scaled = [d * v for v in new_m]
        adj_curl = minus(scaled, *prev_m)
        dot_e, dot_r = 0.0, 0.0
        for k in range(3):
            out_h[k, x] = c[:rows_z] * new_m[k][:rows_z]
            out_e[k, x] = a[:rows_z] * p1[k][:rows_z] - adj_curl[k][:rows_z]
            p = fields[2][k, x]
            dot_e = dot_e + p * e[k][:rows_z]
            dot_r = dot_r + p * curl[k][:rows_z]
        terms = sums[x] + by_e[x] * dot_e + by_r[x] * dot_r
        total = terms[0:8]
        for start in range(8, rows_z, 8):
            total = total + terms[start : start + 8]
        grad[pl.ds(x, 1), :] = jnp.sum(total, axis=0, keepdims=True)
        return new_h[1:], scaled[1:]

    def second_group(group, carry):
        for i in range(UNROLL):
            carry = second(group * UNROLL + i, carry)
        for copy in out_copies(group):
            copy.start()
        return carry

    groups = rows_x // UNROLL
    lax.fori_loop(0, groups, second_group, ([zero, zero], [zero, zero]))

    first_curl = minus([mag[k, 0] for k in range(3)], 0.0, 0.0)
    last_curl = minus([mag[k, last] for k in range(3)], mag[1, last - 1], mag[2, last - 1])
    for k in range(3):
        edge[k], edge[3 + k] = first_curl[k], last_curl[k]
    kept = [ele[1, 0], ele[2, 0]] + [adj_ele[k, 0] for k in range(3)]
    kept += [mag[1, last], mag[2, last], db[last] * adj_mag[1, last], db[last] * adj_mag[2, last]]
    kept += [adj_ele[k, last] for k in range(3)]
    kept += [ref[x] for x in (0, last) for ref in (ca, cb, da, db)] + [da[last - 1], db[last - 1]]
    kept += [full_plane(fields[0], tile, k, 0) for k in (1, 2)]
    kept += [cb[0] * full_plane(fields[2], tile, k, 0) for k in (7, 8)]
    for k, value in enumerate(kept):
        edge[6 + k] = value
    start = 6 + len(kept)
    for k, value in enumerate((by_e[0], by_r[0], by_r[1], by_r[last - 1], by_e[last], by_r[last])):
        edge[start + k, own, :] = value
    for i, x in enumerate((0, 1, last - 1, last)):
        for k in range(3):
            edge_e[k, i] = out_e[k, x]
            edge_h[k, i] = out_h[k, x]
    for group in range(groups):
        for copy in out_copies(group):
            copy.wait()


def response(geometry, box, pml, *refs):
    e_ref, p_ref, edge, local_e, local_h, local_grad, far, near = refs[:8]
    edge_e, edge_h, shares, buffers, tile, grad = refs[8:]
    rows_x, rows_z, cols = geometry[:3]
    last = rows_x - 1
    grid = Grid(box, pml, *geometry)
    even = is_even("xy")
    close = near[pl.ds(0, far.shape[0]), :]
    buffers[0] = jnp.where(even, far[...], close)
    buffers[1] = jnp.where(even, close, far[...])
    grad[...] = jnp.zeros(grad.shape, jnp.float32)
    grad[pl.ds(0, rows_x), :] = local_grad[...]
    for side, rows in enumerate((NEXT_ROWS, PREV_ROWS)):
        for k in range(PLANES):
            tile[side, k] = jnp.zeros(tile.shape[2:], jnp.float32)
        for i, (k, r) in enumerate(rows):
            row = buffers[side, pl.ds(PLANES * rows_z + i, 1), :]
            tile[side, k, pl.ds(r if r >= 0 else EXT + r, 1), :] = row

    def unpack(side):
        return [
            jnp.concatenate([buffers[side, pl.ds(k * rows_z, rows_z), :], tile[side, k]], axis=0)
            for k in range(PLANES)
        ]

    def own(v):
        return v[:rows_z]

    def weight(k):
        return edge[32 + k, pl.ds(0, rows_z), :]

    def add_rows(x, terms):
        total = terms[0:8]
        for start in range(8, rows_z, 8):
            total = total + terms[start : start + 8]
        grad[pl.ds(x, 1), :] += jnp.sum(total, axis=0, keepdims=True)

    def write(ref, local, i, change, scale=1.0):
        for k in range(3):
            ref[k, i] = local[k, i] if change[k] is None else local[k, i] + own(change[k])

    h_y, h_z, h2_y, h2_z, cb_b, m_y, m_z, m2_y, m2_z = unpack(0)
    at = jnp.full(grid.shape, grid.x_start)
    da_b, db_b = grid.magnetic(grid.sigma(-1), at > 0)
    ca_f, cb_f, da_f, db_f = (edge[18 + k] for k in range(4))
    e_y, e_z, u_y, u_z = (edge[28 + k] for k in range(4))
    dh_y, dh_z = db_b * e_z, -(db_b * e_y)
    h_y, h_z = h_y + dh_y, h_z + dh_z
    d_ele = (cb_f * h_z, -(cb_f * h_y))
    ele_y, ele_z = edge[6] + d_ele[0], edge[7] + d_ele[1]
    back = [cb_b * v for v in minus_yz(dh_y, dh_z)]
    h2_y = h2_y + da_b * dh_y - db_b * plus_y(back, ele_z)
    h2_z = h2_z + da_b * dh_z - db_b * plus_z(back, ele_y)
    dm_y, dm_z = -u_z, u_y
    n_y, n_z = db_b * (m_y + dm_y), db_b * (m_z + dm_z)
    d_p = (-n_z, n_y)
    p_y, p_z = edge[9] + d_p[0], edge[10] + d_p[1]
    back = [-(cb_b * v) for v in minus_yz(db_b * dm_y, db_b * dm_z)]
    m2_y = m2_y + da_b * dm_y + plus_y(back, cb_f * p_z)
    m2_z = m2_z + da_b * dm_z + plus_z(back, cb_f * p_y)
    d_h2 = [-(db_f * v) for v in plus_yz(*d_ele)]
    d_m2 = plus_yz(cb_f * d_p[0], cb_f * d_p[1])
    d_r2 = minus(d_h2, h2_y, h2_z)
    d_n2 = [db_f * v for v in d_m2]
    curl = minus(d_n2, db_b * m2_y, db_b * m2_z)
    write(edge_e, local_e, 0, (-curl[0], ca_f * d_p[0] - curl[1], ca_f * d_p[1] - curl[2]))
    write(edge_e, local_e, 1, (None, -d_n2[2], d_n2[1]))
    write(edge_h, local_h, 0, [da_f * v for v in d_m2])
    write(edge_h, local_h, 1, (None, None, None))
    p2 = [p_ref[k, 0] for k in range(3)]
    along_e = sum(
        own(d_p[k - 1]) * e_ref[k, 0] + p2[k] * own(d_ele[k - 1]) for k in (1, 2)
    )
    along_r = dot(p2, [own(v) for v in d_r2])
    along_r = along_r + own(d_p[0] * edge[1] + d_p[1] * edge[2] + p_y * h_z - p_z * h_y)
    add_rows(0, weight(0) * along_e + weight(1) * along_r)
    add_rows(1, weight(2) * (p_ref[1, 1] * own(d_h2[2]) - p_ref[2, 1] * own(d_h2[1])))

    e_y, e_z, e1_y, e1_z, cb_n, u_y, u_z, p_y, p_z = unpack(1)
    ca_l, cb_l, da_l, db_l = (edge[22 + k] for k in range(4))
    da_k, db_k = edge[26], edge[27]
    dh_y, dh_z = db_l * e_z, -(db_l * e_y)
    dm_y, dm_z = -u_z, u_y
    dn_y, dn_z = db_l * dm_y, db_l * dm_z
    d_r1 = minus_yz(dh_y, dh_z)
    d_ele = [cb_l * v for v in d_r1]
    d_p = [-v for v in minus_yz(dn_y, dn_z)]
    e1_y = e1_y + cb_n * (edge[12] + dh_z)
    e1_z = e1_z - cb_n * (edge[11] + dh_y)
    p_y = p_y - (edge[14] + dn_z)
    p_z = p_z + (edge[13] + dn_y)
    d_h2 = [-(db_l * v) for v in plus(d_ele, e1_y, e1_z)]
    d_h2 = [d_h2[0], d_h2[1] + da_l * dh_y, d_h2[2] + da_l * dh_z]
    d_u = [cb_l * v for v in d_p]
    d_m2 = plus(d_u, cb_n * p_y, cb_n * p_z)
    d_m2 = [d_m2[0], d_m2[1] + da_l * dm_y, d_m2[2] + da_l * dm_z]
    k_h2 = (db_k * d_ele[2], -(db_k * d_ele[1]))
    k_m2 = (-d_u[2], d_u[1])
    k_n2 = (db_k * k_m2[0], db_k * k_m2[1])
    k_r2 = minus_yz(*k_h2)
    d_r2 = minus(d_h2, *k_h2)
    write(edge_e, local_e, 2, [-v for v in minus_yz(*k_n2)])
    curl = minus([db_l * v for v in d_m2], *k_n2)
    write(edge_e, local_e, 3, [ca_l * v - c for v, c in zip(d_p, curl)])
    write(edge_h, local_h, 2, (None, da_k * k_m2[0], da_k * k_m2[1]))
    write(edge_h, local_h, 3, [da_l * v for v in d_m2])
    p2 = [p_ref[k, last] for k in range(3)]
    along_e = dot([own(v) for v in d_p], [e_ref[k, last] for k in range(3)])
    along_e = along_e + dot(p2, [own(v) for v in d_ele])
    along_r = dot(p2, [own(v) for v in d_r2])
    for k in range(3):
        new_p = own(edge[15 + k] + d_p[k])
        along_r = along_r + own(d_p[k] * edge[3 + k]) + new_p * own(d_r1[k])
    add_rows(last, weight(4) * along_e + weight(5) * along_r)
    p2 = [p_ref[k, last - 1] for k in range(3)]
    add_rows(last - 1, weight(3) * dot(p2, [own(v) for v in k_r2]))

    shares[...] = jnp.transpose(grad[...])


def finish(parts, edge_e, edge_h, in_e, in_h, out_e, out_h, out, total, sems):
    share, rows_x = out.shape
    last = out_e.shape[1] - 2
    copies = []
    for i, (edge, full) in enumerate(((edge_e, out_e), (edge_h, out_h))):
        for side, start in enumerate((0, last)):
            copy = pltpu.make_async_copy(
                edge.at[:, pl.ds(2 * side, 2)], full.at[:, pl.ds(start, 2)], sems.at[2 * i + side]
            )
            copy.start()
            copies.append(copy)
    rows = [parts[pl.ds(j * share, share), :] for j in range(parts.shape[0] // share)]
    while len(rows) > 1:
        rows = [a + b for a, b in zip(rows[::2], rows[1::2])] + rows[len(rows) // 2 * 2 :]
    total[...] = rows[0][:, :rows_x]
    copy = pltpu.make_async_copy(total, out, sems.at[4])
    copy.start()
    for copy in copies + [copy]:
        copy.wait()


def shards(
    e_check, h_check, adj_e_end, adj_h_end, background, conductivity, pattern, design_box, pml_width
):
    rows_x, rows_z, cols = background.shape
    size_x, size_z = lax.axis_size("xy"), lax.axis_size("gz")
    geometry = (rows_x, rows_z, cols, rows_x * size_x, rows_z * size_z)
    fields = (e_check, h_check, adj_e_end, adj_h_end, background, conductivity)
    f32 = jnp.float32
    params = pltpu.CompilerParams(vmem_limit_bytes=VMEM_LIMIT)

    def array(*shape):
        return jax.ShapeDtypeStruct(shape, f32)

    message = pltpu.VMEM((rows_x * ROWS, cols), f32)
    inputs = fields + (pattern, design_box, pml_width)
    *inputs, design_box, pml_width, rows_far, rows_near = pl.pallas_call(
        load_fields,
        out_shape=tuple(pltpu.VMEM(ref.shape, ref.dtype) for ref in inputs) + (message,) * 2,
        in_specs=[HBM] * 9,
        out_specs=[VMEM] * 11,
        scratch_shapes=[message] * 2 + [pltpu.SemaphoreType.DMA((9,))],
        compiler_params=pltpu.CompilerParams(vmem_limit_bytes=8 * 1024 * 1024),
        name="load_fields",
    )(*(pltpu.with_memory_space_constraint(ref, pltpu.HBM) for ref in inputs))
    rows_far, rows_near = swap_both(rows_far, rows_near, "gz")

    def planes(*lead):
        return pltpu.VMEM(lead + (rows_z + EXT, cols), f32)

    size = PLANES * rows_z + SINGLE_ROWS
    message = pltpu.VMEM((size, cols), f32)
    tile = pltpu.VMEM((SLOTS, rows_x, EXT, cols), f32)
    far, near = pl.pallas_call(
        functools.partial(edge_planes, geometry),
        out_shape=(array(size, cols), array(size + 8, cols)),
        in_specs=[SMEM] * 2 + [VMEM] * 9,
        out_specs=[VMEM] * 2,
        scratch_shapes=[tile, message, message, planes(PLANES)],
        compiler_params=params,
        name="edge_planes",
    )(design_box, pml_width, *inputs, rows_far, rows_near)
    far, near = swap_both(far, near, "xy")

    count = rows_x + 1
    local_e, local_h, local_grad, edge, edge_e, edge_h = pl.pallas_call(
        functools.partial(sweep, geometry),
        out_shape=(
            array(*e_check.shape),
            array(*e_check.shape),
            array(rows_x, cols),
            array(EDGE_PLANES, rows_z + EXT, cols),
            array(3, 4, rows_z, cols),
            array(3, 4, rows_z, cols),
        ),
        in_specs=[SMEM] * 2 + [VMEM] * 9,
        out_specs=[HBM] * 2 + [VMEM] * 4,
        scratch_shapes=[tile]
        + [planes(3, count)] * 4
        + [planes(count)] * 4
        + [pltpu.VMEM((rows_x, rows_z, cols), f32)] * 3
        + [pltpu.VMEM((3, rows_x, rows_z, cols), f32)] * 2
        + [pltpu.SemaphoreType.DMA((2, rows_x // UNROLL))],
        compiler_params=params,
        cost_estimate=pl.CostEstimate(flops=50000000, bytes_accessed=8000000, transcendentals=0),
        name="sweep",
    )(design_box, pml_width, *inputs, rows_far, rows_near)

    edge_e, edge_h, shares = pl.pallas_call(
        functools.partial(response, geometry),
        out_shape=(array(*edge_e.shape), array(*edge_h.shape), array(cols, cols)),
        in_specs=[SMEM] * 2 + [VMEM] * 8,
        out_specs=[VMEM] * 3,
        scratch_shapes=[
            pltpu.VMEM((2, size, cols), f32),
            pltpu.VMEM((2, PLANES, EXT, cols), f32),
            pltpu.VMEM((cols, cols), f32),
        ],
        compiler_params=params,
        name="response",
    )(design_box, pml_width, inputs[0], inputs[2], edge, edge_e, edge_h, local_grad, far, near)

    parts = lax.all_to_all(shares, "gz", split_axis=0, concat_axis=0, tiled=True)
    back_e, back_h, pattern_grad = pl.pallas_call(
        finish,
        out_shape=(array(*e_check.shape), array(*e_check.shape), array(cols // size_z, rows_x)),
        in_specs=[VMEM] * 3 + [HBM] * 2,
        out_specs=[HBM] * 3,
        scratch_shapes=[
            pltpu.VMEM((cols // size_z, rows_x), f32),
            pltpu.SemaphoreType.DMA((5,)),
        ],
        input_output_aliases={3: 0, 4: 1},
        compiler_params=pltpu.CompilerParams(vmem_limit_bytes=8 * 1024 * 1024),
        name="finish",
    )(parts, edge_e, edge_h, local_e, local_h)
    return (back_e, back_h, pattern_grad.T)


def solution(mesh):
    field = P(None, "xy", "gz", None)
    cell = P("xy", "gz", None)
    return jax.shard_map(
        shards,
        mesh=mesh,
        in_specs=(field, field, field, field, cell, cell, P("xy", None), P(), P()),
        out_specs=(field, field, P("xy", "gz")),
        check_vma=False,
    )
```

```python
import functools

import jax
import jax.numpy as jnp
from jax import lax
from jax.experimental import pallas as pl
from jax.experimental.pallas import tpu as pltpu
from jax.sharding import PartitionSpec as P

TIME_STEP = 0.5
SIGMA_PEAK = 1.0
HALF = TIME_STEP / 2
EXT = 8
UNROLL = 4
VMEM_LIMIT = 32 * 1024 * 1024

FIRST_ROWS = (2, 2, 1, 1, 1, 1, 2, 2, 1, 1, 1, 1, 2, 2)
LAST_ROWS = (2, 2, 2, 2, 2, 1, 2, 2, 2, 2, 2, 1, 2, 2)
FIRST_AT = tuple(sum(FIRST_ROWS[:k]) for k in range(14))
LAST_AT = tuple(sum(LAST_ROWS[:k]) for k in range(14))
ROWS = max(sum(FIRST_ROWS), sum(LAST_ROWS))
PERIOD = 4
SLOTS = 14
PLANES = 9
NEXT_ROWS = tuple((k, r) for k in (0, 1, 5, 6) for r in (0, -1)) + ((4, 0),)
PREV_ROWS = tuple(
    (k, r) for k, rs in ((0, (0, -1)), (1, (0, -2, -1)), (5, (0, -1)), (6, (0, -2, -1)))
    for r in rs
) + ((3, -1), (8, -1), (4, -1))
SINGLE_ROWS = 16
EDGE_PLANES = 38

HBM = pl.BlockSpec(memory_space=pltpu.HBM)
VMEM = pl.BlockSpec(memory_space=pltpu.VMEM)
SMEM = pl.BlockSpec(memory_space=pltpu.SMEM)


def swapped(shard, axis, first):
    size = lax.axis_size(axis)
    pairs = [(i, j) for k in range(first, size - 1, 2) for i, j in ((k, k + 1), (k + 1, k))]
    return lax.ppermute(shard, axis, pairs)


def swap_both(far, near, axis):
    far, near = swapped(far, axis, 1), swapped(near, axis, 0)
    return far, near


def is_even(axis):
    return lax.rem(lax.axis_index(axis), 2) == 0


def rows_of(ref, group):
    return ref.at[pl.ds(pl.multiple_of(group * (PERIOD * ROWS), 8), PERIOD * ROWS)]


def load_fields(*refs):
    sources, copies_of, (far, near) = refs[:9], refs[9:18], refs[18:20]
    first, last, sems = refs[20:]
    rows_x, rows_z = sources[4].shape[:2]
    copies = [None] * len(sources)
    for i in (6, 7, 8, 0, 1, 2, 3, 4, 5):
        copies[i] = pltpu.make_async_copy(sources[i], copies_of[i], sems.at[i])
        copies[i].start()

    for i in range(6):
        copies[i].wait()
        field = copies_of[i]

        def pack(group, carry):
            first_rows, last_rows = rows_of(first, group), rows_of(last, group)
            for n in range(PERIOD):
                x = group * PERIOD + n
                for k in range(3 * i, 3 * i + 3) if i < 4 else (8 + i,):
                    at = (k % 3, x) if i < 4 else (x,)
                    count, start = FIRST_ROWS[k], n * ROWS + FIRST_AT[k]
                    rows = field[(*at, slice(0, count), slice(None))]
                    first_rows[start : start + count, :] = rows
                    count, start = LAST_ROWS[k], n * ROWS + LAST_AT[k]
                    rows = field[(*at, slice(rows_z - count, rows_z), slice(None))]
                    last_rows[start : start + count, :] = rows
            return carry

        lax.fori_loop(0, rows_x // PERIOD, pack, 0)
    for copy in copies[6:]:
        copy.wait()
    even = is_even("gz")
    far[...] = jnp.where(even, first[...], last[...])
    near[...] = jnp.where(even, last[...], first[...])


def lane_index(shape):
    return lax.broadcasted_iota(jnp.int32, shape, 1)


def y_ahead(v):
    cols = v.shape[1]
    moved = pltpu.roll(v, cols - 1, 1)
    return jnp.where(lane_index(v.shape) == cols - 1, 0.0, moved) - v


def y_behind(v):
    moved = pltpu.roll(v, 1, 1)
    return v - jnp.where(lane_index(v.shape) == 0, 0.0, moved)


def z_ahead(v):
    return pltpu.roll(v, v.shape[0] - 1, 0) - v


def z_behind(v):
    return v - pltpu.roll(v, 1, 0)


def plus_x(v):
    return y_ahead(v[2]) - z_ahead(v[1])


def plus_y(v, next_z):
    return z_ahead(v[0]) - (next_z - v[2])


def plus_z(v, next_y):
    return (next_y - v[1]) - y_ahead(v[0])


def plus(v, next_y, next_z):
    return plus_x(v), plus_y(v, next_z), plus_z(v, next_y)


def minus(v, prev_y, prev_z):
    return (
        y_behind(v[2]) - z_behind(v[1]),
        z_behind(v[0]) - (v[2] - prev_z),
        (v[1] - prev_y) - y_behind(v[0]),
    )


def plus_yz(v_y, v_z):
    return y_ahead(v_z) - z_ahead(v_y), v_z, -v_y


def minus_yz(v_y, v_z):
    return y_behind(v_z) - z_behind(v_y), -v_z, v_y


def dot(left, right):
    return sum(a * b for a, b in zip(left, right))


def depth_cube(place, total, layer):
    depth = jnp.maximum(jnp.maximum(layer - place, place - (total - 1 - layer)), 0.0) / layer
    return depth * depth * depth


class Grid:
    def __init__(self, box, pml, rows_x, rows_z, cols, total_x, total_z):
        rows = rows_z + EXT
        self.shape = (rows, cols)
        self.box = box
        self.width_x = pml[0].astype(jnp.float32)
        self.total_x = total_x
        self.x_start = lax.axis_index("xy") * rows_x
        self.rows_z = rows_z
        row = lax.broadcasted_iota(jnp.int32, self.shape, 0)
        z = lax.axis_index("gz") * rows_z + jnp.where(row < rows_z + EXT // 2, row, row - rows)
        y = lane_index(self.shape)
        self.inside = (z >= 0) & (z < total_z)
        self.sigma_zy = depth_cube(
            z.astype(jnp.float32), total_z, pml[2].astype(jnp.float32)
        ) + depth_cube(y.astype(jnp.float32), cols, pml[1].astype(jnp.float32))
        picked = (z >= box[4]) & (z < box[5]) & (y >= box[2]) & (y < box[3])
        self.mask_zy = jnp.where(picked, 1.0, 0.0)

    def sigma(self, x):
        place = jnp.full((1, self.shape[1]), (self.x_start + x).astype(jnp.float32))
        return SIGMA_PEAK * (self.sigma_zy + depth_cube(place, self.total_x, self.width_x))

    def mask_x(self, x):
        at = self.x_start + x
        return jnp.where((at >= self.box[0]) & (at < self.box[1]), 1.0, 0.0)

    def magnetic(self, sigma, x_inside=None):
        inside = self.inside if x_inside is None else self.inside & x_inside
        inverse = 1.0 / (1.0 + HALF * sigma)
        return (
            jnp.where(inside, 2.0 * inverse - 1.0, 0.0),
            jnp.where(inside, TIME_STEP * inverse, 0.0),
        )

    def electric(self, x, background, conductivity, pattern_row, sigma):
        permittivity = background + self.mask_zy * (pattern_row * self.mask_x(x))
        loss = HALF * (conductivity + sigma)
        inverse = jnp.where(self.inside, 1.0 / (permittivity + loss), 0.0)
        return (permittivity - loss) * inverse, TIME_STEP * inverse, loss, inverse


def full_plane(ref, tile_ref, k, x):
    own = ref[k % 3, x] if k < 12 else ref[x]
    return jnp.concatenate([own, tile_ref[k, x]], axis=0)


def fill_tiles(tile_ref, far, near, even, group, planes):
    far, near = rows_of(far, group), rows_of(near, group)
    for n in planes:
        x = group * PERIOD + n
        for k in range(SLOTS):
            tile_ref[k, x] = jnp.zeros(tile_ref.shape[2:], jnp.float32)
            for count, at, start in (
                (FIRST_ROWS[k], FIRST_AT[k], 0),
                (LAST_ROWS[k], LAST_AT[k], EXT - LAST_ROWS[k]),
            ):
                rows = pl.ds(n * ROWS + at, count)
                own, other = (near, far) if start == 0 else (far, near)
                tile_ref[k, x, pl.ds(start, count), :] = jnp.where(even, own[rows, :], other[rows, :])


def triple(fields, tile_ref, group, x):
    return tuple(full_plane(fields[group], tile_ref, 3 * group + c, x) for c in range(3))


def edge_planes(geometry, box, pml, *refs):
    fields, pattern, (rows_far, rows_near) = refs[:6], refs[6], refs[7:9]
    far, near, tile, buffers, planes = refs[9], refs[10], refs[11], refs[12:14], refs[14]
    rows_x, rows_z = geometry[:2]
    grid = Grid(box, pml, *geometry)
    even = is_even("gz")
    fill_tiles(tile, rows_far, rows_near, even, 0, (0, 1))
    fill_tiles(tile, rows_far, rows_near, even, rows_x // PERIOD - 1, (PERIOD - 2, PERIOD - 1))

    def coefs(x):
        sigma = grid.sigma(x)
        coef_a, coef_b, _, _ = grid.electric(
            x,
            full_plane(fields[4], tile, 12, x),
            full_plane(fields[5], tile, 13, x),
            pattern[pl.ds(x, 1), :],
            sigma,
        )
        return (coef_a, coef_b) + grid.magnetic(sigma)

    def load(x):
        return [triple(fields, tile, g, x) for g in range(4)]

    def pack(buffer, values, rows):
        for k, value in enumerate(values):
            buffer[pl.ds(k * rows_z, rows_z), :] = value[:rows_z]
            planes[k] = value
        start = PLANES * rows_z
        buffer[pl.ds(start, SINGLE_ROWS), :] = jnp.zeros((SINGLE_ROWS, value.shape[1]), jnp.float32)
        for i, (k, r) in enumerate(rows):
            at = rows_z + r if r >= 0 else rows_z + EXT + r
            buffer[pl.ds(start + i, 1), :] = planes[k, pl.ds(at, 1), :]

    one, two = rows_x - 2, rows_x - 1
    e1, h1, p1, q1 = load(one)
    e2, h2, p2, q2 = load(two)
    _, cb1, da1, db1 = coefs(one)
    ca2, cb2, da2, db2 = coefs(two)
    before = (
        da1 * h1[1] - db1 * plus_y(e1, e2[2]),
        da1 * h1[2] - db1 * plus_z(e1, e2[1]),
    )
    mag = [da2 * h - db2 * c for h, c in zip(h2, plus(e2, 0.0, 0.0))]
    ele = [ca2 * e + cb2 * c for e, c in zip(e2, minus(mag, *before))]
    mag2 = (
        da2 * mag[1] - db2 * plus_y(ele, 0.0),
        da2 * mag[2] - db2 * plus_z(ele, 0.0),
    )
    u1 = [cb1 * v for v in p1]
    u2 = [cb2 * v for v in p2]
    before = (
        db1 * (q1[1] + plus_y(u1, u2[2])),
        db1 * (q1[2] + plus_z(u1, u2[1])),
    )
    adj = [q + c for q, c in zip(q2, plus(u2, 0.0, 0.0))]
    curl = minus([db2 * v for v in adj], *before)
    u2 = [cb2 * (ca2 * p - c) for p, c in zip(p2, curl)]
    adj2 = (da2 * adj[1] + plus_y(u2, 0.0), da2 * adj[2] + plus_z(u2, 0.0))
    pack(buffers[0], (mag[1], mag[2]) + mag2 + (cb2, adj[1], adj[2]) + adj2, NEXT_ROWS)

    e1, h1, p1, q1 = load(0)
    e2, _, p2, _ = load(1)
    ca1, cb1, da1, db1 = coefs(0)
    _, cb2, _, _ = coefs(1)
    mag = [da1 * h - db1 * c for h, c in zip(h1, plus(e1, e2[1], e2[2]))]
    curl = minus(mag, 0.0, 0.0)
    ele = (ca1 * e1[1] + cb1 * curl[1], ca1 * e1[2] + cb1 * curl[2])
    u1 = [cb1 * v for v in p1]
    adj = [db1 * (q + c) for q, c in zip(q1, plus(u1, cb2 * p2[1], cb2 * p2[2]))]
    curl = minus(adj, 0.0, 0.0)
    adj_ele = (ca1 * p1[1] - curl[1], ca1 * p1[2] - curl[2])
    pack(buffers[1], e1[1:] + ele + (cb1, u1[1], u1[2]) + adj_ele, PREV_ROWS)

    even = is_even("xy")
    to_next, to_prev = buffers[0][...], buffers[1][...]
    size = to_next.shape[0]
    far[...] = jnp.where(even, to_prev, to_next)
    near[pl.ds(0, size), :] = jnp.where(even, to_next, to_prev)
    near[pl.ds(size, 8), :] = jnp.zeros((8, to_next.shape[1]), jnp.float32)


def sweep(geometry, box, pml, *refs):
    fields, pattern, (rows_far, rows_near) = refs[:6], refs[6], refs[7:9]
    full_e, full_h, grad, edge, edge_e, edge_h = refs[9:15]
    tile, mag, adj_mag, ele, adj_ele, ca, cb, da, db = refs[15:24]
    by_e, by_r, sums, out_e, out_h, sems = refs[24:]
    rows_x, rows_z, cols = geometry[:3]
    grid = Grid(box, pml, *geometry)
    last = rows_x - 1
    own = pl.ds(0, rows_z)
    even = is_even("gz")

    def fill(group, carry):
        fill_tiles(tile, rows_far, rows_near, even, group, range(PERIOD))
        return carry

    lax.fori_loop(0, rows_x // PERIOD, fill, 0)

    def coefs(x, carry):
        sigma = grid.sigma(x)
        ca[x], cb[x], loss, inverse = grid.electric(
            x,
            full_plane(fields[4], tile, 12, x),
            full_plane(fields[5], tile, 13, x),
            pattern[pl.ds(x, 1), :],
            sigma,
        )
        da[x], db[x] = grid.magnetic(sigma)
        weight = (inverse * inverse * (grid.mask_zy * grid.mask_x(x)))[:rows_z]
        by_e[x] = 2.0 * loss[:rows_z] * weight
        by_r[x] = -TIME_STEP * weight
        return carry

    lax.fori_loop(0, rows_x, coefs, 0, unroll=UNROLL)
    zero = jnp.zeros(grid.shape, jnp.float32)
    cb[rows_x] = zero
    for k in (1, 2):
        ele[k, rows_x] = zero
        adj_ele[k, rows_x] = zero

    def first(x, carry):
        prev_h, prev_m = carry
        at_last = jnp.full(grid.shape, x) == last
        ahead = jnp.minimum(x + 1, last)
        e, h, p, q = [triple(fields, tile, g, x) for g in range(4)]
        a, b, c, d = ca[x], cb[x], da[x], db[x]
        e_y = jnp.where(at_last, 0.0, full_plane(fields[0], tile, 1, ahead))
        e_z = jnp.where(at_last, 0.0, full_plane(fields[0], tile, 2, ahead))
        new_h = [c * v - d * w for v, w in zip(h, plus(e, e_y, e_z))]
        curl = minus(new_h, *prev_h)
        b_ahead = cb[x + 1]
        u_y = b_ahead * full_plane(fields[2], tile, 7, ahead)
        u_z = b_ahead * full_plane(fields[2], tile, 8, ahead)
        new_m = [v + w for v, w in zip(q, plus([b * v for v in p], u_y, u_z))]
        scaled = [d * v for v in new_m]
        adj_curl = minus(scaled, *prev_m)
        dot_e, dot_r = 0.0, 0.0
        for k in range(3):
            mag[k, x] = new_h[k]
            adj_mag[k, x] = new_m[k]
            ele[k, x] = a * e[k] + b * curl[k]
            new_p = a * p[k] - adj_curl[k]
            adj_ele[k, x] = new_p
            dot_e = dot_e + new_p[:rows_z] * e[k][:rows_z]
            dot_r = dot_r + new_p[:rows_z] * curl[k][:rows_z]
        sums[x] = by_e[x] * dot_e + by_r[x] * dot_r
        return new_h[1:], scaled[1:]

    lax.fori_loop(0, rows_x, first, ([zero, zero], [zero, zero]), unroll=UNROLL)

    def out_copies(group):
        part = pl.ds(group * UNROLL, UNROLL)
        return [
            pltpu.make_async_copy(ref.at[:, part], full.at[:, part], sems.at[i, group])
            for i, (ref, full) in enumerate(((out_e, full_e), (out_h, full_h)))
        ]

    def second(x, carry):
        prev_h, prev_m = carry
        e = [ele[k, x] for k in range(3)]
        p1 = [adj_ele[k, x] for k in range(3)]
        a, b, c, d = ca[x], cb[x], da[x], db[x]
        new_h = [
            c * mag[k, x] - d * w for k, w in enumerate(plus(e, ele[1, x + 1], ele[2, x + 1]))
        ]
        curl = minus(new_h, *prev_h)
        b_ahead = cb[x + 1]
        u = [b * v for v in p1]
        ahead = plus(u, b_ahead * adj_ele[1, x + 1], b_ahead * adj_ele[2, x + 1])
        new_m = [c * adj_mag[k, x] + w for k, w in enumerate(ahead)]
        scaled = [d * v for v in new_m]
        adj_curl = minus(scaled, *prev_m)
        dot_e, dot_r = 0.0, 0.0
        for k in range(3):
            out_h[k, x] = c[:rows_z] * new_m[k][:rows_z]
            out_e[k, x] = a[:rows_z] * p1[k][:rows_z] - adj_curl[k][:rows_z]
            p = fields[2][k, x]
            dot_e = dot_e + p * e[k][:rows_z]
            dot_r = dot_r + p * curl[k][:rows_z]
        terms = sums[x] + by_e[x] * dot_e + by_r[x] * dot_r
        total = terms[0:8]
        for start in range(8, rows_z, 8):
            total = total + terms[start : start + 8]
        grad[pl.ds(x, 1), :] = jnp.sum(total, axis=0, keepdims=True)
        return new_h[1:], scaled[1:]

    def second_group(group, carry):
        @pl.when(group > 0)
        def _():
            for copy in out_copies(group - 1):
                copy.start()

        for i in range(UNROLL):
            carry = second(group * UNROLL + i, carry)
        return carry

    groups = rows_x // UNROLL
    lax.fori_loop(0, groups, second_group, ([zero, zero], [zero, zero]))

    first_curl = minus([mag[k, 0] for k in range(3)], 0.0, 0.0)
    last_curl = minus([mag[k, last] for k in range(3)], mag[1, last - 1], mag[2, last - 1])
    for k in range(3):
        edge[k], edge[3 + k] = first_curl[k], last_curl[k]
    kept = [ele[1, 0], ele[2, 0]] + [adj_ele[k, 0] for k in range(3)]
    kept += [mag[1, last], mag[2, last], db[last] * adj_mag[1, last], db[last] * adj_mag[2, last]]
    kept += [adj_ele[k, last] for k in range(3)]
    kept += [ref[x] for x in (0, last) for ref in (ca, cb, da, db)] + [da[last - 1], db[last - 1]]
    kept += [full_plane(fields[0], tile, k, 0) for k in (1, 2)]
    kept += [cb[0] * full_plane(fields[2], tile, k, 0) for k in (7, 8)]
    for k, value in enumerate(kept):
        edge[6 + k] = value
    start = 6 + len(kept)
    for k, value in enumerate((by_e[0], by_r[0], by_r[1], by_r[last - 1], by_e[last], by_r[last])):
        edge[start + k, own, :] = value
    for i, x in enumerate((0, 1, *range(rows_x - UNROLL, rows_x))):
        for k in range(3):
            edge_e[k, i] = out_e[k, x]
            edge_h[k, i] = out_h[k, x]
    for group in range(groups - 1):
        for copy in out_copies(group):
            copy.wait()


def response(geometry, box, pml, *refs):
    e_ref, p_ref, edge, local_e, local_h, local_grad, far, near = refs[:8]
    edge_e, edge_h, shares, tile, grad = refs[8:]
    rows_x, rows_z, cols = geometry[:3]
    last = rows_x - 1
    grid = Grid(box, pml, *geometry)
    even = is_even("xy")

    def received(side, at, count):
        rows = pl.ds(at, count)
        pair = (far[rows, :], near[rows, :])
        return jnp.where(even, pair[side], pair[1 - side])

    grad[...] = local_grad[...]
    for side, rows in enumerate((NEXT_ROWS, PREV_ROWS)):
        for k in range(PLANES):
            tile[side, k] = jnp.zeros(tile.shape[2:], jnp.float32)
        for i, (k, r) in enumerate(rows):
            row = received(side, PLANES * rows_z + i, 1)
            tile[side, k, pl.ds(r if r >= 0 else EXT + r, 1), :] = row

    def unpack(side):
        return [
            jnp.concatenate([received(side, k * rows_z, rows_z), tile[side, k]], axis=0)
            for k in range(PLANES)
        ]

    def own(v):
        return v[:rows_z]

    def weight(k):
        return edge[32 + k, pl.ds(0, rows_z), :]

    def add_rows(x, terms):
        total = terms[0:8]
        for start in range(8, rows_z, 8):
            total = total + terms[start : start + 8]
        grad[pl.ds(x, 1), :] += jnp.sum(total, axis=0, keepdims=True)

    def write(ref, local, i, change, scale=1.0):
        for k in range(3):
            ref[k, i] = local[k, i] if change[k] is None else local[k, i] + own(change[k])

    h_y, h_z, h2_y, h2_z, cb_b, m_y, m_z, m2_y, m2_z = unpack(0)
    at = jnp.full(grid.shape, grid.x_start)
    da_b, db_b = grid.magnetic(grid.sigma(-1), at > 0)
    ca_f, cb_f, da_f, db_f = (edge[18 + k] for k in range(4))
    e_y, e_z, u_y, u_z = (edge[28 + k] for k in range(4))
    dh_y, dh_z = db_b * e_z, -(db_b * e_y)
    h_y, h_z = h_y + dh_y, h_z + dh_z
    d_ele = (cb_f * h_z, -(cb_f * h_y))
    ele_y, ele_z = edge[6] + d_ele[0], edge[7] + d_ele[1]
    back = [cb_b * v for v in minus_yz(dh_y, dh_z)]
    h2_y = h2_y + da_b * dh_y - db_b * plus_y(back, ele_z)
    h2_z = h2_z + da_b * dh_z - db_b * plus_z(back, ele_y)
    dm_y, dm_z = -u_z, u_y
    n_y, n_z = db_b * (m_y + dm_y), db_b * (m_z + dm_z)
    d_p = (-n_z, n_y)
    p_y, p_z = edge[9] + d_p[0], edge[10] + d_p[1]
    back = [-(cb_b * v) for v in minus_yz(db_b * dm_y, db_b * dm_z)]
    m2_y = m2_y + da_b * dm_y + plus_y(back, cb_f * p_z)
    m2_z = m2_z + da_b * dm_z + plus_z(back, cb_f * p_y)
    d_h2 = [-(db_f * v) for v in plus_yz(*d_ele)]
    d_m2 = plus_yz(cb_f * d_p[0], cb_f * d_p[1])
    d_r2 = minus(d_h2, h2_y, h2_z)
    d_n2 = [db_f * v for v in d_m2]
    curl = minus(d_n2, db_b * m2_y, db_b * m2_z)
    write(edge_e, local_e, 0, (-curl[0], ca_f * d_p[0] - curl[1], ca_f * d_p[1] - curl[2]))
    write(edge_e, local_e, 1, (None, -d_n2[2], d_n2[1]))
    write(edge_h, local_h, 0, [da_f * v for v in d_m2])
    write(edge_h, local_h, 1, (None, None, None))
    p2 = [p_ref[k, 0] for k in range(3)]
    along_e = sum(
        own(d_p[k - 1]) * e_ref[k, 0] + p2[k] * own(d_ele[k - 1]) for k in (1, 2)
    )
    along_r = dot(p2, [own(v) for v in d_r2])
    along_r = along_r + own(d_p[0] * edge[1] + d_p[1] * edge[2] + p_y * h_z - p_z * h_y)
    add_rows(0, weight(0) * along_e + weight(1) * along_r)
    add_rows(1, weight(2) * (p_ref[1, 1] * own(d_h2[2]) - p_ref[2, 1] * own(d_h2[1])))

    e_y, e_z, e1_y, e1_z, cb_n, u_y, u_z, p_y, p_z = unpack(1)
    ca_l, cb_l, da_l, db_l = (edge[22 + k] for k in range(4))
    da_k, db_k = edge[26], edge[27]
    dh_y, dh_z = db_l * e_z, -(db_l * e_y)
    dm_y, dm_z = -u_z, u_y
    dn_y, dn_z = db_l * dm_y, db_l * dm_z
    d_r1 = minus_yz(dh_y, dh_z)
    d_ele = [cb_l * v for v in d_r1]
    d_p = [-v for v in minus_yz(dn_y, dn_z)]
    e1_y = e1_y + cb_n * (edge[12] + dh_z)
    e1_z = e1_z - cb_n * (edge[11] + dh_y)
    p_y = p_y - (edge[14] + dn_z)
    p_z = p_z + (edge[13] + dn_y)
    d_h2 = [-(db_l * v) for v in plus(d_ele, e1_y, e1_z)]
    d_h2 = [d_h2[0], d_h2[1] + da_l * dh_y, d_h2[2] + da_l * dh_z]
    d_u = [cb_l * v for v in d_p]
    d_m2 = plus(d_u, cb_n * p_y, cb_n * p_z)
    d_m2 = [d_m2[0], d_m2[1] + da_l * dm_y, d_m2[2] + da_l * dm_z]
    k_h2 = (db_k * d_ele[2], -(db_k * d_ele[1]))
    k_m2 = (-d_u[2], d_u[1])
    k_n2 = (db_k * k_m2[0], db_k * k_m2[1])
    k_r2 = minus_yz(*k_h2)
    d_r2 = minus(d_h2, *k_h2)
    kept, before_last, at_last = range(2, UNROLL), UNROLL, UNROLL + 1
    for i in kept:
        write(edge_e, local_e, i, (None, None, None))
        write(edge_h, local_h, i, (None, None, None))
    write(edge_e, local_e, before_last, [-v for v in minus_yz(*k_n2)])
    curl = minus([db_l * v for v in d_m2], *k_n2)
    write(edge_e, local_e, at_last, [ca_l * v - c for v, c in zip(d_p, curl)])
    write(edge_h, local_h, before_last, (None, da_k * k_m2[0], da_k * k_m2[1]))
    write(edge_h, local_h, at_last, [da_l * v for v in d_m2])
    p2 = [p_ref[k, last] for k in range(3)]
    along_e = dot([own(v) for v in d_p], [e_ref[k, last] for k in range(3)])
    along_e = along_e + dot(p2, [own(v) for v in d_ele])
    along_r = dot(p2, [own(v) for v in d_r2])
    for k in range(3):
        new_p = own(edge[15 + k] + d_p[k])
        along_r = along_r + own(d_p[k] * edge[3 + k]) + new_p * own(d_r1[k])
    add_rows(last, weight(4) * along_e + weight(5) * along_r)
    p2 = [p_ref[k, last - 1] for k in range(3)]
    add_rows(last - 1, weight(3) * dot(p2, [own(v) for v in k_r2]))

    shares[...] = jnp.zeros(shares.shape, jnp.float32)
    shares[:, :rows_x] = jnp.transpose(grad[...])


def finish(parts, edge_e, edge_h, in_e, in_h, out_e, out_h, out, total, sems):
    share, rows_x = out.shape
    tail = out_e.shape[1] - UNROLL
    copies = []
    for i, (edge, full) in enumerate(((edge_e, out_e), (edge_h, out_h))):
        for side, (at, start, count) in enumerate(((0, 0, 2), (2, tail, UNROLL))):
            copy = pltpu.make_async_copy(
                edge.at[:, pl.ds(at, count)], full.at[:, pl.ds(start, count)], sems.at[2 * i + side]
            )
            copy.start()
            copies.append(copy)
    rows = [parts[pl.ds(j * share, share), :] for j in range(parts.shape[0] // share)]
    while len(rows) > 1:
        rows = [a + b for a, b in zip(rows[::2], rows[1::2])] + rows[len(rows) // 2 * 2 :]
    total[...] = rows[0][:, :rows_x]
    copy = pltpu.make_async_copy(total, out, sems.at[4])
    copy.start()
    for copy in copies + [copy]:
        copy.wait()


def shards(
    e_check, h_check, adj_e_end, adj_h_end, background, conductivity, pattern, design_box, pml_width
):
    rows_x, rows_z, cols = background.shape
    size_x, size_z = lax.axis_size("xy"), lax.axis_size("gz")
    geometry = (rows_x, rows_z, cols, rows_x * size_x, rows_z * size_z)
    fields = (e_check, h_check, adj_e_end, adj_h_end, background, conductivity)
    f32 = jnp.float32
    params = pltpu.CompilerParams(vmem_limit_bytes=VMEM_LIMIT)

    def array(*shape):
        return jax.ShapeDtypeStruct(shape, f32)

    message = pltpu.VMEM((rows_x * ROWS, cols), f32)
    inputs = fields + (pattern, design_box, pml_width)
    *inputs, design_box, pml_width, rows_far, rows_near = pl.pallas_call(
        load_fields,
        out_shape=tuple(pltpu.VMEM(ref.shape, ref.dtype) for ref in inputs) + (message,) * 2,
        in_specs=[HBM] * 9,
        out_specs=[VMEM] * 11,
        scratch_shapes=[message] * 2 + [pltpu.SemaphoreType.DMA((9,))],
        compiler_params=pltpu.CompilerParams(vmem_limit_bytes=8 * 1024 * 1024),
        name="load_fields",
    )(*(pltpu.with_memory_space_constraint(ref, pltpu.HBM) for ref in inputs))
    rows_far, rows_near = swap_both(rows_far, rows_near, "gz")

    def planes(*lead):
        return pltpu.VMEM(lead + (rows_z + EXT, cols), f32)

    size = PLANES * rows_z + SINGLE_ROWS
    message = pltpu.VMEM((size, cols), f32)
    tile = pltpu.VMEM((SLOTS, rows_x, EXT, cols), f32)
    far, near = pl.pallas_call(
        functools.partial(edge_planes, geometry),
        out_shape=(array(size, cols), array(size + 8, cols)),
        in_specs=[SMEM] * 2 + [VMEM] * 9,
        out_specs=[VMEM] * 2,
        scratch_shapes=[tile, message, message, planes(PLANES)],
        compiler_params=params,
        name="edge_planes",
    )(design_box, pml_width, *inputs, rows_far, rows_near)
    far, near = swap_both(far, near, "xy")

    count = rows_x + 1
    local_e, local_h, local_grad, edge, edge_e, edge_h = pl.pallas_call(
        functools.partial(sweep, geometry),
        out_shape=(
            array(*e_check.shape),
            array(*e_check.shape),
            array(rows_x, cols),
            array(EDGE_PLANES, rows_z + EXT, cols),
            array(3, 2 + UNROLL, rows_z, cols),
            array(3, 2 + UNROLL, rows_z, cols),
        ),
        in_specs=[SMEM] * 2 + [VMEM] * 9,
        out_specs=[HBM] * 2 + [VMEM] * 4,
        scratch_shapes=[tile]
        + [planes(3, count)] * 4
        + [planes(count)] * 4
        + [pltpu.VMEM((rows_x, rows_z, cols), f32)] * 3
        + [pltpu.VMEM((3, rows_x, rows_z, cols), f32)] * 2
        + [pltpu.SemaphoreType.DMA((2, rows_x // UNROLL))],
        compiler_params=params,
        cost_estimate=pl.CostEstimate(flops=50000000, bytes_accessed=8000000, transcendentals=0),
        name="sweep",
    )(design_box, pml_width, *inputs, rows_far, rows_near)

    edge_e, edge_h, shares = pl.pallas_call(
        functools.partial(response, geometry),
        out_shape=(array(*edge_e.shape), array(*edge_h.shape), array(cols, cols)),
        in_specs=[SMEM] * 2 + [VMEM] * 8,
        out_specs=[VMEM] * 3,
        scratch_shapes=[
            pltpu.VMEM((2, PLANES, EXT, cols), f32),
            pltpu.VMEM((rows_x, cols), f32),
        ],
        compiler_params=params,
        name="response",
    )(design_box, pml_width, inputs[0], inputs[2], edge, edge_e, edge_h, local_grad, far, near)

    parts = lax.all_to_all(shares, "gz", split_axis=0, concat_axis=0, tiled=True)
    back_e, back_h, pattern_grad = pl.pallas_call(
        finish,
        out_shape=(array(*e_check.shape), array(*e_check.shape), array(cols // size_z, rows_x)),
        in_specs=[VMEM] * 3 + [HBM] * 2,
        out_specs=[HBM] * 3,
        scratch_shapes=[
            pltpu.VMEM((cols // size_z, rows_x), f32),
            pltpu.SemaphoreType.DMA((5,)),
        ],
        input_output_aliases={3: 0, 4: 1},
        compiler_params=pltpu.CompilerParams(vmem_limit_bytes=8 * 1024 * 1024),
        name="finish",
    )(parts, edge_e, edge_h, local_e, local_h)
    return (back_e, back_h, pattern_grad.T)


def solution(mesh):
    field = P(None, "xy", "gz", None)
    cell = P("xy", "gz", None)
    return jax.shard_map(
        shards,
        mesh=mesh,
        in_specs=(field, field, field, field, cell, cell, P("xy", None), P(), P()),
        out_specs=(field, field, P("xy", "gz")),
        check_vma=False,
    )
```

```python
import functools

import jax
import jax.numpy as jnp
from jax import lax
from jax.experimental import pallas as pl
from jax.experimental.pallas import tpu as pltpu
from jax.sharding import PartitionSpec as P

TIME_STEP = 0.5
SIGMA_PEAK = 1.0
HALF = TIME_STEP / 2
EXT = 8
UNROLL = 4
VMEM_LIMIT = 32 * 1024 * 1024

FIRST_ROWS = (2, 2, 1, 1, 1, 1, 2, 2, 1, 1, 1, 1, 2, 2)
LAST_ROWS = (2, 2, 2, 2, 2, 1, 2, 2, 2, 2, 2, 1, 2, 2)
FIRST_AT = tuple(sum(FIRST_ROWS[:k]) for k in range(14))
LAST_AT = tuple(sum(LAST_ROWS[:k]) for k in range(14))
ROWS = max(sum(FIRST_ROWS), sum(LAST_ROWS))
PERIOD = 4
SLOTS = 14
PLANES = 9
NEXT_ROWS = tuple((k, r) for k in (0, 1, 5, 6) for r in (0, -1)) + ((4, 0),)
PREV_ROWS = tuple(
    (k, r) for k, rs in ((0, (0, -1)), (1, (0, -2, -1)), (5, (0, -1)), (6, (0, -2, -1)))
    for r in rs
) + ((3, -1), (8, -1), (4, -1))
SINGLE_ROWS = 16
EDGE_PLANES = 38

HBM = pl.BlockSpec(memory_space=pltpu.HBM)
VMEM = pl.BlockSpec(memory_space=pltpu.VMEM)
SMEM = pl.BlockSpec(memory_space=pltpu.SMEM)


def swapped(shard, axis, first):
    size = lax.axis_size(axis)
    pairs = [(i, j) for k in range(first, size - 1, 2) for i, j in ((k, k + 1), (k + 1, k))]
    return lax.ppermute(shard, axis, pairs)


def swap_both(far, near, axis):
    far, near = swapped(far, axis, 1), swapped(near, axis, 0)
    return far, near


def is_even(axis):
    return lax.rem(lax.axis_index(axis), 2) == 0


def rows_of(ref, group):
    return ref.at[pl.ds(pl.multiple_of(group * (PERIOD * ROWS), 8), PERIOD * ROWS)]


def load_fields(*refs):
    sources, copies_of, (far, near) = refs[:9], refs[9:18], refs[18:20]
    first, last, sems = refs[20:]
    rows_x, rows_z = sources[4].shape[:2]
    copies = []
    for i, (source, target) in enumerate(zip(sources, copies_of)):
        copy = pltpu.make_async_copy(source, target, sems.at[i])
        copy.start(priority=i % 2)
        copies.append(copy)

    for i in range(6):
        copies[i].wait()
        field = copies_of[i]

        def pack(group, carry):
            first_rows, last_rows = rows_of(first, group), rows_of(last, group)
            for n in range(PERIOD):
                x = group * PERIOD + n
                for k in range(3 * i, 3 * i + 3) if i < 4 else (8 + i,):
                    at = (k % 3, x) if i < 4 else (x,)
                    count, start = FIRST_ROWS[k], n * ROWS + FIRST_AT[k]
                    rows = field[(*at, slice(0, count), slice(None))]
                    first_rows[start : start + count, :] = rows
                    count, start = LAST_ROWS[k], n * ROWS + LAST_AT[k]
                    rows = field[(*at, slice(rows_z - count, rows_z), slice(None))]
                    last_rows[start : start + count, :] = rows
            return carry

        lax.fori_loop(0, rows_x // PERIOD, pack, 0)
    for copy in copies[6:]:
        copy.wait()
    even = is_even("gz")
    far[...] = jnp.where(even, first[...], last[...])
    near[...] = jnp.where(even, last[...], first[...])


def lane_index(shape):
    return lax.broadcasted_iota(jnp.int32, shape, 1)


def y_ahead(v):
    cols = v.shape[1]
    moved = pltpu.roll(v, cols - 1, 1)
    return jnp.where(lane_index(v.shape) == cols - 1, 0.0, moved) - v


def y_behind(v):
    moved = pltpu.roll(v, 1, 1)
    return v - jnp.where(lane_index(v.shape) == 0, 0.0, moved)


def z_ahead(v):
    return pltpu.roll(v, v.shape[0] - 1, 0) - v


def z_behind(v):
    return v - pltpu.roll(v, 1, 0)


def plus_x(v):
    return y_ahead(v[2]) - z_ahead(v[1])


def plus_y(v, next_z):
    return z_ahead(v[0]) - (next_z - v[2])


def plus_z(v, next_y):
    return (next_y - v[1]) - y_ahead(v[0])


def plus(v, next_y, next_z):
    return plus_x(v), plus_y(v, next_z), plus_z(v, next_y)


def minus(v, prev_y, prev_z):
    return (
        y_behind(v[2]) - z_behind(v[1]),
        z_behind(v[0]) - (v[2] - prev_z),
        (v[1] - prev_y) - y_behind(v[0]),
    )


def plus_yz(v_y, v_z):
    return y_ahead(v_z) - z_ahead(v_y), v_z, -v_y


def minus_yz(v_y, v_z):
    return y_behind(v_z) - z_behind(v_y), -v_z, v_y


def dot(left, right):
    return sum(a * b for a, b in zip(left, right))


def depth_cube(place, total, layer):
    depth = jnp.maximum(jnp.maximum(layer - place, place - (total - 1 - layer)), 0.0) / layer
    return depth * depth * depth


class Grid:
    def __init__(self, box, pml, rows_x, rows_z, cols, total_x, total_z):
        rows = rows_z + EXT
        self.shape = (rows, cols)
        self.box = box
        self.width_x = pml[0].astype(jnp.float32)
        self.total_x = total_x
        self.x_start = lax.axis_index("xy") * rows_x
        self.rows_z = rows_z
        row = lax.broadcasted_iota(jnp.int32, self.shape, 0)
        z = lax.axis_index("gz") * rows_z + jnp.where(row < rows_z + EXT // 2, row, row - rows)
        y = lane_index(self.shape)
        self.inside = (z >= 0) & (z < total_z)
        self.sigma_zy = depth_cube(
            z.astype(jnp.float32), total_z, pml[2].astype(jnp.float32)
        ) + depth_cube(y.astype(jnp.float32), cols, pml[1].astype(jnp.float32))
        picked = (z >= box[4]) & (z < box[5]) & (y >= box[2]) & (y < box[3])
        self.mask_zy = jnp.where(picked, 1.0, 0.0)

    def sigma(self, x):
        place = jnp.full((1, self.shape[1]), (self.x_start + x).astype(jnp.float32))
        return SIGMA_PEAK * (self.sigma_zy + depth_cube(place, self.total_x, self.width_x))

    def mask_x(self, x):
        at = self.x_start + x
        return jnp.where((at >= self.box[0]) & (at < self.box[1]), 1.0, 0.0)

    def magnetic(self, sigma, x_inside=None):
        inside = self.inside if x_inside is None else self.inside & x_inside
        inverse = 1.0 / (1.0 + HALF * sigma)
        return (
            jnp.where(inside, 2.0 * inverse - 1.0, 0.0),
            jnp.where(inside, TIME_STEP * inverse, 0.0),
        )

    def electric(self, x, background, conductivity, pattern_row, sigma):
        permittivity = background + self.mask_zy * (pattern_row * self.mask_x(x))
        loss = HALF * (conductivity + sigma)
        inverse = jnp.where(self.inside, 1.0 / (permittivity + loss), 0.0)
        return (permittivity - loss) * inverse, TIME_STEP * inverse, loss, inverse


def full_plane(ref, tile_ref, k, x):
    own = ref[k % 3, x] if k < 12 else ref[x]
    return jnp.concatenate([own, tile_ref[k, x]], axis=0)


def fill_tiles(tile_ref, far, near, even, group, planes):
    far, near = rows_of(far, group), rows_of(near, group)
    for n in planes:
        x = group * PERIOD + n
        for k in range(SLOTS):
            tile_ref[k, x] = jnp.zeros(tile_ref.shape[2:], jnp.float32)
            for count, at, start in (
                (FIRST_ROWS[k], FIRST_AT[k], 0),
                (LAST_ROWS[k], LAST_AT[k], EXT - LAST_ROWS[k]),
            ):
                rows = pl.ds(n * ROWS + at, count)
                own, other = (near, far) if start == 0 else (far, near)
                tile_ref[k, x, pl.ds(start, count), :] = jnp.where(even, own[rows, :], other[rows, :])


def triple(fields, tile_ref, group, x):
    return tuple(full_plane(fields[group], tile_ref, 3 * group + c, x) for c in range(3))


def edge_planes(geometry, box, pml, *refs):
    fields, pattern, (rows_far, rows_near) = refs[:6], refs[6], refs[7:9]
    far, near, tile, buffers, planes = refs[9], refs[10], refs[11], refs[12:14], refs[14]
    rows_x, rows_z = geometry[:2]
    grid = Grid(box, pml, *geometry)
    even = is_even("gz")
    fill_tiles(tile, rows_far, rows_near, even, 0, (0, 1))
    fill_tiles(tile, rows_far, rows_near, even, rows_x // PERIOD - 1, (PERIOD - 2, PERIOD - 1))

    def coefs(x):
        sigma = grid.sigma(x)
        coef_a, coef_b, _, _ = grid.electric(
            x,
            full_plane(fields[4], tile, 12, x),
            full_plane(fields[5], tile, 13, x),
            pattern[pl.ds(x, 1), :],
            sigma,
        )
        return (coef_a, coef_b) + grid.magnetic(sigma)

    def load(x):
        return [triple(fields, tile, g, x) for g in range(4)]

    def pack(buffer, values, rows):
        for k, value in enumerate(values):
            buffer[pl.ds(k * rows_z, rows_z), :] = value[:rows_z]
            planes[k] = value
        start = PLANES * rows_z
        buffer[pl.ds(start, SINGLE_ROWS), :] = jnp.zeros((SINGLE_ROWS, value.shape[1]), jnp.float32)
        for i, (k, r) in enumerate(rows):
            at = rows_z + r if r >= 0 else rows_z + EXT + r
            buffer[pl.ds(start + i, 1), :] = planes[k, pl.ds(at, 1), :]

    one, two = rows_x - 2, rows_x - 1
    e1, h1, p1, q1 = load(one)
    e2, h2, p2, q2 = load(two)
    _, cb1, da1, db1 = coefs(one)
    ca2, cb2, da2, db2 = coefs(two)
    before = (
        da1 * h1[1] - db1 * plus_y(e1, e2[2]),
        da1 * h1[2] - db1 * plus_z(e1, e2[1]),
    )
    mag = [da2 * h - db2 * c for h, c in zip(h2, plus(e2, 0.0, 0.0))]
    ele = [ca2 * e + cb2 * c for e, c in zip(e2, minus(mag, *before))]
    mag2 = (
        da2 * mag[1] - db2 * plus_y(ele, 0.0),
        da2 * mag[2] - db2 * plus_z(ele, 0.0),
    )
    u1 = [cb1 * v for v in p1]
    u2 = [cb2 * v for v in p2]
    before = (
        db1 * (q1[1] + plus_y(u1, u2[2])),
        db1 * (q1[2] + plus_z(u1, u2[1])),
    )
    adj = [q + c for q, c in zip(q2, plus(u2, 0.0, 0.0))]
    curl = minus([db2 * v for v in adj], *before)
    u2 = [cb2 * (ca2 * p - c) for p, c in zip(p2, curl)]
    adj2 = (da2 * adj[1] + plus_y(u2, 0.0), da2 * adj[2] + plus_z(u2, 0.0))
    pack(buffers[0], (mag[1], mag[2]) + mag2 + (cb2, adj[1], adj[2]) + adj2, NEXT_ROWS)

    e1, h1, p1, q1 = load(0)
    e2, _, p2, _ = load(1)
    ca1, cb1, da1, db1 = coefs(0)
    _, cb2, _, _ = coefs(1)
    mag = [da1 * h - db1 * c for h, c in zip(h1, plus(e1, e2[1], e2[2]))]
    curl = minus(mag, 0.0, 0.0)
    ele = (ca1 * e1[1] + cb1 * curl[1], ca1 * e1[2] + cb1 * curl[2])
    u1 = [cb1 * v for v in p1]
    adj = [db1 * (q + c) for q, c in zip(q1, plus(u1, cb2 * p2[1], cb2 * p2[2]))]
    curl = minus(adj, 0.0, 0.0)
    adj_ele = (ca1 * p1[1] - curl[1], ca1 * p1[2] - curl[2])
    pack(buffers[1], e1[1:] + ele + (cb1, u1[1], u1[2]) + adj_ele, PREV_ROWS)

    even = is_even("xy")
    to_next, to_prev = buffers[0][...], buffers[1][...]
    size = to_next.shape[0]
    far[...] = jnp.where(even, to_prev, to_next)
    near[pl.ds(0, size), :] = jnp.where(even, to_next, to_prev)
    near[pl.ds(size, 8), :] = jnp.zeros((8, to_next.shape[1]), jnp.float32)


def sweep(geometry, box, pml, *refs):
    fields, pattern, (rows_far, rows_near) = refs[:6], refs[6], refs[7:9]
    full_e, full_h, grad, edge, edge_e, edge_h = refs[9:15]
    tile, mag, adj_mag, ele, adj_ele, ca, cb, da, db = refs[15:24]
    by_e, by_r, sums, out_e, out_h, sems = refs[24:]
    rows_x, rows_z, cols = geometry[:3]
    grid = Grid(box, pml, *geometry)
    last = rows_x - 1
    own = pl.ds(0, rows_z)
    even = is_even("gz")

    def fill(group, carry):
        fill_tiles(tile, rows_far, rows_near, even, group, range(PERIOD))
        return carry

    lax.fori_loop(0, rows_x // PERIOD, fill, 0)

    def coefs(x, carry):
        sigma = grid.sigma(x)
        ca[x], cb[x], loss, inverse = grid.electric(
            x,
            full_plane(fields[4], tile, 12, x),
            full_plane(fields[5], tile, 13, x),
            pattern[pl.ds(x, 1), :],
            sigma,
        )
        da[x], db[x] = grid.magnetic(sigma)
        weight = (inverse * inverse * (grid.mask_zy * grid.mask_x(x)))[:rows_z]
        by_e[x] = 2.0 * loss[:rows_z] * weight
        by_r[x] = -TIME_STEP * weight
        return carry

    lax.fori_loop(0, rows_x, coefs, 0, unroll=UNROLL)
    zero = jnp.zeros(grid.shape, jnp.float32)
    cb[rows_x] = zero
    for k in (1, 2):
        ele[k, rows_x] = zero
        adj_ele[k, rows_x] = zero

    def first(x, carry):
        prev_h, prev_m = carry
        at_last = jnp.full(grid.shape, x) == last
        ahead = jnp.minimum(x + 1, last)
        e, h, p, q = [triple(fields, tile, g, x) for g in range(4)]
        a, b, c, d = ca[x], cb[x], da[x], db[x]
        e_y = jnp.where(at_last, 0.0, full_plane(fields[0], tile, 1, ahead))
        e_z = jnp.where(at_last, 0.0, full_plane(fields[0], tile, 2, ahead))
        new_h = [c * v - d * w for v, w in zip(h, plus(e, e_y, e_z))]
        curl = minus(new_h, *prev_h)
        b_ahead = cb[x + 1]
        u_y = b_ahead * full_plane(fields[2], tile, 7, ahead)
        u_z = b_ahead * full_plane(fields[2], tile, 8, ahead)
        new_m = [v + w for v, w in zip(q, plus([b * v for v in p], u_y, u_z))]
        scaled = [d * v for v in new_m]
        adj_curl = minus(scaled, *prev_m)
        dot_e, dot_r = 0.0, 0.0
        for k in range(3):
            mag[k, x] = new_h[k]
            adj_mag[k, x] = new_m[k]
            ele[k, x] = a * e[k] + b * curl[k]
            new_p = a * p[k] - adj_curl[k]
            adj_ele[k, x] = new_p
            dot_e = dot_e + new_p[:rows_z] * e[k][:rows_z]
            dot_r = dot_r + new_p[:rows_z] * curl[k][:rows_z]
        sums[x] = by_e[x] * dot_e + by_r[x] * dot_r
        return new_h[1:], scaled[1:]

    lax.fori_loop(0, rows_x, first, ([zero, zero], [zero, zero]), unroll=UNROLL)

    def out_copies(group):
        part = pl.ds(group * UNROLL, UNROLL)
        return [
            pltpu.make_async_copy(ref.at[:, part], full.at[:, part], sems.at[i, group])
            for i, (ref, full) in enumerate(((out_e, full_e), (out_h, full_h)))
        ]

    def second(x, carry):
        prev_h, prev_m = carry
        e = [ele[k, x] for k in range(3)]
        p1 = [adj_ele[k, x] for k in range(3)]
        a, b, c, d = ca[x], cb[x], da[x], db[x]
        new_h = [
            c * mag[k, x] - d * w for k, w in enumerate(plus(e, ele[1, x + 1], ele[2, x + 1]))
        ]
        curl = minus(new_h, *prev_h)
        b_ahead = cb[x + 1]
        u = [b * v for v in p1]
        ahead = plus(u, b_ahead * adj_ele[1, x + 1], b_ahead * adj_ele[2, x + 1])
        new_m = [c * adj_mag[k, x] + w for k, w in enumerate(ahead)]
        scaled = [d * v for v in new_m]
        adj_curl = minus(scaled, *prev_m)
        dot_e, dot_r = 0.0, 0.0
        for k in range(3):
            out_h[k, x] = c[:rows_z] * new_m[k][:rows_z]
            out_e[k, x] = a[:rows_z] * p1[k][:rows_z] - adj_curl[k][:rows_z]
            p = fields[2][k, x]
            dot_e = dot_e + p * e[k][:rows_z]
            dot_r = dot_r + p * curl[k][:rows_z]
        terms = sums[x] + by_e[x] * dot_e + by_r[x] * dot_r
        total = terms[0:8]
        for start in range(8, rows_z, 8):
            total = total + terms[start : start + 8]
        grad[pl.ds(x, 1), :] = jnp.sum(total, axis=0, keepdims=True)
        return new_h[1:], scaled[1:]

    def second_group(group, carry):
        for i in range(UNROLL):
            carry = second(group * UNROLL + i, carry)
        for copy in out_copies(group):
            copy.start()
        return carry

    groups = rows_x // UNROLL
    lax.fori_loop(0, groups, second_group, ([zero, zero], [zero, zero]))

    first_curl = minus([mag[k, 0] for k in range(3)], 0.0, 0.0)
    last_curl = minus([mag[k, last] for k in range(3)], mag[1, last - 1], mag[2, last - 1])
    for k in range(3):
        edge[k], edge[3 + k] = first_curl[k], last_curl[k]
    kept = [ele[1, 0], ele[2, 0]] + [adj_ele[k, 0] for k in range(3)]
    kept += [mag[1, last], mag[2, last], db[last] * adj_mag[1, last], db[last] * adj_mag[2, last]]
    kept += [adj_ele[k, last] for k in range(3)]
    kept += [ref[x] for x in (0, last) for ref in (ca, cb, da, db)] + [da[last - 1], db[last - 1]]
    kept += [full_plane(fields[0], tile, k, 0) for k in (1, 2)]
    kept += [cb[0] * full_plane(fields[2], tile, k, 0) for k in (7, 8)]
    for k, value in enumerate(kept):
        edge[6 + k] = value
    start = 6 + len(kept)
    for k, value in enumerate((by_e[0], by_r[0], by_r[1], by_r[last - 1], by_e[last], by_r[last])):
        edge[start + k, own, :] = value
    for i, x in enumerate((0, 1, last - 1, last)):
        for k in range(3):
            edge_e[k, i] = out_e[k, x]
            edge_h[k, i] = out_h[k, x]
    for group in range(groups):
        for copy in out_copies(group):
            copy.wait()


def response(geometry, box, pml, *refs):
    e_ref, p_ref, edge, local_e, local_h, local_grad, far, near = refs[:8]
    edge_e, edge_h, shares, buffers, tile, grad = refs[8:]
    rows_x, rows_z, cols = geometry[:3]
    last = rows_x - 1
    grid = Grid(box, pml, *geometry)
    even = is_even("xy")
    close = near[pl.ds(0, far.shape[0]), :]
    buffers[0] = jnp.where(even, far[...], close)
    buffers[1] = jnp.where(even, close, far[...])
    grad[...] = jnp.zeros(grad.shape, jnp.float32)
    grad[pl.ds(0, rows_x), :] = local_grad[...]
    for side, rows in enumerate((NEXT_ROWS, PREV_ROWS)):
        for k in range(PLANES):
            tile[side, k] = jnp.zeros(tile.shape[2:], jnp.float32)
        for i, (k, r) in enumerate(rows):
            row = buffers[side, pl.ds(PLANES * rows_z + i, 1), :]
            tile[side, k, pl.ds(r if r >= 0 else EXT + r, 1), :] = row

    def unpack(side):
        return [
            jnp.concatenate([buffers[side, pl.ds(k * rows_z, rows_z), :], tile[side, k]], axis=0)
            for k in range(PLANES)
        ]

    def own(v):
        return v[:rows_z]

    def weight(k):
        return edge[32 + k, pl.ds(0, rows_z), :]

    def add_rows(x, terms):
        total = terms[0:8]
        for start in range(8, rows_z, 8):
            total = total + terms[start : start + 8]
        grad[pl.ds(x, 1), :] += jnp.sum(total, axis=0, keepdims=True)

    def write(ref, local, i, change, scale=1.0):
        for k in range(3):
            ref[k, i] = local[k, i] if change[k] is None else local[k, i] + own(change[k])

    h_y, h_z, h2_y, h2_z, cb_b, m_y, m_z, m2_y, m2_z = unpack(0)
    at = jnp.full(grid.shape, grid.x_start)
    da_b, db_b = grid.magnetic(grid.sigma(-1), at > 0)
    ca_f, cb_f, da_f, db_f = (edge[18 + k] for k in range(4))
    e_y, e_z, u_y, u_z = (edge[28 + k] for k in range(4))
    dh_y, dh_z = db_b * e_z, -(db_b * e_y)
    h_y, h_z = h_y + dh_y, h_z + dh_z
    d_ele = (cb_f * h_z, -(cb_f * h_y))
    ele_y, ele_z = edge[6] + d_ele[0], edge[7] + d_ele[1]
    back = [cb_b * v for v in minus_yz(dh_y, dh_z)]
    h2_y = h2_y + da_b * dh_y - db_b * plus_y(back, ele_z)
    h2_z = h2_z + da_b * dh_z - db_b * plus_z(back, ele_y)
    dm_y, dm_z = -u_z, u_y
    n_y, n_z = db_b * (m_y + dm_y), db_b * (m_z + dm_z)
    d_p = (-n_z, n_y)
    p_y, p_z = edge[9] + d_p[0], edge[10] + d_p[1]
    back = [-(cb_b * v) for v in minus_yz(db_b * dm_y, db_b * dm_z)]
    m2_y = m2_y + da_b * dm_y + plus_y(back, cb_f * p_z)
    m2_z = m2_z + da_b * dm_z + plus_z(back, cb_f * p_y)
    d_h2 = [-(db_f * v) for v in plus_yz(*d_ele)]
    d_m2 = plus_yz(cb_f * d_p[0], cb_f * d_p[1])
    d_r2 = minus(d_h2, h2_y, h2_z)
    d_n2 = [db_f * v for v in d_m2]
    curl = minus(d_n2, db_b * m2_y, db_b * m2_z)
    write(edge_e, local_e, 0, (-curl[0], ca_f * d_p[0] - curl[1], ca_f * d_p[1] - curl[2]))
    write(edge_e, local_e, 1, (None, -d_n2[2], d_n2[1]))
    write(edge_h, local_h, 0, [da_f * v for v in d_m2])
    write(edge_h, local_h, 1, (None, None, None))
    p2 = [p_ref[k, 0] for k in range(3)]
    along_e = sum(
        own(d_p[k - 1]) * e_ref[k, 0] + p2[k] * own(d_ele[k - 1]) for k in (1, 2)
    )
    along_r = dot(p2, [own(v) for v in d_r2])
    along_r = along_r + own(d_p[0] * edge[1] + d_p[1] * edge[2] + p_y * h_z - p_z * h_y)
    add_rows(0, weight(0) * along_e + weight(1) * along_r)
    add_rows(1, weight(2) * (p_ref[1, 1] * own(d_h2[2]) - p_ref[2, 1] * own(d_h2[1])))

    e_y, e_z, e1_y, e1_z, cb_n, u_y, u_z, p_y, p_z = unpack(1)
    ca_l, cb_l, da_l, db_l = (edge[22 + k] for k in range(4))
    da_k, db_k = edge[26], edge[27]
    dh_y, dh_z = db_l * e_z, -(db_l * e_y)
    dm_y, dm_z = -u_z, u_y
    dn_y, dn_z = db_l * dm_y, db_l * dm_z
    d_r1 = minus_yz(dh_y, dh_z)
    d_ele = [cb_l * v for v in d_r1]
    d_p = [-v for v in minus_yz(dn_y, dn_z)]
    e1_y = e1_y + cb_n * (edge[12] + dh_z)
    e1_z = e1_z - cb_n * (edge[11] + dh_y)
    p_y = p_y - (edge[14] + dn_z)
    p_z = p_z + (edge[13] + dn_y)
    d_h2 = [-(db_l * v) for v in plus(d_ele, e1_y, e1_z)]
    d_h2 = [d_h2[0], d_h2[1] + da_l * dh_y, d_h2[2] + da_l * dh_z]
    d_u = [cb_l * v for v in d_p]
    d_m2 = plus(d_u, cb_n * p_y, cb_n * p_z)
    d_m2 = [d_m2[0], d_m2[1] + da_l * dm_y, d_m2[2] + da_l * dm_z]
    k_h2 = (db_k * d_ele[2], -(db_k * d_ele[1]))
    k_m2 = (-d_u[2], d_u[1])
    k_n2 = (db_k * k_m2[0], db_k * k_m2[1])
    k_r2 = minus_yz(*k_h2)
    d_r2 = minus(d_h2, *k_h2)
    write(edge_e, local_e, 2, [-v for v in minus_yz(*k_n2)])
    curl = minus([db_l * v for v in d_m2], *k_n2)
    write(edge_e, local_e, 3, [ca_l * v - c for v, c in zip(d_p, curl)])
    write(edge_h, local_h, 2, (None, da_k * k_m2[0], da_k * k_m2[1]))
    write(edge_h, local_h, 3, [da_l * v for v in d_m2])
    p2 = [p_ref[k, last] for k in range(3)]
    along_e = dot([own(v) for v in d_p], [e_ref[k, last] for k in range(3)])
    along_e = along_e + dot(p2, [own(v) for v in d_ele])
    along_r = dot(p2, [own(v) for v in d_r2])
    for k in range(3):
        new_p = own(edge[15 + k] + d_p[k])
        along_r = along_r + own(d_p[k] * edge[3 + k]) + new_p * own(d_r1[k])
    add_rows(last, weight(4) * along_e + weight(5) * along_r)
    p2 = [p_ref[k, last - 1] for k in range(3)]
    add_rows(last - 1, weight(3) * dot(p2, [own(v) for v in k_r2]))

    shares[...] = jnp.transpose(grad[...])


def finish(parts, edge_e, edge_h, in_e, in_h, out_e, out_h, out, total, sems):
    share, rows_x = out.shape
    last = out_e.shape[1] - 2
    copies = []
    for i, (edge, full) in enumerate(((edge_e, out_e), (edge_h, out_h))):
        for side, start in enumerate((0, last)):
            copy = pltpu.make_async_copy(
                edge.at[:, pl.ds(2 * side, 2)], full.at[:, pl.ds(start, 2)], sems.at[2 * i + side]
            )
            copy.start()
            copies.append(copy)
    rows = [parts[pl.ds(j * share, share), :] for j in range(parts.shape[0] // share)]
    while len(rows) > 1:
        rows = [a + b for a, b in zip(rows[::2], rows[1::2])] + rows[len(rows) // 2 * 2 :]
    total[...] = rows[0][:, :rows_x]
    copy = pltpu.make_async_copy(total, out, sems.at[4])
    copy.start()
    for copy in copies + [copy]:
        copy.wait()


def shards(
    e_check, h_check, adj_e_end, adj_h_end, background, conductivity, pattern, design_box, pml_width
):
    rows_x, rows_z, cols = background.shape
    size_x, size_z = lax.axis_size("xy"), lax.axis_size("gz")
    geometry = (rows_x, rows_z, cols, rows_x * size_x, rows_z * size_z)
    fields = (e_check, h_check, adj_e_end, adj_h_end, background, conductivity)
    f32 = jnp.float32
    params = pltpu.CompilerParams(vmem_limit_bytes=VMEM_LIMIT)

    def array(*shape):
        return jax.ShapeDtypeStruct(shape, f32)

    message = pltpu.VMEM((rows_x * ROWS, cols), f32)
    inputs = fields + (pattern, design_box, pml_width)
    *inputs, design_box, pml_width, rows_far, rows_near = pl.pallas_call(
        load_fields,
        out_shape=tuple(pltpu.VMEM(ref.shape, ref.dtype) for ref in inputs) + (message,) * 2,
        in_specs=[HBM] * 9,
        out_specs=[VMEM] * 11,
        scratch_shapes=[message] * 2 + [pltpu.SemaphoreType.DMA((9,))],
        compiler_params=pltpu.CompilerParams(vmem_limit_bytes=8 * 1024 * 1024),
        name="load_fields",
    )(*(pltpu.with_memory_space_constraint(ref, pltpu.HBM) for ref in inputs))
    rows_far, rows_near = swap_both(rows_far, rows_near, "gz")

    def planes(*lead):
        return pltpu.VMEM(lead + (rows_z + EXT, cols), f32)

    size = PLANES * rows_z + SINGLE_ROWS
    message = pltpu.VMEM((size, cols), f32)
    tile = pltpu.VMEM((SLOTS, rows_x, EXT, cols), f32)
    far, near = pl.pallas_call(
        functools.partial(edge_planes, geometry),
        out_shape=(array(size, cols), array(size + 8, cols)),
        in_specs=[SMEM] * 2 + [VMEM] * 9,
        out_specs=[VMEM] * 2,
        scratch_shapes=[tile, message, message, planes(PLANES)],
        compiler_params=params,
        name="edge_planes",
    )(design_box, pml_width, *inputs, rows_far, rows_near)
    far, near = swap_both(far, near, "xy")

    count = rows_x + 1
    local_e, local_h, local_grad, edge, edge_e, edge_h = pl.pallas_call(
        functools.partial(sweep, geometry),
        out_shape=(
            array(*e_check.shape),
            array(*e_check.shape),
            array(rows_x, cols),
            array(EDGE_PLANES, rows_z + EXT, cols),
            array(3, 4, rows_z, cols),
            array(3, 4, rows_z, cols),
        ),
        in_specs=[SMEM] * 2 + [VMEM] * 9,
        out_specs=[HBM] * 2 + [VMEM] * 4,
        scratch_shapes=[tile]
        + [planes(3, count)] * 4
        + [planes(count)] * 4
        + [pltpu.VMEM((rows_x, rows_z, cols), f32)] * 3
        + [pltpu.VMEM((3, rows_x, rows_z, cols), f32)] * 2
        + [pltpu.SemaphoreType.DMA((2, rows_x // UNROLL))],
        compiler_params=params,
        cost_estimate=pl.CostEstimate(flops=50000000, bytes_accessed=8000000, transcendentals=0),
        name="sweep",
    )(design_box, pml_width, *inputs, rows_far, rows_near)

    edge_e, edge_h, shares = pl.pallas_call(
        functools.partial(response, geometry),
        out_shape=(array(*edge_e.shape), array(*edge_h.shape), array(cols, cols)),
        in_specs=[SMEM] * 2 + [VMEM] * 8,
        out_specs=[VMEM] * 3,
        scratch_shapes=[
            pltpu.VMEM((2, size, cols), f32),
            pltpu.VMEM((2, PLANES, EXT, cols), f32),
            pltpu.VMEM((cols, cols), f32),
        ],
        compiler_params=params,
        name="response",
    )(design_box, pml_width, inputs[0], inputs[2], edge, edge_e, edge_h, local_grad, far, near)

    parts = lax.all_to_all(shares, "gz", split_axis=0, concat_axis=0, tiled=True)
    back_e, back_h, pattern_grad = pl.pallas_call(
        finish,
        out_shape=(array(*e_check.shape), array(*e_check.shape), array(cols // size_z, rows_x)),
        in_specs=[VMEM] * 3 + [HBM] * 2,
        out_specs=[HBM] * 3,
        scratch_shapes=[
            pltpu.VMEM((cols // size_z, rows_x), f32),
            pltpu.SemaphoreType.DMA((5,)),
        ],
        input_output_aliases={3: 0, 4: 1},
        compiler_params=pltpu.CompilerParams(vmem_limit_bytes=8 * 1024 * 1024),
        name="finish",
    )(parts, edge_e, edge_h, local_e, local_h)
    return (back_e, back_h, pattern_grad.T)


def solution(mesh):
    field = P(None, "xy", "gz", None)
    cell = P("xy", "gz", None)
    return jax.shard_map(
        shards,
        mesh=mesh,
        in_specs=(field, field, field, field, cell, cell, P("xy", None), P(), P()),
        out_specs=(field, field, P("xy", "gz")),
        check_vma=False,
    )
```
